32 devices in a mesh: dp: 8 (over y, x, core), mp: 4 (over z).
Axes of the slice: x: 2, y: 2, z: 4, core: 2. Of those that a mesh axis runs over, the one named last changes fastest.
Arguments:
- inputs: bfloat16 [16384, 768], P(('dp', 'mp')), may hold values from -6 to 6
- gain_attn: bfloat16 [768], replicated, may hold values from 0.5 to 1.5
- w_query: bfloat16 [768, 768], P(None, 'mp'), may hold values from -0.109375 to 0.109375
- w_key: bfloat16 [768, 768], P(None, 'mp'), may hold values from -0.109375 to 0.109375
- w_value: bfloat16 [768, 768], P(None, 'mp'), may hold values from -0.21875 to 0.21875
- w_out: bfloat16 [768, 768], P('mp'), may hold values from -1.25 to 1.25
- rel_table: bfloat16 [32, 12], P(None, 'mp'), may hold values from -4 to 4
- gain_ffn: bfloat16 [768], replicated, may hold values from 0.5 to 1.5
- w_in: bfloat16 [768, 3072], P(None, 'mp'), may hold values from -0.21875 to 0.21875
- w_down: bfloat16 [3072, 768], P('mp'), may hold values from -0.109375 to 0.109375
- cotangent: bfloat16 [16384, 768], P(('dp', 'mp')), may hold values from -6 to 6
- bucket: int32 [8], P('dp'), may hold values from 256 to 512, as said below
- lengths: int32 [8, 8], P('dp'), may hold values from 0 to 512, as said below
Outputs:
- outputs: bfloat16 [16384, 768], P(('dp', 'mp'))
- grad_inputs: bfloat16 [16384, 768], P(('dp', 'mp'))
- grad_query: float32 [768, 768], P(None, 'mp')
- grad_key: float32 [768, 768], P(None, 'mp')
- grad_value: float32 [768, 768], P(None, 'mp')
- grad_out: float32 [768, 768], P('mp')
- grad_table: float32 [32, 12], P(None, 'mp')
- grad_gain_attn: float32 [768], replicated
- grad_gain_ffn: float32 [768], replicated
- grad_in: float32 [768, 3072], P(None, 'mp')
- grad_down: float32 [3072, 768], P('mp')
The draws below stay inside these ranges and needn't reach their ends.
Inputs may be any that keep to these rules, and one draw needn't show every extreme that they name: `bucket`: half of the indices of dp hold 512 and the other half 512 // 2. `lengths`: the sequences of index i of dp fill its 2048 rows in slots of bucket[i] rows; slots beyond 2048 // bucket[i] hold 0; a used slot holds max(bucket[i] // 4, 1) to bucket[i], and one used slot of each index holds exactly bucket[i].
All inputs are finite; a program needn't handle non-finite values.
Results may differ from the reference program's by a relative error of at most 0.014.
The reference program's roundings to bfloat16 on the way count: a program that leaves them out, or rounds other values in their place, can miss the bound.
Values may be sent and summed in bfloat16 or wider, within the bound.
No kernel may reach another device: no remote copies, remote signals or barrier semaphores. Data moves between devices by JAX's collectives and lax.ppermute only.
A program may use at most 128 MiB of HBM per device.

```python
import jax
import jax.numpy as jnp
from jax import lax

D = 768
HEADS = 12
HEAD_DIM = 64
FF = 3072
NBUCKET = 32
BIG = 512
BLOCKS_DEV = 4
ROWS_DEV = 2048
TOKENS = 16384
N_DP = 8


def bucket_sizes(key):
    order = jax.random.permutation(jax.random.fold_in(key, 5), N_DP).astype(jnp.int32)
    return jnp.where(order % 2 == 0, BIG, BIG // 2).astype(jnp.int32)


def draw_bucket(key, part):
    sizes = bucket_sizes(key)
    return sizes


def draw_lengths(key, part):
    sizes = bucket_sizes(key)
    key = jax.random.fold_in(key, 17)
    first_key, second_key = jax.random.split(key)
    slot_count = 2 * BLOCKS_DEV
    shortest = jnp.maximum(sizes // 4, 1)[:, None]
    drawn = jax.random.randint(first_key, (N_DP, slot_count), shortest, sizes[:, None] + 1, dtype=jnp.int32)
    used_slots = (ROWS_DEV // sizes).astype(jnp.int32)
    chosen = jax.random.randint(second_key, (N_DP,), 0, used_slots, dtype=jnp.int32)
    slot_index = jnp.arange(slot_count, dtype=jnp.int32)[None, :]
    drawn = jnp.where(slot_index == chosen[:, None], sizes[:, None], drawn)
    return jnp.where(slot_index < used_slots[:, None], drawn, 0).astype(jnp.int32)


def block_scale(rng, shape, pieces, smallest, high):
    def one(dim, parts):
        draws = jax.random.uniform(jax.random.fold_in(jax.random.fold_in(rng, 6), dim), (parts,), jnp.float32, smallest / len(pieces), high / len(pieces))
        return jnp.repeat(jnp.exp(draws), shape[dim] // parts).reshape((-1,) + (1,) * (len(shape) - dim - 1))

    level = one(*pieces[0])
    for cut in pieces[1:]:
        level = level * one(*cut)
    return level


def scatter_about(key, dims, spread, bound, cuts=(), held_as=jnp.bfloat16):
    values = jax.random.normal(key, dims, jnp.float32) * spread
    if len(cuts) > 0:
        values = block_scale(key, dims, cuts, -0.22, 0.18) * values
    return jnp.clip(values, min=-bound, max=bound).astype(held_as)


def setup_inputs(seed: int = 0) -> dict:
    arg_keys = jax.random.split(jax.random.key(seed), 14)
    return {
        "inputs": scatter_about(arg_keys[0], (TOKENS, D), 1.0, 6.0, ((0, 32),)),
        "gain_attn": jnp.clip(1.0 + 0.1 * jax.random.normal(arg_keys[1], (D,), jnp.float32), 0.5, 1.5).astype(jnp.bfloat16),
        "w_query": scatter_about(arg_keys[2], (D, D), (4 * D) ** -0.5, 0.109375, ((1, 4),)),
        "w_key": scatter_about(arg_keys[3], (D, D), (4 * D) ** -0.5, 0.109375, ((1, 4),)),
        "w_value": scatter_about(arg_keys[4], (D, D), D ** -0.5, 0.21875, ((1, 4),)),
        "w_out": scatter_about(arg_keys[5], (D, D), (D // 32) ** -0.5, 1.25, ((0, 4),)),
        "rel_table": scatter_about(arg_keys[6], (NBUCKET, HEADS), 1.0, 4.0, ((1, 4),)),
        "gain_ffn": jnp.clip(1.0 + 0.1 * jax.random.normal(arg_keys[7], (D,), jnp.float32), 0.5, 1.5).astype(jnp.bfloat16),
        "w_in": scatter_about(arg_keys[8], (D, FF), D ** -0.5, 0.21875, ((1, 4),)),
        "w_down": scatter_about(arg_keys[9], (FF, D), FF ** -0.5, 0.109375, ((0, 4),)),
        "cotangent": scatter_about(arg_keys[10], (TOKENS, D), 1.0, 6.0, ((0, 32),)),
        "bucket": draw_bucket(jax.random.fold_in(arg_keys[13], 71), 0),
        "lengths": draw_lengths(jax.random.fold_in(arg_keys[13], 71), 0),
    }


EPS = 1e-06
THRESHOLDS = (12, 16, 23, 32, 46, 64, 91)
MASKED = -1e+30
HIGH = lax.Precision.HIGHEST

@jax.custom_vjp
def low(v):
    return lax.optimization_barrier(v.astype(jnp.bfloat16)).astype(jnp.float32)

@jax.custom_vjp
def low_back(v):
    return v

def low_keep(v):
    return (low(v), None)

def low_pass(kept, grad):
    return (grad,)

def back_keep(v):
    return (v, None)

def back_low(kept, grad):
    return (low(grad),)
low.defvjp(low_keep, low_pass)
low_back.defvjp(back_keep, back_low)

def bucket_matrix(block_rows):
    index_row = jnp.arange(block_rows, dtype=jnp.int32)
    offsets = index_row[None, :] - index_row[:, None]
    distance = jnp.abs(offsets)
    far_part = 8 + sum(((distance >= threshold).astype(jnp.int32) for threshold in THRESHOLDS))
    nearby = jnp.where(distance < 8, distance, far_part)
    return nearby + jnp.where(offsets > 0, 16, 0).astype(jnp.int32)

def rms_norm(values, gain_vec):
    return values * lax.rsqrt(lax.optimization_barrier(jnp.mean(values * values, axis=-1, keepdims=True)) + EPS) * gain_vec

def matmul(left_side, right_side):
    return jnp.dot(left_side, right_side, precision=HIGH)

def reference(inputs, gain_attn, w_query, w_key, w_value, w_out, rel_table, gain_ffn, w_in, w_down, cotangent, bucket, lengths):
    block_rows = BIG
    block_count = TOKENS // block_rows
    row_index = jnp.arange(TOKENS, dtype=jnp.int32)
    device = row_index // ROWS_DEV
    local_index = row_index - device * ROWS_DEV
    bucket_size = bucket[device]
    segment = local_index // bucket_size
    position = local_index - segment * bucket_size
    seq_length = lengths[device, segment]
    valid_key = position < seq_length
    segments = segment.reshape(block_count, block_rows)
    valids = valid_key.reshape(block_count, block_rows)
    buckets = bucket_matrix(block_rows)

    def forward(x_value, gain_one, query_w, key_w, value_w, out_w, table, gain_two, in_w, down_w):
        normed_one = low(rms_norm(x_value, gain_one))

        def heads_of(weight):
            return low(low_back(matmul(normed_one, weight))).reshape(block_count, block_rows, HEADS, HEAD_DIM)
        queries = heads_of(query_w)
        keys_all = heads_of(key_w)
        values_all = heads_of(value_w)
        rel_bias = jnp.transpose(table[buckets], (2, 0, 1))

        def attend(block_items):
            query_block, key_block, value_block, segment_block, valid_block = block_items
            scores = low_back(jnp.einsum('qhd,khd->hqk', query_block, key_block, precision=HIGH) + rel_bias)
            allowed = (segment_block[:, None] == segment_block[None, :]) & valid_block[None, :]
            scores = jnp.where(allowed[None], scores, MASKED)
            row_max = lax.optimization_barrier(jnp.max(scores, axis=2, keepdims=True))
            weights = jnp.exp(scores - row_max)
            probability = weights / lax.optimization_barrier(jnp.sum(weights, axis=2, keepdims=True))
            mixed_heads = jnp.einsum('hqk,khd->qhd', low(probability), value_block, precision=HIGH)
            return low(low_back(mixed_heads))
        heads_out = lax.map(jax.checkpoint(attend), (queries, keys_all, values_all, segments, valids))
        attn_branch = low_back(matmul(heads_out.reshape(TOKENS, D), out_w))
        hidden = x_value + attn_branch
        normed_two = low(rms_norm(hidden, gain_two))
        pre_act = low_back(matmul(normed_two, in_w))
        activation = low(jax.nn.gelu(pre_act, approximate=True))
        return hidden + low_back(matmul(activation, down_w))
    floats = tuple((argument.astype(jnp.float32) for argument in (inputs, gain_attn, w_query, w_key, w_value, w_out, rel_table, gain_ffn, w_in, w_down)))
    result, pullback = jax.vjp(forward, *floats)
    grads = pullback(cotangent.astype(jnp.float32))
    return (result.astype(jnp.bfloat16), grads[0].astype(jnp.bfloat16), grads[2], grads[3], grads[4], grads[5], grads[6], grads[1], grads[7], grads[8], grads[9])
```

```python
import functools

import jax
import jax.numpy as jnp
import numpy as np
from jax import lax
from jax.experimental import pallas as pl
from jax.experimental.pallas import tpu as pltpu
from jax.sharding import PartitionSpec as P

BIG = 512
HEAD = 64
EPS = 1e-06
THRESHOLDS = (12, 16, 23, 32, 46, 64, 91)
MASKED = -1e30
TILE = 128
SPAN = 1024
BF = jnp.bfloat16
F32 = jnp.float32
MIB = 1024 * 1024


def offset_one_hot(buckets):
    u = np.arange(SPAN)
    offsets = np.where(u < 896, u, u - SPAN) - 3 * TILE
    distance = np.abs(offsets)
    far = 8 + sum((distance >= t).astype(np.int32) for t in THRESHOLDS)
    bucket = np.where(distance < 8, distance, far) + np.where(offsets > 0, 16, 0)
    return (bucket[:, None] == np.arange(buckets)[None, :]).astype(np.float32)


def dot_nn(a, b):
    return lax.dot_general(a, b, (((1,), (0,)), ((), ())), preferred_element_type=F32)


def dot_nt(a, b):
    return lax.dot_general(a, b, (((1,), (1,)), ((), ())), preferred_element_type=F32)


def dot_tn(a, b):
    return lax.dot_general(a, b, (((0,), (0,)), ((), ())), preferred_element_type=F32)


def mask_rows(meta_ref, slots):
    bucket = meta_ref[0]
    half = BIG // 2
    segs, starts = [], []
    for part in range(2):
        first = meta_ref[1] + part * half
        seg = jnp.int32(0)
        for j in range(1, slots):
            seg = seg + jnp.where(first >= j * bucket, 1, 0).astype(jnp.int32)
        segs.append(seg)
        starts.append(first - seg * bucket)
    iota = lax.broadcasted_iota(jnp.int32, (1, half), 1)
    rows = []
    for query_part in range(2):
        cols = []
        for key_part in range(2):
            same = segs[query_part] == segs[key_part]
            limit = jnp.where(same, meta_ref[2 + segs[key_part]] - starts[key_part], 0)
            cols.append(jnp.where(iota < limit, 0.0, MASKED).astype(F32))
        rows.append(jnp.concatenate(cols, axis=1))
    return rows


def bias_band(rel_row):
    wide = jnp.broadcast_to(rel_row, (TILE, SPAN))
    return pltpu.roll(wide, 0, 1, stride=1, stride_axis=0)


def attn_fwd_kernel(slots, heads, meta_ref, n1_ref, a_ref, rel_ref, qkv_ref, o_ref, lse_ref, hp_ref, band):
    step = pl.program_id(0)
    width = heads * HEAD
    qkv_ref[0] = dot_nn(n1_ref[...], a_ref[0]).astype(BF)
    masks = mask_rows(meta_ref, slots)
    for h in range(heads):
        band[...] = bias_band(rel_ref[0, h : h + 1, :].astype(F32))
        q = qkv_ref[0, :, width + h * HEAD : width + (h + 1) * HEAD]
        k = qkv_ref[0, :, 2 * width + h * HEAD : 2 * width + (h + 1) * HEAD]
        v = qkv_ref[0, :, 3 * width + h * HEAD : 3 * width + (h + 1) * HEAD]
        for i in range(BIG // TILE):
            rows = slice(i * TILE, (i + 1) * TILE)
            s = dot_nt(q[rows], k) + band[:, (3 - i) * TILE : (7 - i) * TILE] + masks[i // 2]
            top = jnp.max(s, axis=1, keepdims=True)
            e = jnp.exp(s - top)
            total = jnp.sum(e, axis=1, keepdims=True)
            pb = (e * (1.0 / total)).astype(BF)
            o_ref[0, rows, h * HEAD : (h + 1) * HEAD] = dot_nn(pb, v).astype(BF)
            lse_ref[0, rows, h : h + 1] = top + jnp.log(total)
    part = dot_nt(o_ref[0], a_ref[0, :, :width])

    @pl.when(step == 0)
    def _():
        hp_ref[...] = part

    @pl.when(step > 0)
    def _():
        hp_ref[...] += part


def attn_fwd(meta, n1, a, rel, slots, heads):
    shards, depth, cols = a.shape
    rows = n1.shape[0]
    width = heads * HEAD
    return pl.pallas_call(
        functools.partial(attn_fwd_kernel, slots, heads),
        grid=(shards,),
        in_specs=[
            pl.BlockSpec(memory_space=pltpu.SMEM),
            pl.BlockSpec((rows, depth), lambda s: (0, 0)),
            pl.BlockSpec((1, depth, cols), lambda s: (s, 0, 0)),
            pl.BlockSpec((1,) + rel.shape[1:], lambda s: (s, 0, 0)),
        ],
        out_specs=[
            pl.BlockSpec((1, rows, cols), lambda s: (s, 0, 0)),
            pl.BlockSpec((1, rows, width), lambda s: (s, 0, 0)),
            pl.BlockSpec((1, rows, TILE), lambda s: (s, 0, 0)),
            pl.BlockSpec((rows, depth), lambda s: (0, 0)),
        ],
        out_shape=[
            jax.ShapeDtypeStruct((shards, rows, cols), BF),
            jax.ShapeDtypeStruct((shards, rows, width), BF),
            jax.ShapeDtypeStruct((shards, rows, TILE), F32),
            jax.ShapeDtypeStruct((rows, depth), F32),
        ],
        scratch_shapes=[pltpu.VMEM((TILE, SPAN), F32)],
        compiler_params=pltpu.CompilerParams(vmem_limit_bytes=40 * MIB),
        cost_estimate=pl.CostEstimate(flops=shards * 2 * 10**9, bytes_accessed=shards * 4 * 10**6, transcendentals=0),
        name="attn_fwd",
    )(meta, n1, a, rel)


def ffn_kernel(n2_ref, cot_ref, i_ref, w_ref, out_ref, gn_ref, gi_ref, gw_ref):
    step = pl.program_id(0)
    c0 = 0.7978845608028654
    c1 = 0.044715
    n2 = n2_ref[...]
    cot = cot_ref[...]
    pre = dot_nn(n2, i_ref[0])
    square = pre * pre
    th = jnp.tanh(pre * (c0 + (c0 * c1) * square))
    half = 0.5 * (1.0 + th)
    act = (pre * half).astype(BF)
    slope = half + (0.5 * pre) * (1.0 - th * th) * (c0 + (3.0 * c0 * c1) * square)
    out = dot_nn(act, w_ref[0])
    gp = (dot_nt(cot, w_ref[0]) * slope).astype(BF)
    gn = dot_nt(gp, i_ref[0])

    @pl.when(step == 0)
    def _():
        out_ref[...] = out
        gn_ref[...] = gn

    @pl.when(step > 0)
    def _():
        out_ref[...] += out
        gn_ref[...] += gn

    gi_ref[0] = dot_tn(n2, gp).astype(BF)
    gw_ref[0] = dot_tn(act, cot).astype(BF)


def ffn(n2, cot, i, w):
    shards, depth, units = i.shape
    rows = n2.shape[0]
    full = pl.BlockSpec((rows, depth), lambda s: (0, 0))
    i_spec = pl.BlockSpec((1, depth, units), lambda s: (s, 0, 0))
    w_spec = pl.BlockSpec((1, units, depth), lambda s: (s, 0, 0))
    return pl.pallas_call(
        ffn_kernel,
        grid=(shards,),
        in_specs=[full, full, i_spec, w_spec],
        out_specs=[full, full, i_spec, w_spec],
        out_shape=[
            jax.ShapeDtypeStruct((rows, depth), F32),
            jax.ShapeDtypeStruct((rows, depth), F32),
            jax.ShapeDtypeStruct(i.shape, BF),
            jax.ShapeDtypeStruct(w.shape, BF),
        ],
        compiler_params=pltpu.CompilerParams(vmem_limit_bytes=48 * MIB),
        cost_estimate=pl.CostEstimate(flops=shards * 5 * 10**9, bytes_accessed=shards * 8 * 10**6, transcendentals=0),
        name="ffn",
    )(n2, cot, i, w)


def attn_bwd_kernel(
    slots, heads, meta_ref, n1_ref, gh_ref, a_ref, qkv_ref, o_ref, lse_ref, rel_ref,
    ga_ref, gn_ref, diag_ref, band, acc, gs_all, pb_all, gq_all,
):
    step = pl.program_id(0)
    width = heads * HEAD
    gh = gh_ref[...]
    go_all = dot_nn(gh, a_ref[0, :, :width]).astype(BF)
    masks = mask_rows(meta_ref, slots)
    gq_all[:, :width] = jnp.zeros((gq_all.shape[0], width), BF)
    diag_ref[0] = jnp.zeros(diag_ref.shape[1:], F32)
    for h in range(heads):
        band[...] = bias_band(rel_ref[0, h : h + 1, :].astype(F32))
        acc[...] = jnp.zeros_like(acc)
        q = qkv_ref[0, :, width + h * HEAD : width + (h + 1) * HEAD]
        k = qkv_ref[0, :, 2 * width + h * HEAD : 2 * width + (h + 1) * HEAD]
        v = qkv_ref[0, :, 3 * width + h * HEAD : 3 * width + (h + 1) * HEAD]
        go = go_all[:, h * HEAD : (h + 1) * HEAD]
        for i in range(BIG // TILE):
            rows = slice(i * TILE, (i + 1) * TILE)
            window = slice((3 - i) * TILE, (7 - i) * TILE)
            s = dot_nt(q[rows], k) + band[:, window] + masks[i // 2]
            p = jnp.exp(s - lse_ref[0, rows, h : h + 1])
            dp = dot_nt(go[rows], v)
            inner = jnp.sum(p * dp, axis=1, keepdims=True)
            gs = (p * (dp - inner)).astype(BF)
            gs_all[rows, :] = gs
            pb_all[rows, :] = p.astype(BF)
            acc[:, window] += gs.astype(F32)
        gq_all[:, width + h * HEAD : width + (h + 1) * HEAD] = dot_nn(gs_all[...], k).astype(BF)
        gq_all[:, 2 * width + h * HEAD : 2 * width + (h + 1) * HEAD] = dot_tn(gs_all[...], q).astype(BF)
        gq_all[:, 3 * width + h * HEAD : 3 * width + (h + 1) * HEAD] = dot_tn(pb_all[...], go).astype(BF)
        fold = acc[...]
        n = TILE // 2
        while n >= 8:
            fold = fold[:n] + pltpu.roll(fold[n:], SPAN - n, 1)
            n //= 2
        line = fold[0:1]
        for j in range(1, 8):
            line = line + pltpu.roll(fold[j : j + 1], SPAN - j, 1)
        diag_ref[0, h : h + 1, :] = line
    grads = gq_all[...]
    gn = dot_nt(grads, a_ref[0])

    @pl.when(step == 0)
    def _():
        gn_ref[...] = gn

    @pl.when(step > 0)
    def _():
        gn_ref[...] += gn

    ga_ref[0] = dot_tn(n1_ref[...], grads).astype(BF)
    ga_ref[0, :, :width] = dot_tn(gh, o_ref[0]).astype(BF)


def attn_bwd(meta, n1, gh, a, qkv, o, lse, rel, slots, heads):
    shards, depth, cols = a.shape
    rows = n1.shape[0]
    width = heads * HEAD
    full = pl.BlockSpec((rows, depth), lambda s: (0, 0))
    a_spec = pl.BlockSpec((1, depth, cols), lambda s: (s, 0, 0))
    return pl.pallas_call(
        functools.partial(attn_bwd_kernel, slots, heads),
        grid=(shards,),
        in_specs=[
            pl.BlockSpec(memory_space=pltpu.SMEM),
            full,
            full,
            a_spec,
            pl.BlockSpec((1, rows, cols), lambda s: (s, 0, 0)),
            pl.BlockSpec((1, rows, width), lambda s: (s, 0, 0)),
            pl.BlockSpec((1, rows, TILE), lambda s: (s, 0, 0)),
            pl.BlockSpec((1,) + rel.shape[1:], lambda s: (s, 0, 0)),
        ],
        out_specs=[a_spec, full, pl.BlockSpec((1, 8, SPAN), lambda s: (s, 0, 0))],
        out_shape=[
            jax.ShapeDtypeStruct(a.shape, BF),
            jax.ShapeDtypeStruct((rows, depth), F32),
            jax.ShapeDtypeStruct((shards, 8, SPAN), F32),
        ],
        scratch_shapes=[
            pltpu.VMEM((TILE, SPAN), F32),
            pltpu.VMEM((TILE, SPAN), F32),
            pltpu.VMEM((BIG, BIG), BF),
            pltpu.VMEM((BIG, BIG), BF),
            pltpu.VMEM((rows, cols), BF),
        ],
        compiler_params=pltpu.CompilerParams(vmem_limit_bytes=48 * MIB),
        cost_estimate=pl.CostEstimate(flops=shards * 4 * 10**9, bytes_accessed=shards * 8 * 10**6, transcendentals=0),
        name="attn_bwd",
    )(meta, n1, gh, a, qkv, o, lse, rel)


def place_kernel(starts, count, index_ref, *refs):
    parts, out_ref, sems = refs[:-2], refs[-2], refs[-1]
    rows = parts[0].shape[1]
    copies = []
    j = 0
    for part in parts:
        for e in range(part.shape[0] // count):
            first = pl.multiple_of(index_ref[j] * rows, rows)
            for s in range(count):
                copies.append(
                    pltpu.make_async_copy(
                        part.at[e * count + s],
                        out_ref.at[s, pl.ds(first, rows), :],
                        sems.at[j * count + s],
                    )
                )
            j += 1
    for copy in copies:
        copy.start()
    for copy in copies:
        copy.wait()


def place(index, parts, count):
    blocks = index.shape[0]
    rows, cols = parts[0].shape[1:]
    return pl.pallas_call(
        functools.partial(place_kernel, None, count),
        in_specs=[pl.BlockSpec(memory_space=pltpu.SMEM)] + [pl.BlockSpec(memory_space=pl.ANY)] * len(parts),
        out_specs=pl.BlockSpec(memory_space=pl.ANY),
        out_shape=jax.ShapeDtypeStruct((count, blocks * rows, cols), parts[0].dtype),
        scratch_shapes=[pltpu.SemaphoreType.DMA((blocks * count,))],
        name="place",
    )(index, *parts)


class Ring:
    def __init__(self, n_dp, n_mp, depth):
        self.n_dp, self.n_mp = n_dp, n_mp
        self.all_bits = (n_dp - 1).bit_length()
        self.bits = min(3, self.all_bits)
        self.d = lax.axis_index("dp")
        self.z = lax.axis_index("mp")
        self.blocks = 1 << self.bits
        self.block_rows = depth // self.blocks
        self.low = self.d & (self.blocks - 1)

    def row_block(self, low):
        return ((low & 1) << (self.bits - 1)) | (low >> 1)

    def swap(self, x, bit):
        return lax.ppermute(x, "dp", [(i, i ^ (1 << bit)) for i in range(self.n_dp)])

    def pull(self, x, shift):
        return lax.ppermute(x, "mp", [(i, (i - shift) % self.n_mp) for i in range(self.n_mp)])

    def push(self, x, shift):
        return lax.ppermute(x, "mp", [(i, (i + shift) % self.n_mp) for i in range(self.n_mp)])

    def order(self, flip):
        high = list(range(1, self.bits))
        return (high[::-1] if flip else high) + [0]

    def gather(self, arr, flip):
        count = arr.shape[0]
        order = self.order(flip)
        masks = [0]
        for bit in order[:-1]:
            arr = jnp.concatenate([arr, self.swap(arr, bit)], axis=0)
            masks = masks + [m | (1 << bit) for m in masks]
        parts = [arr, self.swap(arr, order[-1])]
        masks = masks + [m | (1 << order[-1]) for m in masks]
        index = jnp.stack([self.row_block(self.low ^ m) for m in masks]).astype(jnp.int32)
        return place(index, parts, count)

    def own_block(self, mats):
        first = self.row_block(self.low) * self.block_rows
        return lax.dynamic_slice_in_dim(mats, first, self.block_rows, axis=1)

    def scatter(self, mats, flip):
        count, _, cols = mats.shape
        arr = mats.reshape((count,) + (2,) * self.bits + (self.block_rows, cols))
        axes = [0] + list(range(self.bits - 1, 0, -1))
        order = self.order(flip)[::-1]
        for bit in order:
            axis = 1 + axes.index(bit)
            axes.remove(bit)
            mine = (self.low >> bit) & 1
            send = lax.dynamic_index_in_dim(arr, 1 - mine, axis, keepdims=False)
            keep = lax.dynamic_index_in_dim(arr, mine, axis, keepdims=False)
            arr = (keep.astype(F32) + self.swap(send, bit).astype(F32)).astype(BF)
        for bit in range(self.bits, self.all_bits):
            arr = (arr.astype(F32) + self.swap(arr, bit).astype(F32)).astype(BF)
        return arr

    def owners(self, pieces):
        total = pieces[0].astype(F32)
        for s in range(1, self.n_mp):
            total = total + self.push(pieces[s], s).astype(F32)
        return total


def rms_forward(values, gain_vec):
    inv_root = lax.rsqrt(jnp.mean(values * values, axis=1, keepdims=True) + EPS)
    unit_rows = values * inv_root
    return (unit_rows, inv_root, unit_rows * gain_vec)


def rms_backward(grad_normed, unit_rows, inv_root, gain_vec):
    grad_unit = grad_normed * gain_vec
    grad_gain = jnp.sum(grad_normed * unit_rows, axis=0)
    centred = grad_unit - unit_rows * jnp.mean(grad_unit * unit_rows, axis=1, keepdims=True)
    return (inv_root * centred, grad_gain)


def body(
    n_dp, n_mp, inputs, gain_attn, w_query, w_key, w_value, w_out, rel_table, gain_ffn, w_in, w_down,
    cotangent, bucket, lengths,
):
    depth = inputs.shape[1]
    buckets, heads = rel_table.shape
    width = heads * HEAD
    slots = lengths.shape[1]
    ring = Ring(n_dp, n_mp, depth)
    shifts = range(1, n_mp)

    a_own = jnp.concatenate([w_out.T, w_query, w_key, w_value], axis=1)[None]
    i_own = w_in[None]
    w_own = w_down[None]
    one_hot = jnp.asarray(offset_one_hot(buckets), BF)
    rel_own = lax.dot_general(rel_table, one_hot, (((0,), (1,)), ((), ())), preferred_element_type=F32)
    rel_own = jnp.concatenate([rel_own.astype(BF), jnp.zeros((16 - heads, SPAN), BF)], axis=0)[None]

    a_piece = ring.own_block(a_own)
    a_in = jnp.concatenate([ring.pull(a_piece, s) for s in shifts], axis=0)
    rel_rest = jnp.concatenate([ring.pull(rel_own, s) for s in shifts], axis=0)
    f_piece = ring.own_block(jnp.concatenate([i_own, w_own], axis=0))
    f_in = [ring.pull(f_piece, s) for s in shifts]

    a_rest = ring.gather(a_in, False)
    f_full = [ring.gather(f_in[j], j % 2 == 0) for j in range(n_mp - 1)]

    meta = jnp.concatenate([bucket, (ring.z * BIG)[None].astype(jnp.int32), lengths[0]])
    x_value = inputs.astype(F32)
    gain_one = gain_attn.astype(F32)
    unit_one, root_one, normed_one = rms_forward(x_value, gain_one)
    n1 = normed_one.astype(BF)
    qkv0, o0, lse0, hp0 = attn_fwd(meta, n1, a_own, rel_own, slots, heads)
    qkv1, o1, lse1, hp1 = attn_fwd(meta, n1, a_rest, rel_rest, slots, heads)
    hidden = x_value + (hp0 + hp1)
    gain_two = gain_ffn.astype(F32)
    unit_two, root_two, normed_two = rms_forward(hidden, gain_two)
    n2 = normed_two.astype(BF)

    f_mats = [(i_own, w_own)] + [(f[0:1], f[1:2]) for f in f_full]
    outs, gns, f_grads = [], [], []
    for s in range(n_mp):
        out, gn, gi, gw = ffn(n2, cotangent, f_mats[s][0], f_mats[s][1])
        outs.append(out)
        gns.append(gn)
        f_grads.append(ring.scatter(jnp.concatenate([gi, gw], axis=0), s % 2 == 0))
    outputs = (hidden + sum(outs)).astype(BF)
    grad_middle, grad_gain_two = rms_backward(sum(gns), unit_two, root_two, gain_two)
    grad_hidden = cotangent.astype(F32) + grad_middle
    gh = grad_hidden.astype(BF)

    ga0, gn0, diag0 = attn_bwd(meta, n1, gh, a_own, qkv0, o0, lse0, rel_own, slots, heads)
    ga1, gn1, diag1 = attn_bwd(meta, n1, gh, a_rest, qkv1, o1, lse1, rel_rest, slots, heads)
    a_grads = ring.scatter(jnp.concatenate([ga0, ga1], axis=0), False)
    grad_lower, grad_gain_one = rms_backward(gn0 + gn1, unit_one, root_one, gain_one)
    grad_inputs = (grad_hidden + grad_lower).astype(BF)

    f_sum = ring.owners(f_grads).astype(BF)
    f_out = ring.gather(f_sum, True)
    a_sum = ring.owners([a_grads[s] for s in range(n_mp)]).astype(BF)
    a_out = ring.gather(a_sum[None], False)[0].astype(F32)
    grad_in, grad_down = f_out[0].astype(F32), f_out[1].astype(F32)
    grad_out = a_out[:, :width].T
    grad_query, grad_key, grad_value = (a_out[:, j * width : (j + 1) * width] for j in (1, 2, 3))

    diag = jnp.concatenate([diag0, diag1], axis=0)[:, :heads]
    tables = jnp.einsum("shu,ub->sbh", diag, jnp.asarray(offset_one_hot(buckets)), precision=lax.Precision.HIGHEST)
    size = buckets * heads
    small = jnp.concatenate([tables.reshape(-1), grad_gain_one, grad_gain_two])
    for bit in range(ring.all_bits):
        small = small + ring.swap(small, bit)
    gains = small[n_mp * size :]
    mine = [jnp.concatenate([small[s * size : (s + 1) * size], gains]) for s in range(n_mp)]
    total = ring.owners(mine)
    grad_table = total[:size].reshape(buckets, heads)
    grad_gain_one = total[size : size + depth]
    grad_gain_two = total[size + depth :]
    return (
        outputs, grad_inputs, grad_query, grad_key, grad_value, grad_out, grad_table,
        grad_gain_one, grad_gain_two, grad_in, grad_down,
    )


def solution(mesh):
    placed = (
        P(("dp", "mp"), None), P(), P(None, "mp"), P(None, "mp"), P(None, "mp"), P("mp", None),
        P(None, "mp"), P(), P(None, "mp"), P("mp", None), P(("dp", "mp"), None), P("dp"), P("dp", None),
    )
    return jax.shard_map(
        functools.partial(body, mesh.shape["dp"], mesh.shape["mp"]),
        mesh=mesh,
        in_specs=placed,
        out_specs=(
            P(("dp", "mp"), None), P(("dp", "mp"), None), P(None, "mp"), P(None, "mp"), P(None, "mp"),
            P("mp", None), P(None, "mp"), P(), P(), P(None, "mp"), P("mp", None),
        ),
        check_vma=False,
    )
```

```python
import functools

import jax
import jax.numpy as jnp
import numpy as np
from jax import lax
from jax.experimental import pallas as pl
from jax.experimental.pallas import tpu as pltpu
from jax.sharding import PartitionSpec as P

BIG = 512
HEAD = 64
EPS = 1e-06
THRESHOLDS = (12, 16, 23, 32, 46, 64, 91)
MASKED = -1e30
TILE = 128
SPAN = 1024
BF = jnp.bfloat16
F32 = jnp.float32
MIB = 1024 * 1024


def offset_one_hot(buckets):
    u = np.arange(SPAN)
    offsets = np.where(u < 896, u, u - SPAN) - 3 * TILE
    distance = np.abs(offsets)
    far = 8 + sum((distance >= t).astype(np.int32) for t in THRESHOLDS)
    bucket = np.where(distance < 8, distance, far) + np.where(offsets > 0, 16, 0)
    return (bucket[:, None] == np.arange(buckets)[None, :]).astype(np.float32)


def dot_nn(a, b):
    return lax.dot_general(a, b, (((1,), (0,)), ((), ())), preferred_element_type=F32)


def dot_nt(a, b):
    return lax.dot_general(a, b, (((1,), (1,)), ((), ())), preferred_element_type=F32)


def dot_tn(a, b):
    return lax.dot_general(a, b, (((0,), (0,)), ((), ())), preferred_element_type=F32)


def mask_rows(meta_ref, slots):
    bucket = meta_ref[0]
    half = BIG // 2
    segs, starts = [], []
    for part in range(2):
        first = meta_ref[1] + part * half
        seg = jnp.int32(0)
        for j in range(1, slots):
            seg = seg + jnp.where(first >= j * bucket, 1, 0).astype(jnp.int32)
        segs.append(seg)
        starts.append(first - seg * bucket)
    iota = lax.broadcasted_iota(jnp.int32, (1, half), 1)
    rows = []
    for query_part in range(2):
        cols = []
        for key_part in range(2):
            same = segs[query_part] == segs[key_part]
            limit = jnp.where(same, meta_ref[2 + segs[key_part]] - starts[key_part], 0)
            cols.append(jnp.where(iota < limit, 0.0, MASKED).astype(F32))
        rows.append(jnp.concatenate(cols, axis=1))
    return rows


def bias_band(rel_row):
    wide = jnp.broadcast_to(rel_row, (TILE, SPAN))
    return pltpu.roll(wide, 0, 1, stride=1, stride_axis=0)


def put_blocks(index_ref, part_refs, mat, which=0):
    if len(part_refs) == 1:
        mat[...] = part_refs[0][which]
        return
    rows = part_refs[0].shape[1]
    for j, part in enumerate(part_refs):
        first = pl.multiple_of(index_ref[j] * rows, rows)
        mat[pl.ds(first, rows), :] = part[which]


def accumulate(step, ref, value):
    @pl.when(step == 0)
    def _():
        ref[...] = value

    @pl.when(step > 0)
    def _():
        ref[...] += value


def attn_fwd_kernel(slots, heads, parts, meta_ref, index_ref, n1_ref, *refs):
    a_parts, (rel_ref, qkv_ref, o_ref, lse_ref, hp_ref, mat, band) = refs[:parts], refs[parts:]
    step = pl.program_id(0)
    width = heads * HEAD
    put_blocks(index_ref, a_parts, mat)
    qkv_ref[0] = dot_nn(n1_ref[...], mat[...]).astype(BF)
    masks = mask_rows(meta_ref, slots)
    for h in range(heads):
        band[...] = bias_band(rel_ref[0, h : h + 1, :].astype(F32))
        q = qkv_ref[0, :, width + h * HEAD : width + (h + 1) * HEAD]
        k = qkv_ref[0, :, 2 * width + h * HEAD : 2 * width + (h + 1) * HEAD]
        v = qkv_ref[0, :, 3 * width + h * HEAD : 3 * width + (h + 1) * HEAD]
        for i in range(BIG // TILE):
            rows = slice(i * TILE, (i + 1) * TILE)
            s = dot_nt(q[rows], k) + band[:, (3 - i) * TILE : (7 - i) * TILE] + masks[i // 2]
            top = jnp.max(s, axis=1, keepdims=True)
            e = jnp.exp(s - top)
            total = jnp.sum(e, axis=1, keepdims=True)
            pb = (e * (1.0 / total)).astype(BF)
            o_ref[0, rows, h * HEAD : (h + 1) * HEAD] = dot_nn(pb, v).astype(BF)
            lse_ref[0, rows, h : h + 1] = top + jnp.log(total)
    accumulate(step, hp_ref, dot_nt(o_ref[0], mat[:, :width]))


def block_specs(parts):
    return [pl.BlockSpec((1,) + part.shape[1:], lambda s: (s, 0, 0)) for part in parts]


SMEM = pl.BlockSpec(memory_space=pltpu.SMEM)


def attn_fwd(meta, index, n1, a_parts, rel, slots, heads):
    shards, _, cols = a_parts[0].shape
    rows, depth = n1.shape
    width = heads * HEAD
    return pl.pallas_call(
        functools.partial(attn_fwd_kernel, slots, heads, len(a_parts)),
        grid=(shards,),
        in_specs=[SMEM, SMEM, pl.BlockSpec((rows, depth), lambda s: (0, 0))]
        + block_specs(a_parts)
        + [pl.BlockSpec((1,) + rel.shape[1:], lambda s: (s, 0, 0))],
        out_specs=[
            pl.BlockSpec((1, rows, cols), lambda s: (s, 0, 0)),
            pl.BlockSpec((1, rows, width), lambda s: (s, 0, 0)),
            pl.BlockSpec((1, rows, TILE), lambda s: (s, 0, 0)),
            pl.BlockSpec((rows, depth), lambda s: (0, 0)),
        ],
        out_shape=[
            jax.ShapeDtypeStruct((shards, rows, cols), BF),
            jax.ShapeDtypeStruct((shards, rows, width), BF),
            jax.ShapeDtypeStruct((shards, rows, TILE), F32),
            jax.ShapeDtypeStruct((rows, depth), F32),
        ],
        scratch_shapes=[pltpu.VMEM((depth, cols), BF), pltpu.VMEM((TILE, SPAN), F32)],
        compiler_params=pltpu.CompilerParams(vmem_limit_bytes=40 * MIB),
        cost_estimate=pl.CostEstimate(flops=shards * 2 * 10**9, bytes_accessed=shards * 4 * 10**6, transcendentals=0),
        name="attn_fwd",
    )(meta, index, n1, *a_parts, rel)


def ffn_kernel(parts, index_ref, side_ref, n2_ref, cot_ref, *refs):
    f_parts, (out_ref, gn_ref, send_ref, keep_ref, i_mat, w_mat, act_ref) = refs[:parts], refs[parts:]
    c0 = 0.7978845608028654
    c1 = 0.044715
    put_blocks(index_ref, f_parts, i_mat, 0)
    put_blocks(index_ref, f_parts, w_mat, 1)
    cot = cot_ref[...]
    pre = dot_nn(n2_ref[...], i_mat[...])
    square = pre * pre
    th = jnp.tanh(pre * (c0 + (c0 * c1) * square))
    half = 0.5 * (1.0 + th)
    act = (pre * half).astype(BF)
    act_ref[...] = act
    slope = half + (0.5 * pre) * (1.0 - th * th) * (c0 + (3.0 * c0 * c1) * square)
    out_ref[...] = dot_nn(act, w_mat[...])
    gp = (dot_nt(cot, w_mat[...]) * slope).astype(BF)
    gn_ref[...] = dot_nt(gp, i_mat[...])
    size = send_ref.shape[1]
    for ref, side in ((send_ref, 1 - side_ref[0]), (keep_ref, side_ref[0])):
        cols = pl.ds(pl.multiple_of(side * size, size), size)
        ref[0] = dot_tn(n2_ref[:, cols], gp).astype(BF)
        ref[1] = dot_tn(act_ref[:, cols], cot).astype(BF)


def ffn(index, side, n2, cot, f_parts):
    rows, depth = n2.shape
    units = f_parts[0].shape[2]
    vmem = pl.BlockSpec(memory_space=pltpu.VMEM)
    half = jax.ShapeDtypeStruct((2, depth // 2, units), BF)
    return pl.pallas_call(
        functools.partial(ffn_kernel, len(f_parts)),
        in_specs=[SMEM, SMEM] + [vmem] * (2 + len(f_parts)),
        out_specs=[vmem] * 4,
        out_shape=[jax.ShapeDtypeStruct((rows, depth), F32), jax.ShapeDtypeStruct((rows, depth), F32), half, half],
        scratch_shapes=[pltpu.VMEM((depth, units), BF), pltpu.VMEM((units, depth), BF), pltpu.VMEM((rows, units), BF)],
        compiler_params=pltpu.CompilerParams(vmem_limit_bytes=48 * MIB),
        cost_estimate=pl.CostEstimate(flops=5 * 10**9, bytes_accessed=8 * 10**6, transcendentals=0),
        name="ffn",
    )(index, side, n2, cot, *f_parts)


def attn_bwd_kernel(slots, heads, parts, meta_ref, index_ref, side_ref, n1_ref, gh_ref, *refs):
    a_parts = refs[:parts]
    qkv_ref, o_ref, lse_ref, rel_ref = refs[parts : parts + 4]
    send_ref, keep_ref, gn_ref, diag_ref, mat, band, acc, gs_all, pb_all, gq_all = refs[parts + 4 :]
    step = pl.program_id(0)
    width = heads * HEAD
    put_blocks(index_ref, a_parts, mat)
    gh = gh_ref[...]
    go_all = dot_nn(gh, mat[:, :width]).astype(BF)
    masks = mask_rows(meta_ref, slots)
    gq_all[:, :width] = jnp.zeros((gq_all.shape[0], width), BF)
    diag_ref[0] = jnp.zeros(diag_ref.shape[1:], F32)
    for h in range(heads):
        band[...] = bias_band(rel_ref[0, h : h + 1, :].astype(F32))
        acc[...] = jnp.zeros_like(acc)
        q = qkv_ref[0, :, width + h * HEAD : width + (h + 1) * HEAD]
        k = qkv_ref[0, :, 2 * width + h * HEAD : 2 * width + (h + 1) * HEAD]
        v = qkv_ref[0, :, 3 * width + h * HEAD : 3 * width + (h + 1) * HEAD]
        go = go_all[:, h * HEAD : (h + 1) * HEAD]
        for i in range(BIG // TILE):
            rows = slice(i * TILE, (i + 1) * TILE)
            window = slice((3 - i) * TILE, (7 - i) * TILE)
            s = dot_nt(q[rows], k) + band[:, window] + masks[i // 2]
            p = jnp.exp(s - lse_ref[0, rows, h : h + 1])
            dp = dot_nt(go[rows], v)
            inner = jnp.sum(p * dp, axis=1, keepdims=True)
            gs = (p * (dp - inner)).astype(BF)
            gs_all[rows, :] = gs
            pb_all[rows, :] = p.astype(BF)
            acc[:, window] += gs.astype(F32)
        gq_all[:, width + h * HEAD : width + (h + 1) * HEAD] = dot_nn(gs_all[...], k).astype(BF)
        gq_all[:, 2 * width + h * HEAD : 2 * width + (h + 1) * HEAD] = dot_tn(gs_all[...], q).astype(BF)
        gq_all[:, 3 * width + h * HEAD : 3 * width + (h + 1) * HEAD] = dot_tn(pb_all[...], go).astype(BF)
        fold = acc[...]
        n = TILE // 2
        while n >= 8:
            fold = fold[:n] + pltpu.roll(fold[n:], SPAN - n, 1)
            n //= 2
        line = fold[0:1]
        for j in range(1, 8):
            line = line + pltpu.roll(fold[j : j + 1], SPAN - j, 1)
        diag_ref[0, h : h + 1, :] = line
    grads = gq_all[...]
    accumulate(step, gn_ref, dot_nt(grads, mat[...]))
    size = send_ref.shape[1]
    for ref, side in ((send_ref, 1 - side_ref[0]), (keep_ref, side_ref[0])):
        cols = pl.ds(pl.multiple_of(side * size, size), size)
        ref[0] = dot_tn(n1_ref[:, cols], grads).astype(BF)
        ref[0, :, :width] = dot_tn(gh_ref[:, cols], o_ref[0]).astype(BF)


def attn_bwd(meta, index, side, n1, gh, a_parts, qkv, o, lse, rel, slots, heads):
    shards, _, cols = a_parts[0].shape
    rows, depth = n1.shape
    full = pl.BlockSpec((rows, depth), lambda s: (0, 0))
    kept = [qkv, o, lse, rel]
    half = pl.BlockSpec((1, depth // 2, cols), lambda s: (s, 0, 0))
    half_shape = jax.ShapeDtypeStruct((shards, depth // 2, cols), BF)
    return pl.pallas_call(
        functools.partial(attn_bwd_kernel, slots, heads, len(a_parts)),
        grid=(shards,),
        in_specs=[SMEM, SMEM, SMEM, full, full] + block_specs(a_parts) + block_specs(kept),
        out_specs=[half, half, full, pl.BlockSpec((1, 8, SPAN), lambda s: (s, 0, 0))],
        out_shape=[
            half_shape,
            half_shape,
            jax.ShapeDtypeStruct((rows, depth), F32),
            jax.ShapeDtypeStruct((shards, 8, SPAN), F32),
        ],
        scratch_shapes=[
            pltpu.VMEM((depth, cols), BF),
            pltpu.VMEM((TILE, SPAN), F32),
            pltpu.VMEM((TILE, SPAN), F32),
            pltpu.VMEM((BIG, BIG), BF),
            pltpu.VMEM((BIG, BIG), BF),
            pltpu.VMEM((rows, cols), BF),
        ],
        compiler_params=pltpu.CompilerParams(vmem_limit_bytes=48 * MIB),
        cost_estimate=pl.CostEstimate(flops=shards * 4 * 10**9, bytes_accessed=shards * 8 * 10**6, transcendentals=0),
        name="attn_bwd",
    )(meta, index, side, n1, gh, *a_parts, qkv, o, lse, rel)


def fold_kernel(axis, side_ref, keep_ref, recv_ref, *out_refs):
    if axis is None:
        out_refs[0][...] = (keep_ref[...].astype(F32) + recv_ref[...].astype(F32)).astype(BF)
        return
    for ref, side in zip(out_refs, (1 - side_ref[0], side_ref[0])):
        at = (slice(None),) * axis + (side,)
        ref[...] = (keep_ref[at].astype(F32) + recv_ref[at].astype(F32)).astype(BF)


def fold(side, keep, recv, axis):
    vmem = pl.BlockSpec(memory_space=pltpu.VMEM)
    shape = keep.shape if axis is None else keep.shape[:axis] + keep.shape[axis + 1 :]
    outs = 1 if axis is None else 2
    return pl.pallas_call(
        functools.partial(fold_kernel, axis),
        in_specs=[SMEM, vmem, vmem],
        out_specs=[vmem] * outs,
        out_shape=[jax.ShapeDtypeStruct(shape, BF)] * outs,
        compiler_params=pltpu.CompilerParams(vmem_limit_bytes=24 * MIB),
        cost_estimate=pl.CostEstimate(flops=10**6, bytes_accessed=4 * 10**6, transcendentals=0),
        name="fold",
    )(side, keep, recv)


def finish_kernel(width, index_ref, *refs):
    parts, (out_ref, q_ref, k_ref, v_ref, mat) = refs[:-5], refs[-5:]
    put_blocks(index_ref, parts, mat)
    out_ref[...] = mat[:, :width].astype(F32).T
    for j, ref in enumerate((q_ref, k_ref, v_ref)):
        ref[...] = mat[:, (j + 1) * width : (j + 2) * width].astype(F32)


def finish(index, parts, width):
    depth = len(parts) * parts[0].shape[1]
    cols = parts[0].shape[2]
    vmem = pl.BlockSpec(memory_space=pltpu.VMEM)
    wide = jax.ShapeDtypeStruct((depth, width), F32)
    return pl.pallas_call(
        functools.partial(finish_kernel, width),
        in_specs=[SMEM] + [vmem] * len(parts),
        out_specs=[vmem] * 4,
        out_shape=[jax.ShapeDtypeStruct((width, depth), F32), wide, wide, wide],
        scratch_shapes=[pltpu.VMEM((depth, cols), BF)],
        compiler_params=pltpu.CompilerParams(vmem_limit_bytes=32 * MIB),
        cost_estimate=pl.CostEstimate(flops=10**6, bytes_accessed=4 * 10**6, transcendentals=0),
        name="finish",
    )(index, *parts)


class Ring:
    def __init__(self, n_dp, n_mp, depth):
        self.n_dp, self.n_mp = n_dp, n_mp
        self.all_bits = (n_dp - 1).bit_length()
        self.bits = min(3, self.all_bits)
        self.d = lax.axis_index("dp")
        self.z = lax.axis_index("mp")
        self.blocks = 1 << self.bits
        self.block_rows = depth // self.blocks
        self.low = self.d & (self.blocks - 1)
        self.sides = [((self.low >> bit) & 1)[None].astype(jnp.int32) for bit in range(self.bits)]
        self.orders = {flip: self.order(flip) for flip in (False, True)}
        self.index = {flip: self.block_index(flip) for flip in (False, True)}

    def row_block(self, low):
        return ((low & 1) << (self.bits - 1)) | (low >> 1)

    def order(self, flip):
        high = list(range(1, self.bits))
        return (high[::-1] if flip else high) + [0]

    def block_index(self, flip):
        masks = [0]
        for bit in self.orders[flip]:
            masks = masks + [m | (1 << bit) for m in masks]
        low = self.low ^ jnp.asarray(masks, jnp.int32)
        return self.row_block(low).astype(jnp.int32)

    def swap(self, x, bit):
        return lax.ppermute(x, "dp", [(i, i ^ (1 << bit)) for i in range(self.n_dp)])

    def pull(self, x, shift):
        return lax.ppermute(x, "mp", [(i, (i - shift) % self.n_mp) for i in range(self.n_mp)])

    def push(self, x, shift):
        return lax.ppermute(x, "mp", [(i, (i + shift) % self.n_mp) for i in range(self.n_mp)])

    def gather(self, arr, flip):
        parts = [arr]
        for bit in self.orders[flip]:
            parts = parts + [self.swap(part, bit) for part in parts]
        return parts

    def own_block(self, mats):
        first = self.row_block(self.low) * self.block_rows
        return lax.dynamic_slice_in_dim(mats, first, self.block_rows, axis=1)

    def scatter(self, send, keep, flip):
        count, _, cols = keep.shape
        shape = (count,) + (2,) * (self.bits - 1) + (self.block_rows, cols)
        axes = list(range(self.bits - 1, 0, -1))
        order = self.orders[flip][-2::-1] + [None]
        bit = 0
        send, keep = send.reshape(shape), keep.reshape(shape)
        for later in order:
            recv = self.swap(send, bit)
            if later is None:
                keep = fold(self.sides[0], keep, recv, None)[0]
            else:
                axis = 1 + axes.index(later)
                axes.remove(later)
                send, keep = fold(self.sides[later], keep, recv, axis)
            bit = later
        for bit in range(self.bits, self.all_bits):
            keep = fold(self.sides[0], keep, self.swap(keep, bit), None)[0]
        return keep

    def owners(self, pieces):
        total = pieces[0].astype(F32)
        for s in range(1, self.n_mp):
            total = total + self.push(pieces[s], s).astype(F32)
        return total

    def gather_all(self, piece):
        groups = [[g + i for i in range(self.blocks)] for g in range(0, self.n_dp, self.blocks)]
        both = lax.all_gather(piece, "dp", axis_index_groups=groups)
        return jnp.concatenate([both[0::2], both[1::2]], axis=0).transpose(1, 0, 2, 3).reshape(
            piece.shape[0], -1, piece.shape[2]
        )


def rms_forward(values, gain_vec):
    inv_root = lax.rsqrt(jnp.mean(values * values, axis=1, keepdims=True) + EPS)
    unit_rows = values * inv_root
    return (unit_rows, inv_root, unit_rows * gain_vec)


def rms_backward(grad_normed, unit_rows, inv_root, gain_vec):
    grad_unit = grad_normed * gain_vec
    grad_gain = jnp.sum(grad_normed * unit_rows, axis=0)
    centred = grad_unit - unit_rows * jnp.mean(grad_unit * unit_rows, axis=1, keepdims=True)
    return (inv_root * centred, grad_gain)


def body(
    n_dp, n_mp, inputs, gain_attn, w_query, w_key, w_value, w_out, rel_table, gain_ffn, w_in, w_down,
    cotangent, bucket, lengths,
):
    depth = inputs.shape[1]
    buckets, heads = rel_table.shape
    width = heads * HEAD
    slots = lengths.shape[1]
    ring = Ring(n_dp, n_mp, depth)
    shifts = range(1, n_mp)

    a_own = jnp.concatenate([w_out.T, w_query, w_key, w_value], axis=1)[None]
    f_own = jnp.stack([w_in, w_down])
    one_hot = jnp.asarray(offset_one_hot(buckets), BF)
    rel_own = lax.dot_general(rel_table, one_hot, (((0,), (1,)), ((), ())), preferred_element_type=F32)
    rel_own = jnp.concatenate([rel_own.astype(BF), jnp.zeros((16 - heads, SPAN), BF)], axis=0)[None]

    a_piece = ring.own_block(a_own)
    a_in = jnp.concatenate([ring.pull(a_piece, s) for s in shifts], axis=0)
    rel_rest = jnp.concatenate([ring.pull(rel_own, s) for s in shifts], axis=0)
    f_piece = ring.own_block(f_own)
    f_in = [ring.pull(f_piece, s) for s in shifts]

    a_rest = ring.gather(a_in, False)
    f_mats = [[f_own]] + [ring.gather(f_in[j], j % 2 == 0) for j in range(n_mp - 1)]

    meta = jnp.concatenate([bucket, (ring.z * BIG)[None].astype(jnp.int32), lengths[0]])
    x_value = inputs.astype(F32)
    gain_one = gain_attn.astype(F32)
    unit_one, root_one, normed_one = rms_forward(x_value, gain_one)
    n1 = normed_one.astype(BF)
    a_index, f_index = ring.index[False], [ring.index[False]] + [ring.index[j % 2 == 0] for j in range(n_mp - 1)]
    qkv0, o0, lse0, hp0 = attn_fwd(meta, a_index, n1, [a_own], rel_own, slots, heads)
    qkv1, o1, lse1, hp1 = attn_fwd(meta, a_index, n1, a_rest, rel_rest, slots, heads)
    hidden = x_value + (hp0 + hp1)
    gain_two = gain_ffn.astype(F32)
    unit_two, root_two, normed_two = rms_forward(hidden, gain_two)
    n2 = normed_two.astype(BF)

    side = ring.sides[0]
    outs, gns, f_grads = [], [], []
    for s in range(n_mp):
        out, gn, send, keep = ffn(f_index[s], side, n2, cotangent, f_mats[s])
        outs.append(out)
        gns.append(gn)
        f_grads.append(ring.scatter(send, keep, s % 2 == 0))
    outputs = (hidden + sum(outs)).astype(BF)
    grad_middle, grad_gain_two = rms_backward(sum(gns), unit_two, root_two, gain_two)
    grad_hidden = cotangent.astype(F32) + grad_middle
    gh = grad_hidden.astype(BF)

    send0, keep0, gn0, diag0 = attn_bwd(meta, a_index, side, n1, gh, [a_own], qkv0, o0, lse0, rel_own, slots, heads)
    send1, keep1, gn1, diag1 = attn_bwd(meta, a_index, side, n1, gh, a_rest, qkv1, o1, lse1, rel_rest, slots, heads)
    a_first = ring.scatter(send0, keep0, True)
    a_later = ring.scatter(send1, keep1, False)
    grad_lower, grad_gain_one = rms_backward(gn0 + gn1, unit_one, root_one, gain_one)
    grad_inputs = (grad_hidden + grad_lower).astype(BF)

    f_out = ring.gather_all(ring.owners(f_grads).astype(BF))
    grad_in, grad_down = f_out[0].astype(F32), f_out[1].astype(F32)
    a_sum = ring.owners([a_first] + [a_later[s : s + 1] for s in range(n_mp - 1)]).astype(BF)
    grad_out, grad_query, grad_key, grad_value = finish(a_index, ring.gather(a_sum, False), width)

    diag = jnp.concatenate([diag0, diag1], axis=0)[:, :heads]
    tables = jnp.einsum("shu,ub->sbh", diag, jnp.asarray(offset_one_hot(buckets)), precision=lax.Precision.HIGHEST)
    size = buckets * heads
    small = jnp.concatenate([tables.reshape(-1), grad_gain_one, grad_gain_two])
    for bit in range(ring.all_bits):
        small = small + ring.swap(small, bit)
    gains = small[n_mp * size :]
    mine = [jnp.concatenate([small[s * size : (s + 1) * size], gains]) for s in range(n_mp)]
    total = ring.owners(mine)
    grad_table = total[:size].reshape(buckets, heads)
    grad_gain_one = total[size : size + depth]
    grad_gain_two = total[size + depth :]
    return (
        outputs, grad_inputs, grad_query, grad_key, grad_value, grad_out, grad_table,
        grad_gain_one, grad_gain_two, grad_in, grad_down,
    )


def solution(mesh):
    placed = (
        P(("dp", "mp"), None), P(), P(None, "mp"), P(None, "mp"), P(None, "mp"), P("mp", None),
        P(None, "mp"), P(), P(None, "mp"), P("mp", None), P(("dp", "mp"), None), P("dp"), P("dp", None),
    )
    return jax.shard_map(
        functools.partial(body, mesh.shape["dp"], mesh.shape["mp"]),
        mesh=mesh,
        in_specs=placed,
        out_specs=(
            P(("dp", "mp"), None), P(("dp", "mp"), None), P(None, "mp"), P(None, "mp"), P(None, "mp"),
            P("mp", None), P(None, "mp"), P(), P(), P(None, "mp"), P("mp", None),
        ),
        check_vma=False,
    )
```

```python
import functools

import jax
import jax.numpy as jnp
import numpy as np
from jax import lax
from jax.experimental import pallas as pl
from jax.experimental.pallas import tpu as pltpu
from jax.sharding import PartitionSpec as P

BIG = 512
HEAD = 64
EPS = 1e-06
THRESHOLDS = (12, 16, 23, 32, 46, 64, 91)
MASKED = -1e30
TILE = 128
SPAN = 512
EXTRA = 16
BF = jnp.bfloat16
F32 = jnp.float32
MIB = 1024 * 1024
LIMIT = 60
SMEM = pl.BlockSpec(memory_space=pltpu.SMEM)
VMEM = pl.BlockSpec(memory_space=pltpu.VMEM)
ANY = pl.BlockSpec(memory_space=pl.ANY)


def offset_one_hot(buckets):
    offsets = np.arange(SPAN) - SPAN // 2
    distance = np.abs(offsets)
    far = 8 + sum((distance >= t).astype(np.int32) for t in THRESHOLDS)
    bucket = np.where(distance < 8, distance, far) + np.where(offsets > 0, buckets // 2, 0)
    return (np.arange(TILE)[:, None] == bucket[None, :]).astype(np.float32)


def dot_nn(a, b):
    return lax.dot_general(a, b, (((1,), (0,)), ((), ())), preferred_element_type=F32)


def dot_nt(a, b):
    return lax.dot_general(a, b, (((1,), (1,)), ((), ())), preferred_element_type=F32)


def dot_tn(a, b):
    return lax.dot_general(a, b, (((0,), (0,)), ((), ())), preferred_element_type=F32)


def like(shape, dtype):
    return jax.ShapeDtypeStruct(shape, dtype)


def params(mib):
    return pltpu.CompilerParams(vmem_limit_bytes=mib * MIB)


def cost(micros):
    return pl.CostEstimate(flops=micros * 10**9, bytes_accessed=micros * 10**6, transcendentals=0)


def mask_rows(meta_ref, slots):
    bucket = meta_ref[0]
    half = BIG // 2
    segs, starts = [], []
    for part in range(2):
        first = meta_ref[1] + part * half
        seg = jnp.int32(0)
        for j in range(1, slots):
            seg = seg + jnp.where(first >= j * bucket, 1, 0).astype(jnp.int32)
        segs.append(seg)
        starts.append(first - seg * bucket)
    iota = lax.broadcasted_iota(jnp.int32, (1, half), 1)
    rows = []
    for query_part in range(2):
        cols = []
        for key_part in range(2):
            same = segs[query_part] == segs[key_part]
            limit = jnp.where(same, meta_ref[2 + segs[key_part]] - starts[key_part], 0)
            cols.append(jnp.where(iota < limit, 0.0, MASKED).astype(F32))
        rows.append(jnp.concatenate(cols, axis=1))
    return rows


def bias_band(rel_row):
    return pltpu.roll(jnp.broadcast_to(rel_row, (TILE, SPAN)), 0, 1, stride=1, stride_axis=0)


def masked_bias(i, near, rel_row, mask):
    tiles = []
    for j in range(BIG // TILE):
        keys = mask[:, j * TILE : (j + 1) * TILE]
        if abs(j - i) <= 1:
            tiles.append(near[:, (j - i + 2) * TILE : (j - i + 3) * TILE] + keys)
        else:
            far = rel_row[:, SPAN - 1 :] if j > i else rel_row[:, :1]
            tiles.append(jnp.broadcast_to(far + keys, (TILE, TILE)))
    return jnp.concatenate(tiles, axis=1)


class Mover:
    def __init__(self, sems):
        self.sems, self.used, self.out = sems, 0, []

    def copy(self, source, target):
        one = pltpu.make_async_copy(source, target, self.sems.at[self.used])
        self.used += 1
        one.start()
        return one

    def load(self, source, target):
        return [self.copy(source, target)]

    def blocks(self, index_ref, part_refs, mat, which):
        copies, j, first = [], 0, 0
        for part in part_refs:
            if index_ref is None:
                copies.append(self.copy(part, mat.at[pl.ds(first, part.shape[0])]))
                first += part.shape[0]
                continue
            rows = part.shape[2]
            for e in range(part.shape[0]):
                at = pl.ds(pl.multiple_of(index_ref[j] * rows, rows), rows)
                copies.append(self.copy(part.at[e, which], mat.at[at]))
                j += 1
        return copies

    def store(self, source, target):
        self.out.append(self.copy(source, target))

    def halves(self, side_ref, source, send, keep):
        size = source.shape[0] // 2
        for ref, side in ((send, 1 - side_ref[0]), (keep, side_ref[0])):
            self.store(source.at[pl.ds(pl.multiple_of(side * size, size), size)], ref)

    def finish(self):
        wait(self.out)


def wait(copies):
    for one in copies:
        one.wait()


def put_blocks(index_ref, part_refs, mat, which):
    j = 0
    for part in part_refs:
        rows = part.shape[2]
        for e in range(part.shape[0]):
            mat[pl.ds(pl.multiple_of(index_ref[j] * rows, rows), rows), :] = part[e, which].astype(mat.dtype)
            j += 1


def rms(values):
    root = lax.rsqrt(jnp.mean(values * values, axis=1, keepdims=True) + EPS)
    return values * root, root


def rms_back(grad, unit, root, gain):
    scaled = grad * gain
    centred = scaled - unit * jnp.mean(scaled * unit, axis=1, keepdims=True)
    return root * centred, jnp.sum(grad * unit, axis=0, keepdims=True)


def head_slices(qkv_ref, heads, h):
    width = heads * HEAD
    return [qkv_ref[:, j * width + h * HEAD : j * width + (h + 1) * HEAD] for j in (1, 2, 3)]


def forward_scores(h, band, rel, masks, scores, lse_ref):
    probs = []
    for i in range(BIG // TILE):
        rows = slice(i * TILE, (i + 1) * TILE)
        s = scores[h, rows, :] + masked_bias(i, band[h], rel[h : h + 1], masks[i // 2])
        top = jnp.max(s, axis=1, keepdims=True)
        e = jnp.exp(s - top)
        total = jnp.sum(e, axis=1, keepdims=True)
        probs.append((e * (1.0 / total)).astype(BF))
        lse_ref[rows, h : h + 1] = top + jnp.log(total)
    return jnp.concatenate(probs, axis=0)


def attn_fwd_kernel(slots, heads, parts, start, shards, own, last, meta_ref, *refs):
    refs = list(refs)
    take = lambda n: [refs.pop(0) for _ in range(n)]
    index_ref = None if own else take(1)[0]
    n1_hbm = take(1)[0]
    a_parts = take(parts)
    tab_hbm, hot_hbm, prior_hbm = take(3)
    gain_hbm = take(1)[0] if last else None
    qkv_out, o_out, lse_out, hid_out = take(4)
    n2_out = take(1)[0] if last else None
    n1_ref, mat, tab_ref, hot_ref, prior_ref, gain_ref, qkv_ref, o_ref, lse_ref, hid_ref, n2_ref, band, scores, sems = refs
    move = Mover(sems)
    width = heads * HEAD
    half = BIG // 2
    got_mat = [move.blocks(index_ref, a_parts, mat.at[0], start)]
    got_n1 = move.load(n1_hbm, n1_ref)
    got_tab = move.load(tab_hbm.at[pl.ds(start, shards)], tab_ref) + move.load(hot_hbm, hot_ref)
    masks = mask_rows(meta_ref, slots)
    wait(got_tab)
    wait(got_n1)
    for s in range(shards):
        rel = dot_nn(tab_ref[s], hot_ref[...])
        for h in range(heads):
            band[h] = bias_band(rel[h : h + 1])
        wait(got_mat[s])
        if s == 0:
            got_mat += [move.blocks(index_ref, a_parts, mat.at[t], start + t) for t in range(1, shards)]
            got_prior = move.load(prior_hbm, prior_ref)
            if last:
                got_prior += move.load(gain_hbm, gain_ref)
        qkv_ref[s] = dot_nt(n1_ref[...], mat[s]).astype(BF)
        move.store(qkv_ref.at[s], qkv_out.at[s])
        for h in range(heads):
            q, k, _ = head_slices(qkv_ref.at[s], heads, h)
            scores[h] = dot_nt(q, k)
        for h in range(heads):
            v = head_slices(qkv_ref.at[s], heads, h)[2]
            pb = forward_scores(h, band, rel, masks, scores, lse_ref.at[s])
            o_ref[s, :, h * HEAD : (h + 1) * HEAD] = dot_nn(pb, v).astype(BF)
        move.store(o_ref.at[s], o_out.at[s])
        move.store(lse_ref.at[s], lse_out.at[s])
        if s == 0:
            wait(got_prior)
        for part in range(2):
            rows = pl.ds(part * half, half)
            before = prior_ref[rows, :].astype(F32) if s == 0 else hid_ref[rows, :]
            hidden = before + dot_nn(o_ref[s, rows, :], mat[s, :width, :])
            hid_ref[rows, :] = hidden
            if s == shards - 1:
                move.store(hid_ref.at[rows], hid_out.at[rows])
                if last:
                    n2_ref[rows, :] = (rms(hidden)[0] * gain_ref[...].astype(F32)).astype(BF)
                    move.store(n2_ref.at[rows], n2_out.at[rows])
    move.finish()


HBM = pl.BlockSpec(memory_space=pltpu.HBM)


def attn_fwd(meta, index, n1, a_parts, start, shards, tab, hot, prior, gain, slots, heads):
    own, last = index is None, gain is not None
    rows, depth = n1.shape
    width = heads * HEAD
    cols = 4 * width
    scalars = [meta] if own else [meta, index]
    args = [n1, *a_parts, tab, hot, prior] + ([gain] if last else [])
    out_shape = [
        like((shards, rows, cols), BF),
        like((shards, rows, width), BF),
        like((shards, rows, TILE), F32),
        like((rows, depth), F32),
    ]
    if last:
        out_shape.append(like((rows, depth), BF))
    return pl.pallas_call(
        functools.partial(attn_fwd_kernel, slots, heads, len(a_parts), start, shards, own, last),
        in_specs=[SMEM] * len(scalars) + [ANY] * len(args),
        out_specs=[HBM] * len(out_shape),
        out_shape=out_shape,
        scratch_shapes=[
            pltpu.VMEM((rows, depth), BF),
            pltpu.VMEM((shards, cols, depth), BF),
            pltpu.VMEM((shards,) + tab.shape[1:], BF),
            pltpu.VMEM(hot.shape, BF),
            pltpu.VMEM(prior.shape, prior.dtype),
            pltpu.VMEM((1, depth), BF),
            pltpu.VMEM((shards, rows, cols), BF),
            pltpu.VMEM((shards, rows, width), BF),
            pltpu.VMEM((shards, rows, TILE), F32),
            pltpu.VMEM((rows, depth), F32),
            pltpu.VMEM((rows, depth), BF),
            pltpu.VMEM((heads, TILE, SPAN), F32),
            pltpu.VMEM((heads, BIG, BIG), F32),
            pltpu.SemaphoreType.DMA((12 + 12 * shards,)),
        ],
        compiler_params=params(LIMIT),
        cost_estimate=cost(16 * shards),
        name="attn_fwd",
    )(*scalars, *args)


def attn_bwd_kernel(slots, heads, shards, rest, sources, own, first, befores, meta_ref, side_ref, index_ref, *refs):
    refs = list(refs)
    take = lambda n: [refs.pop(0) for _ in range(n)]
    last = None in shards
    count = len(shards)
    n1_hbm, gh_hbm, hot_hbm = take(3)
    rest_parts = take(rest)
    rest_tab = take(1)[0]
    rest_kept, rest_at = {}, {}
    for places in sources:
        kept = take(3) + [rest_tab]
        for base, which in enumerate(places):
            rest_kept[which], rest_at[which] = kept, base
    own_parts, own_kept = (take(own), take(4)) if last else ([], [])
    prior_hbm = None if first else take(1)[0]
    if last:
        x_hbm, gain_hbm, ghid_hbm, gain2_hbm = take(4)
        tabs_hbm = take(befores)
        send_out, keep_out, gin_out = take(3)
    else:
        send_out, keep_out, gn_out, tabs_out = take(4)
    n1_ref, gh_ref, hot_ref, mat, qkv_ref, o_ref, lse_ref, tab_ref, gn_ref = take(9)
    band, acc, gs_all, pb_all, gq_all, grads_mat, tabs_ref, sems = take(8)
    move = Mover(sems)
    width = heads * HEAD
    half = BIG // 2
    if last:
        x_ref, gain_ref, ghid_ref, gain2_ref, before_ref, small, packed = take(7)

    def load(c):
        which = shards[c]
        parts, kept = (own_parts, own_kept) if which is None else (rest_parts, rest_kept[which])
        at = 0 if which is None else which
        base = 0 if which is None else rest_at[which]
        got_tab = move.load(kept[3].at[at], tab_ref.at[c])
        got_mat = move.blocks(None if which is None else index_ref, parts, mat.at[c], at)
        got_kept = move.load(kept[0].at[base], qkv_ref.at[c]) + move.load(kept[2].at[base], lse_ref.at[c])
        return got_tab, got_mat, got_kept, move.load(kept[1].at[base], o_ref.at[c])

    got_first = move.load(hot_hbm, hot_ref) + move.load(gh_hbm, gh_ref)
    got = [load(0)]
    got_n1 = move.load(n1_hbm, n1_ref)
    masks = mask_rows(meta_ref, slots)
    lane = lax.broadcasted_iota(jnp.int32, (1, SPAN), 1)
    wait(got_first)
    gh = gh_ref[...]
    for c in range(count):
        got_tab, got_mat, got_kept, got_late = got[c]
        acc[...] = jnp.zeros(acc.shape, F32)
        gq_all[c, :, :width] = jnp.zeros((gq_all.shape[1], width), BF)
        wait(got_tab)
        rel = dot_nn(tab_ref[c], hot_ref[...])
        for h in range(heads):
            band[h] = bias_band(rel[h : h + 1])
        wait(got_mat)
        go_all = dot_nt(gh, mat[c, :width, :]).astype(BF)
        wait(got_kept)
        if c == 0:
            got += [load(t) for t in range(1, count)]
            got_prior = [] if first else move.load(prior_hbm, gn_ref)
            if last:
                got_prior += move.load(x_hbm, x_ref) + move.load(gain_hbm, gain_ref)
                got_prior += move.load(ghid_hbm, ghid_ref) + move.load(gain2_hbm, gain2_ref)
                done = 0
                for ref in tabs_hbm:
                    got_prior += move.load(ref, before_ref.at[pl.ds(done, ref.shape[0])])
                    done += ref.shape[0]
        far = []
        for h in range(heads):
            q, k, v = head_slices(qkv_ref.at[c], heads, h)
            go = go_all[:, h * HEAD : (h + 1) * HEAD]
            low = jnp.zeros((1, TILE), F32)
            high = jnp.zeros((1, TILE), F32)
            for i in range(BIG // TILE):
                rows = slice(i * TILE, (i + 1) * TILE)
                s = dot_nt(q[rows], k) + masked_bias(i, band[h], rel[h : h + 1], masks[i // 2])
                p = jnp.exp(s - lse_ref[c, rows, h : h + 1])
                dp = dot_nt(go[rows], v)
                inner = jnp.sum(p * dp, axis=1, keepdims=True)
                gs = (p * (dp - inner)).astype(BF)
                gs_all[h, rows, :] = gs
                pb_all[h, rows, :] = p.astype(BF)
                wide = gs.astype(F32)
                for j in range(BIG // TILE):
                    tile = wide[:, j * TILE : (j + 1) * TILE]
                    if abs(j - i) <= 1:
                        acc[h, :, (j - i + 2) * TILE : (j - i + 3) * TILE] += tile
                    elif j > i:
                        high = high + jnp.sum(tile, axis=0, keepdims=True)
                    else:
                        low = low + jnp.sum(tile, axis=0, keepdims=True)
            at = lambda j: slice(j * width + h * HEAD, j * width + (h + 1) * HEAD)
            gq_all[c, :, at(1)] = dot_nn(gs_all[h], k).astype(BF)
            gq_all[c, :, at(2)] = dot_tn(gs_all[h], q).astype(BF)
            gq_all[c, :, at(3)] = dot_tn(pb_all[h], go).astype(BF)
            far.append((low, high))
        wait(got_late)
        if c == 0:
            wait(got_n1)
        grads_mat[c] = dot_tn(gq_all[c], n1_ref[...]).astype(BF)
        grads_mat[c, :width, :] = dot_tn(o_ref[c], gh).astype(BF)
        size = pl.ds(0, grads_mat.shape[1] // 2)
        move.halves(side_ref, grads_mat.at[c], send_out.at[c, size], keep_out.at[c, size])
        near = acc[...]
        n = TILE // 2
        while n >= 8:
            near = near[:, :n] + pltpu.roll(near[:, n:], SPAN - n, 2)
            n //= 2
        line = near[:, 0:1]
        for j in range(1, 8):
            line = line + pltpu.roll(near[:, j : j + 1], SPAN - j, 2)
        lines = []
        for h, (low, high) in enumerate(far):
            ends = jnp.where(lane == 0, jnp.sum(low, axis=1, keepdims=True), 0.0)
            ends = ends + jnp.where(lane == SPAN - 1, jnp.sum(high, axis=1, keepdims=True), 0.0)
            lines.append(line[h] + ends)
        lines = jnp.concatenate(lines + [jnp.zeros((8 - heads, SPAN), F32)], axis=0)
        tabs_ref[c] = lax.dot_general(
            lines, hot_ref[...].astype(F32), (((1,), (1,)), ((), ())),
            precision=lax.Precision.HIGHEST, preferred_element_type=F32,
        )
        if c == 0:
            wait(got_prior)
        for part in range(2):
            rows = pl.ds(part * half, half)
            gn = dot_nn(gq_all[c, rows, :], mat[c])
            if not (first and c == 0):
                gn = gn + gn_ref[rows, :]
            gn_ref[rows, :] = gn
            if c == count - 1 and not last:
                move.store(gn_ref.at[rows], gn_out.at[rows])
    if not last:
        move.store(tabs_ref, tabs_out)
        move.finish()
        return
    unit, root = rms(x_ref[...].astype(F32))
    back, gain_grad = rms_back(gn_ref[...], unit, root, gain_ref[...].astype(F32))
    small[...] = jnp.zeros_like(small)
    total = before_ref.shape[0] + count
    tables = [tabs_ref[count - 1]] + [before_ref[j] for j in range(total - count)]
    tables += [tabs_ref[c] for c in range(count - 1)]
    for row, value in enumerate(tables):
        for h in range(heads):
            small[row : row + 1, h * TILE : (h + 1) * TILE] = value[h : h + 1]
    small[total : total + 1, :] = gain_grad
    small[total + 1 : total + 2, :] = gain2_ref[0:1, :]
    packed[...] = split_small(small[...])
    tail = pl.ds(grads_mat.shape[1] // 2, EXTRA)
    for c in range(count):
        move.store(packed, send_out.at[c, tail])
        move.store(packed, keep_out.at[c, tail])
    gh_ref[...] = (ghid_ref[...] + back).astype(BF)
    move.store(gh_ref, gin_out)
    move.finish()


def split_small(value):
    high = value.astype(BF)
    low = (value - high.astype(F32)).astype(BF)
    return jnp.concatenate([high.astype(F32), low.astype(F32)], axis=0).astype(BF)


def join_small(packed):
    wide = packed.astype(F32)
    return wide[: EXTRA // 2] + wide[EXTRA // 2 :]


def attn_bwd(meta, index, side, n1, gh, hot, shards, rest, own, prior, final, slots, heads):
    last, first = None in shards, prior is None
    count = len(shards)
    rows, depth = n1.shape
    width = heads * HEAD
    cols = 4 * width
    parts, tab, sources = rest
    sources = [(places, kept) for places, kept in sources if set(places) & set(shards)]
    args = [n1, gh, hot, *parts, tab] + [k for _, kept in sources for k in kept]
    args += [*own[0], *own[1]] if last else []
    args += ([] if first else [prior]) + (list(final) if last else [])
    befores = len(final) - 4 if last else 0
    half = like((count, cols // 2 + (EXTRA if last else 0), depth), BF)
    if last:
        out_shape = [half, half, like((rows, depth), BF)]
    else:
        out_shape = [half, half, like((rows, depth), F32), like((count, 8, TILE), F32)]
    scratch = [
        pltpu.VMEM((rows, depth), BF),
        pltpu.VMEM((rows, depth), BF),
        pltpu.VMEM(hot.shape, BF),
        pltpu.VMEM((count, cols, depth), BF),
        pltpu.VMEM((count, rows, cols), BF),
        pltpu.VMEM((count, rows, width), BF),
        pltpu.VMEM((count, rows, TILE), F32),
        pltpu.VMEM((count,) + tab.shape[1:], BF),
        pltpu.VMEM((rows, depth), F32),
        pltpu.VMEM((heads, TILE, SPAN), F32),
        pltpu.VMEM((heads, TILE, SPAN), F32),
        pltpu.VMEM((heads, BIG, BIG), BF),
        pltpu.VMEM((heads, BIG, BIG), BF),
        pltpu.VMEM((count, rows, cols), BF),
        pltpu.VMEM((count, cols, depth), BF),
        pltpu.VMEM((count, 8, TILE), F32),
        pltpu.SemaphoreType.DMA((16 + 18 * count,)),
    ]
    if last:
        scratch += [
            pltpu.VMEM((rows, depth), BF),
            pltpu.VMEM((1, depth), BF),
            pltpu.VMEM((rows, depth), F32),
            pltpu.VMEM((8, depth), F32),
            pltpu.VMEM((sum(f.shape[0] for f in final[4:]), 8, TILE), F32),
            pltpu.VMEM((8, depth), F32),
            pltpu.VMEM((EXTRA, depth), BF),
        ]
    return pl.pallas_call(
        functools.partial(
            attn_bwd_kernel, slots, heads, tuple(shards), len(parts), tuple(p for p, _ in sources),
            len(own[0]) if last else 0, first, befores,
        ),
        in_specs=[SMEM] * 3 + [ANY] * len(args),
        out_specs=[HBM] * len(out_shape),
        out_shape=out_shape,
        scratch_shapes=scratch,
        compiler_params=params(LIMIT),
        cost_estimate=cost(32 * count),
        name="attn_bwd",
    )(meta, side, index, *args)


def ffn_kernel(parts, first, last, side_ref, *refs):
    refs = list(refs)
    take = lambda n: [refs.pop(0) for _ in range(n)]
    count = len(parts)
    index_refs = take(sum(1 for n in parts if n))
    n2_hbm, cot_hbm = take(2)
    f_parts = [take(n or 2) for n in parts]
    out_in, gn_in = (None, None) if first else take(2)
    if last:
        hid_in, gain_in = take(2)
        out_out, send_out, keep_out, ghid_out, gh_out, gg_out = take(6)
    else:
        out_out, gn_out, send_out, keep_out = take(4)
    n2_ref, cot_ref, i_mat, w_mat, act_ref, gp_ref, gi_mat, gw_mat, out_ref, gn_ref, sems = take(11)
    move = Mover(sems)
    hid_ref, gain_ref, y_ref, gg_ref = take(4) if last else [None] * 4

    def load(c):
        if not parts[c]:
            return move.load(f_parts[c][0], i_mat.at[c]), move.load(f_parts[c][1], w_mat.at[c])
        index_ref = index_refs[sum(1 for n in parts[:c] if n)]
        return tuple(move.blocks(index_ref, f_parts[c], mat.at[c], j) for j, mat in enumerate((i_mat, w_mat)))

    got_n2 = move.load(n2_hbm, n2_ref)
    got = [load(0)]
    got_cot = move.load(cot_hbm, cot_ref)
    c0 = 0.7978845608028654
    c1 = 0.044715
    size = n2_ref.shape[0] // 2
    gain_grad = None
    for c in range(count):
        wait(got[c][0])
        if c == 0:
            wait(got_n2)
            got += [load(t) for t in range(1, count)]
            got_sums = [] if first else move.load(out_in, out_ref) + move.load(gn_in, gn_ref)
            if last:
                got_sums += move.load(hid_in, hid_ref) + move.load(gain_in, gain_ref)
        pre = dot_nn(n2_ref[...], i_mat[c])
        square = pre * pre
        th = jnp.tanh(pre * (c0 + (c0 * c1) * square))
        half = 0.5 * (1.0 + th)
        act_ref[c] = (pre * half).astype(BF)
        slope = half + (0.5 * pre) * (1.0 - th * th) * (c0 + (3.0 * c0 * c1) * square)
        wait(got[c][1])
        if c == 0:
            wait(got_cot)
        cot = cot_ref[...]
        gp_ref[c] = (dot_nt(cot, w_mat[c]) * slope).astype(BF)
        gw_mat[c] = dot_tn(act_ref[c], cot).astype(BF)
        move.halves(side_ref, gw_mat.at[c], send_out.at[2 * c + 1], keep_out.at[2 * c + 1])
        gi_mat[c] = dot_tn(n2_ref[...], gp_ref[c]).astype(BF)
        move.halves(side_ref, gi_mat.at[c], send_out.at[2 * c], keep_out.at[2 * c])
        if c == 0:
            wait(got_sums)
        ending = c == count - 1
        for part in range(2):
            rows = pl.ds(part * size, size)
            gn = dot_nt(gp_ref[c, rows, :], i_mat[c])
            out = dot_nn(act_ref[c, rows, :], w_mat[c])
            if not (first and c == 0):
                out = out + out_ref[rows, :]
                gn = gn + gn_ref[rows, :]
            if not (last and ending):
                gn_ref[rows, :] = gn
                out_ref[rows, :] = out
                if ending:
                    move.store(gn_ref.at[rows], gn_out.at[rows])
                    move.store(out_ref.at[rows], out_out.at[rows])
                continue
            hidden = hid_ref[rows, :]
            y_ref[rows, :] = (hidden + out).astype(BF)
            move.store(y_ref.at[rows], out_out.at[rows])
            unit, root = rms(hidden)
            back, gain_part = rms_back(gn, unit, root, gain_ref[...].astype(F32))
            gain_grad = gain_part if gain_grad is None else gain_grad + gain_part
            grad_hidden = cot_ref[rows, :].astype(F32) + back
            gn_ref[rows, :] = grad_hidden
            move.store(gn_ref.at[rows], ghid_out.at[rows])
            n2_ref[rows, :] = grad_hidden.astype(BF)
            move.store(n2_ref.at[rows], gh_out.at[rows])
    if last:
        gg_ref[...] = jnp.broadcast_to(gain_grad, gg_ref.shape)
        move.store(gg_ref, gg_out)
    move.finish()


def ffn(side, n2, cot, shards, sums, final):
    first, last = sums is None, final is not None
    rows, depth = n2.shape
    count = len(shards)
    units = shards[-1][1][0].shape[-1]
    half = like((2 * count, depth // 2, units), BF)
    total = like((rows, depth), F32)
    scalars = [side] + [index for index, _ in shards if index is not None]
    args = [n2, cot] + [p for _, ps in shards for p in ps]
    args += ([] if first else list(sums)) + ([] if not last else list(final))
    if last:
        out_shape = [like((rows, depth), BF), half, half, total, like((rows, depth), BF), like((8, depth), F32)]
    else:
        out_shape = [total, total, half, half]
    scratch = [
        pltpu.VMEM((rows, depth), BF),
        pltpu.VMEM((rows, depth), BF),
        pltpu.VMEM((count, depth, units), BF),
        pltpu.VMEM((count, units, depth), BF),
        pltpu.VMEM((count, rows, units), BF),
        pltpu.VMEM((count, rows, units), BF),
        pltpu.VMEM((count, depth, units), BF),
        pltpu.VMEM((count, units, depth), BF),
        pltpu.VMEM((rows, depth), F32),
        pltpu.VMEM((rows, depth), F32),
        pltpu.SemaphoreType.DMA((20 + 20 * count,)),
    ]
    if last:
        scratch += [
            pltpu.VMEM((rows, depth), F32),
            pltpu.VMEM((1, depth), BF),
            pltpu.VMEM((rows, depth), BF),
            pltpu.VMEM((8, depth), F32),
        ]
    return pl.pallas_call(
        functools.partial(ffn_kernel, tuple(0 if i is None else len(p) for i, p in shards), first, last),
        in_specs=[SMEM] * len(scalars) + [ANY] * len(args),
        out_specs=[HBM] * len(out_shape),
        out_shape=out_shape,
        scratch_shapes=scratch,
        compiler_params=params(LIMIT),
        cost_estimate=cost(32 * count),
        name="ffn",
    )(*scalars, *args)


def prep_kernel(rows, count, index_ref, *refs):
    mats, (tab_ref, in_ref, down_ref, a_ref, f_ref, sems) = refs[:count], refs[count:]
    block = index_ref[0]
    first = pl.ds(pl.multiple_of(block * rows, rows), rows)
    copies = [
        pltpu.make_async_copy(in_ref.at[first], f_ref.at[0], sems.at[0]),
        pltpu.make_async_copy(down_ref.at[first], f_ref.at[1], sems.at[1]),
    ]
    per = mats[0].shape[0] // rows

    def piece(j, mat):
        at = pl.ds(pl.multiple_of((block - j * per) * rows, rows), rows)
        return pltpu.make_async_copy(mat.at[at], a_ref.at[pl.ds(0, rows)], sems.at[2])

    for j, mat in enumerate(mats):
        @pl.when(block // per == j)
        def _():
            piece(j, mat).start()

    for copy in copies:
        copy.start()
    a_ref[rows:, :] = jnp.zeros((EXTRA, a_ref.shape[1]), BF)
    a_ref[rows:, :TILE] = tab_ref[...]
    for j, mat in enumerate(mats):
        @pl.when(block // per == j)
        def _():
            piece(j, mat).wait()

    for copy in copies:
        copy.wait()


def prep(index, mats, tab, w_in, w_down, rows):
    depth = w_in.shape[0]
    return pl.pallas_call(
        functools.partial(prep_kernel, rows, len(mats)),
        in_specs=[SMEM] + [ANY] * len(mats) + [VMEM, ANY, ANY],
        out_specs=[VMEM, VMEM],
        out_shape=[like((rows + EXTRA, depth), BF), like((2, rows, depth), BF)],
        scratch_shapes=[pltpu.SemaphoreType.DMA((3,))],
        compiler_params=params(60),
        cost_estimate=cost(1),
        name="prep",
    )(index, *mats, tab, w_in, w_down)


def join_kernel(count, *refs):
    parts, (a_ref, tab_ref) = refs[:count], refs[count:]
    rows = a_ref.shape[1]
    for j, part in enumerate(parts):
        a_ref[j] = part[:rows, :]
        tab_ref[j] = part[rows:, :TILE]


def join(parts):
    rows, depth = parts[0].shape
    return pl.pallas_call(
        functools.partial(join_kernel, len(parts)),
        in_specs=[VMEM] * len(parts),
        out_specs=[VMEM, VMEM],
        out_shape=[like((len(parts), rows - EXTRA, depth), BF), like((len(parts), EXTRA, TILE), BF)],
        compiler_params=params(16),
        cost_estimate=cost(1),
        name="join",
    )(*parts)


def row_runs(left, bit, rows):
    inner = rows
    for b in left[left.index(bit) + 1 :]:
        inner *= 2
    outer = 1
    for b in left[: left.index(bit)]:
        outer *= 2
    return [(o * 2 * inner, inner, o * inner) for o in range(outer)]


def fold_kernel(runs, extra, joined, sides_ref, *refs):
    if joined:
        keep_ref, recv_ref = refs[:2]
        n = keep_ref.shape[0] // 2
        ins = [(keep_ref.at[pl.ds(g * n, n)], recv_ref.at[pl.ds(g * n, n)]) for g in range(2)]
        outs = refs[2:]
    else:
        ins, outs = [refs[0:2], refs[2:4]], refs[4:]
    packed = None
    if extra:
        keep, recv = ins[1]
        tail = pl.ds(keep.shape[1] - extra, extra)
        packed = split_small(join_small(keep[0, tail, :]) + join_small(recv[0, tail, :]))
    for g, (keep, recv) in enumerate(ins):
        def total(rows):
            return (keep[:, rows, :].astype(F32) + recv[:, rows, :].astype(F32)).astype(BF)

        if runs is None:
            rows, n = outs[0].shape[1], outs[0].shape[0] // 2
            outs[0][g * n : (g + 1) * n] = total(pl.ds(0, rows))
            continue
        bit, group_runs = runs[g]
        mine = sides_ref[bit]
        for ref, side in ((outs[2 * g], 1 - mine), (outs[2 * g + 1], mine)):
            for source, length, target in group_runs:
                ref[:, target : target + length, :] = total(pl.ds(pl.multiple_of(source + side * length, length), length))
            if extra and g == 1:
                done = sum(length for _, length, _ in group_runs)
                for m in range(ref.shape[0]):
                    ref[m, done:, :] = packed
    if extra and runs is None:
        outs[1][...] = packed


def fold(sides, groups, runs, extra):
    joined = len(groups) == 1
    arrays = [a for group in groups for a in group]
    if joined:
        count = arrays[0].shape[0] // 2
        bodies = [arrays[0].shape[1] - extra] * 2
    else:
        count = arrays[0].shape[0]
        bodies = [arrays[0].shape[1], arrays[2].shape[1] - extra]
    cols = arrays[0].shape[2]
    if runs is None:
        out_shape = [like((2 * count, bodies[0], cols), BF)] + ([like((extra, cols), BF)] if extra else [])
    else:
        tails = (0, extra)
        out_shape = [like((count, bodies[g] // 2 + tails[g], cols), BF) for g in (0, 0, 1, 1)]
    return pl.pallas_call(
        functools.partial(fold_kernel, runs, extra, joined),
        in_specs=[SMEM] + [VMEM] * len(arrays),
        out_specs=[VMEM] * len(out_shape),
        out_shape=out_shape,
        compiler_params=params(24),
        cost_estimate=cost(1),
        name="fold",
    )(sides, *arrays)


def add_kernel(a_ref, b_ref, out_ref):
    out_ref[...] = (a_ref[...].astype(F32) + b_ref[...].astype(F32)).astype(BF)


def add(a, b):
    return pl.pallas_call(
        add_kernel, in_specs=[VMEM, VMEM], out_specs=VMEM, out_shape=like(a.shape, BF),
        compiler_params=params(16), cost_estimate=cost(1), name="add",
    )(a, b)


def add_small_kernel(a_ref, b_ref, out_ref):
    out_ref[...] = split_small(join_small(a_ref[...]) + join_small(b_ref[...]))


def add_small(a, b):
    return pl.pallas_call(
        add_small_kernel, in_specs=[VMEM, VMEM], out_specs=VMEM, out_shape=like(a.shape, BF),
        compiler_params=params(16), cost_estimate=cost(1), name="add_small",
    )(a, b)


def total_kernel(count, *refs):
    parts, out_ref = refs[:count], refs[count]
    total = parts[0][...].astype(F32)
    for part in parts[1:]:
        total = total + part[...].astype(F32)
    out_ref[...] = total.astype(BF)


def total_of(parts):
    return pl.pallas_call(
        functools.partial(total_kernel, len(parts)),
        in_specs=[VMEM] * len(parts),
        out_specs=VMEM,
        out_shape=like(parts[0].shape, BF),
        compiler_params=params(16),
        cost_estimate=cost(1),
        name="total",
    )(*parts)


def small_kernel(count, *refs):
    parts, (tab_ref, gains_ref) = refs[:count], refs[count:]
    table, gains = None, None
    for j, part in enumerate(parts):
        wide = join_small(part[...])
        table = wide[j : j + 1] if table is None else table + wide[j : j + 1]
        gains = wide if gains is None else gains + wide
    tab_ref[...] = jnp.broadcast_to(table, tab_ref.shape)
    gains_ref[...] = gains


def small_of(parts):
    depth = parts[0].shape[1]
    shape = like((EXTRA // 2, depth), F32)
    return pl.pallas_call(
        functools.partial(small_kernel, len(parts)),
        in_specs=[VMEM] * len(parts),
        out_specs=[VMEM, VMEM],
        out_shape=[shape, shape],
        compiler_params=params(16),
        cost_estimate=cost(1),
        name="small",
    )(*parts)


def cat_kernel(count, *refs):
    for j in range(count):
        refs[count][j] = refs[j][...]


def cat(parts):
    return pl.pallas_call(
        functools.partial(cat_kernel, len(parts)),
        in_specs=[VMEM] * len(parts),
        out_specs=VMEM,
        out_shape=like((len(parts),) + parts[0].shape, BF),
        compiler_params=params(16),
        cost_estimate=cost(1),
        name="cat",
    )(*parts)


def finish_kernel(count, split, index_ref, *refs):
    parts, out_refs, mat = refs[:count], refs[count:-1], refs[-1]
    for j in range(parts[0].shape[1]):
        if split:
            put_blocks(index_ref, parts, mat, j)
            rows = mat.shape[0] // len(out_refs)
            for i, ref in enumerate(out_refs):
                ref[...] = mat[i * rows : (i + 1) * rows, :].astype(F32)
        else:
            put_blocks(index_ref, parts, out_refs[j], j)


def finish(index, parts, outs, rows):
    depth = parts[0].shape[-1]
    split = parts[0].shape[1] != outs
    return pl.pallas_call(
        functools.partial(finish_kernel, len(parts), split),
        in_specs=[SMEM] + [VMEM] * len(parts),
        out_specs=[VMEM] * outs,
        out_shape=[like((rows, depth), F32)] * outs,
        scratch_shapes=[pltpu.VMEM((depth, depth), BF)],
        compiler_params=params(24),
        cost_estimate=cost(2),
        name="finish",
    )(index, *parts)


def bar(*values):
    return list(lax.optimization_barrier(values))


def after(x, *deps):
    return lax.optimization_barrier((x,) + deps)[0]


class Ring:
    def __init__(self, n_dp, n_mp, depth):
        self.n_dp, self.n_mp = n_dp, n_mp
        self.all_bits = (n_dp - 1).bit_length()
        self.bits = min(3, self.all_bits)
        self.z = lax.axis_index("mp")
        self.blocks = 1 << self.bits
        self.rows = depth // self.blocks
        self.low = lax.axis_index("dp") & (self.blocks - 1)
        self.sides = [((self.low >> bit) & 1)[None].astype(jnp.int32) for bit in range(self.bits)]
        self.all_sides = jnp.concatenate(self.sides)
        self.mine = self.row_block(self.low)[None].astype(jnp.int32)
        self.orders = {flip: self.order(flip) for flip in (False, True)}
        self.index = {flip: self.block_index(flip) for flip in (False, True)}

    def row_block(self, low):
        return ((low & 1) << (self.bits - 1)) | (low >> 1)

    def order(self, flip):
        high = list(range(1, self.bits))
        return (high[::-1] if flip else high) + [0]

    def block_index(self, flip):
        masks = [0]
        for bit in self.orders[flip]:
            masks = masks + [m | (1 << bit) for m in masks]
        low = self.low ^ jnp.asarray(masks, jnp.int32)
        return self.row_block(low).astype(jnp.int32)

    def swap(self, x, mask):
        return lax.ppermute(x, "dp", [(i, i ^ mask) for i in range(self.n_dp)])

    def pull(self, x, shift):
        return lax.ppermute(x, "mp", [(i, (i - shift) % self.n_mp) for i in range(self.n_mp)])

    def push(self, x, shift):
        return lax.ppermute(x, "mp", [(i, (i + shift) % self.n_mp) for i in range(self.n_mp)])

    def gather_all(self, piece):
        groups = [[g + i for i in range(self.blocks)] for g in range(0, self.n_dp, self.blocks)]
        return lax.all_gather(piece, "dp", axis_index_groups=groups)

    def group_index(self):
        return jnp.asarray([self.row_block(low) for low in range(self.blocks)], jnp.int32)


class Reduce:
    def __init__(self, ring, send, keep, extra=0):
        self.ring, self.extra = ring, extra
        order = list(range(1, ring.bits))
        self.orders = [order, order[::-1]]
        self.left = [order[::-1], order[::-1]]
        self.groups = [[keep, ring.swap(send, 1)]]
        self.done = False

    def received(self):
        return [group[1] for group in self.groups]

    def set_received(self, values):
        for group, value in zip(self.groups, values):
            group[1] = value

    def step(self):
        ring = self.ring
        if not self.orders[0]:
            out = fold(ring.all_sides, self.groups, None, self.extra)
            self.out, self.small = out[0], out[1] if self.extra else None
            for bit in range(ring.bits, ring.all_bits):
                self.out = add(self.out, ring.swap(self.out, 1 << bit))
                if self.extra:
                    self.small = add_small(self.small, ring.swap(self.small, 1 << bit))
            self.done = True
            return [self.out]
        runs, bits = [], []
        for g in range(2):
            bit = self.orders[g].pop(0)
            runs.append((bit, row_runs(self.left[g], bit, ring.rows)))
            self.left[g] = [b for b in self.left[g] if b != bit]
            bits.append(bit)
        outs = fold(ring.all_sides, self.groups, runs, self.extra)
        self.groups = [[outs[2 * g + 1], ring.swap(outs[2 * g], 1 << bits[g])] for g in range(2)]
        return [outs[1], outs[3]]


def body(
    n_dp, n_mp, inputs, gain_attn, w_query, w_key, w_value, w_out, rel_table, gain_ffn, w_in, w_down,
    cotangent, bucket, lengths,
):
    rows, depth = inputs.shape
    buckets, heads = rel_table.shape
    width = heads * HEAD
    slots = lengths.shape[1]
    ring = Ring(n_dp, n_mp, depth)
    side = ring.sides[0]
    shifts = list(range(1, n_mp))
    meta = jnp.concatenate([bucket, (ring.z * BIG)[None].astype(jnp.int32), lengths[0]])
    hot = jnp.asarray(offset_one_hot(buckets), BF)
    gain_one, gain_two = gain_attn[None], gain_ffn[None]

    a_own = [w_out, w_query.T, w_key.T, w_value.T]
    tab_own = jnp.pad(rel_table.T, ((0, EXTRA - heads), (0, TILE - buckets)))
    a_piece, f_piece = prep(ring.mine, a_own, tab_own, w_in, w_down, ring.rows)
    tab_own = tab_own[None]
    v = {}

    def close(*keys):
        v.update(zip(keys, bar(*[v[key] for key in keys])))

    def swap(new, old, mask):
        v[new] = ring.swap(v[old], mask)

    shift_order = [s for s in shifts if s != n_mp // 2] + [n_mp // 2]
    f1, f3, f2 = shift_order
    v["piece"] = f_piece
    for s in shifts:
        v["z", s] = ring.pull(a_piece, s)
    x_value = inputs.astype(F32)
    n1 = (rms(x_value)[0] * gain_attn.astype(F32)).astype(BF)
    *kept_own, v["hidden"] = attn_fwd(meta, None, n1, a_own, 0, 1, tab_own, hot, inputs, None, slots, heads)
    close(*[("z", s) for s in shifts], "hidden")
    v["a"], tab_rest = join([v["z", s] for s in shifts])
    close("a", "piece")
    swap("ax", "a", 2)
    swap("ay", "a", 4)
    v["f", f1] = ring.pull(v["piece"], f1)
    v["f", f3] = ring.pull(v["piece"], f3)
    close("ax", "ay", "a", ("f", f1), "piece")
    swap("ayx", "ax", 4)
    v["a3"] = cat([v["a"], v["ax"], v["ay"]])
    swap("a3c", "a3", 1)
    swap(("fx", f1), ("f", f1), 2)
    v["f", f2] = ring.pull(v["piece"], f2)
    close("ayx", "a3c", ("fx", f1), ("f", f3))
    v["a1"] = v["ayx"][None]
    swap("a1c", "a1", 1)
    v["cat", f1] = cat([v["f", f1], v["fx", f1]])
    swap(("far", f1), ("cat", f1), 4)
    swap(("fy", f3), ("f", f3), 4)
    close("a1c", "hidden")
    a_parts = [v["a3"], v["a1"], v["a3c"], v["a1c"]]
    a_index = ring.index[False]
    cut = n_mp - 2
    *kept_one, v["hidden"] = attn_fwd(
        meta, a_index, n1, a_parts, 0, cut, tab_rest, hot, v["hidden"], None, slots, heads
    )
    close("hidden", ("f", f2))
    swap(("fx", f2), ("f", f2), 2)
    *kept_two, v["hidden"], v["n2"] = attn_fwd(
        meta, a_index, n1, a_parts, cut, 1, tab_rest, hot, v["hidden"], gain_two, slots, heads
    )
    close("hidden", "n2", ("far", f1), ("fy", f3), ("fx", f2))

    def cores(s):
        swap(("catc", s), ("cat", s), 1)
        swap(("farc", s), ("far", s), 1)

    def parts_of(s):
        return ring.index[s == f3], [v["cat", s], v["far", s], v["catc", s], v["farc", s]]

    cores(f1)
    v["cat", f3] = cat([v["f", f3], v["fy", f3]])
    swap(("far", f3), ("cat", f3), 2)
    v["cat", f2] = cat([v["f", f2], v["fx", f2]])
    swap(("far", f2), ("cat", f2), 4)
    close("n2", ("catc", f1), ("farc", f1))
    v["out"], v["gn"], v["send"], v["keep"] = ffn(
        side, v["n2"], cotangent, [(None, [w_in, w_down]), parts_of(f1)], None, None
    )
    close("out", "gn", "n2", "send", "keep", ("far", f3), ("far", f2))
    red = {}

    def reduce(name, extra=0):
        red[name] = Reduce(ring, v["send"], v["keep"], extra)

    def close_with(names, *keys):
        groups = [group for name in names for group in red[name].groups]
        values = bar(*[group[1] for group in groups], *[v[key] for key in keys])
        for group, value in zip(groups, values):
            group[1] = value
        v.update(zip(keys, values[len(groups) :]))

    def folded(names, *keys):
        outs = [out for name in names for out in red[name].step()]
        v.update(zip(keys, bar(*[v[key] for key in keys], *outs)))

    cores(f3)
    cores(f2)
    reduce("a")
    close_with(["a"], "n2", "out", "gn", ("catc", f3), ("farc", f3), ("catc", f2), ("farc", f2))
    folded(["a"], "n2", "out", "gn")
    outputs, v["send"], v["keep"], grad_hidden, v["gh"], gg = ffn(
        side, v["n2"], cotangent, [parts_of(f3), parts_of(f2)], (v["out"], v["gn"]), (v["hidden"], gain_two)
    )
    close_with(["a"], "send", "keep", "gh")
    folded(["a"], "gh")
    reduce("b")

    places = [(tuple(range(cut)), kept_one), ((cut,), kept_two)]
    rest = (a_parts, tab_rest, places)
    own = (a_own, [*kept_own, tab_own])
    v["send"], v["keep"], v["gn"], tabs = attn_bwd(
        meta, a_index, side, n1, v["gh"], hot, list(range(cut)), rest, None, None, None, slots, heads
    )
    close_with(["a", "b"], "send", "keep", "gh", "gn")
    reduce("c")
    folded(["b", "a"], "gh", "gn")
    v["f1"] = ring.push(red["a"].out[2:], f1)
    close_with(["c"], "gh", "gn")
    folded(["c"], "gh", "gn")
    final = (inputs, gain_one, grad_hidden, gg, tabs)
    v["send"], v["keep"], v["gin"] = attn_bwd(
        meta, a_index, side, n1, v["gh"], hot, [cut, None], rest, own, v["gn"], final, slots, heads
    )
    close_with(["b", "c"], "send", "keep", "gin", "f1")
    grad_inputs = v["gin"]
    reduce("d", EXTRA)
    folded(["b", "c"], "gin")
    close_with(["d"], "gin")
    folded(["d"], "gin")
    close_with(["b", "c"], "gin")
    folded(["b", "c"], "gin")
    v["f3"] = ring.push(red["b"].out[:2], f3)
    v["f2"] = ring.push(red["b"].out[2:], f2)
    v["a1"], v["a2"] = ring.push(red["c"].out[:1], 1), ring.push(red["c"].out[1:], 2)
    close_with(["d"], "gin")
    folded(["d"], "gin")
    close("f3", "f2", "gin")

    def spread(name, piece):
        v[name, 0] = piece
        for mask in (2, 4, 6):
            v[name, mask] = ring.swap(piece, mask)

    def gathered(name):
        v[name] = cat([v[name, mask] for mask in (0, 2, 4, 6)])
        v[name, 1] = ring.swap(v[name], 1)

    spread("f", total_of([red["a"].out[:2], v["f1"], v["f3"], v["f2"]]))
    close_with(["d"], "gin")
    folded(["d"], "gin")
    v["a3"] = ring.push(red["d"].out[:1], 3)
    small = red["d"].small
    smalls = [ring.push(small, s) for s in shifts]
    close("a1", "a2", "a3", ("f", 2), ("f", 4), ("f", 6))
    spread("a", total_of([red["d"].out[1:], v["a1"], v["a2"], v["a3"]]))
    gathered("f")
    close(("f", 1), ("a", 2), ("a", 4), ("a", 6))
    gathered("a")
    v["f_done"] = finish(a_index, [v["f"], v["f", 1]], 2, depth)
    grad_in, grad_down = v["f_done"]
    grads = finish(a_index, [v["a"], v["a", 1]], 4, width)
    grad_out, grad_query, grad_key, grad_value = grads[0], grads[1].T, grads[2].T, grads[3].T

    table, gains = small_of([small] + smalls)
    grad_table = table[0, : heads * TILE].reshape(heads, TILE)[:, :buckets].T
    return (
        outputs, grad_inputs, grad_query, grad_key, grad_value, grad_out, grad_table,
        gains[n_mp], gains[n_mp + 1], grad_in, grad_down,
    )


def solution(mesh):
    placed = (
        P(("dp", "mp"), None), P(), P(None, "mp"), P(None, "mp"), P(None, "mp"), P("mp", None),
        P(None, "mp"), P(), P(None, "mp"), P("mp", None), P(("dp", "mp"), None), P("dp"), P("dp", None),
    )
    return jax.shard_map(
        functools.partial(body, mesh.shape["dp"], mesh.shape["mp"]),
        mesh=mesh,
        in_specs=placed,
        out_specs=(
            P(("dp", "mp"), None), P(("dp", "mp"), None), P(None, "mp"), P(None, "mp"), P(None, "mp"),
            P("mp", None), P(None, "mp"), P(), P(), P(None, "mp"), P("mp", None),
        ),
        check_vma=False,
    )
```

```python
import functools

import jax
import jax.numpy as jnp
import numpy as np
from jax import lax
from jax.experimental import pallas as pl
from jax.experimental.pallas import tpu as pltpu
from jax.sharding import PartitionSpec as P

BIG = 512
HEAD = 64
EPS = 1e-06
THRESHOLDS = (12, 16, 23, 32, 46, 64, 91)
MASKED = -1e30
TILE = 128
SPAN = 512
EXTRA = 16
BF = jnp.bfloat16
F32 = jnp.float32
MIB = 1024 * 1024
LIMIT = 60
SMEM = pl.BlockSpec(memory_space=pltpu.SMEM)
VMEM = pl.BlockSpec(memory_space=pltpu.VMEM)
ANY = pl.BlockSpec(memory_space=pl.ANY)


def offset_one_hot(buckets):
    offsets = np.arange(SPAN) - SPAN // 2
    distance = np.abs(offsets)
    far = 8 + sum((distance >= t).astype(np.int32) for t in THRESHOLDS)
    bucket = np.where(distance < 8, distance, far) + np.where(offsets > 0, buckets // 2, 0)
    return (np.arange(TILE)[:, None] == bucket[None, :]).astype(np.float32)


def dot_nn(a, b):
    return lax.dot_general(a, b, (((1,), (0,)), ((), ())), preferred_element_type=F32)


def dot_nt(a, b):
    return lax.dot_general(a, b, (((1,), (1,)), ((), ())), preferred_element_type=F32)


def dot_tn(a, b):
    return lax.dot_general(a, b, (((0,), (0,)), ((), ())), preferred_element_type=F32)


def like(shape, dtype):
    return jax.ShapeDtypeStruct(shape, dtype)


def params(mib):
    return pltpu.CompilerParams(vmem_limit_bytes=mib * MIB)


def cost(micros):
    return pl.CostEstimate(flops=micros * 10**9, bytes_accessed=micros * 10**6, transcendentals=0)


def mask_rows(ids_ref, slots):
    bucket = ids_ref[1]
    half = BIG // 2
    segs, starts = [], []
    for part in range(2):
        first = ids_ref[2] + part * half
        seg = jnp.int32(0)
        for j in range(1, slots):
            seg = seg + jnp.where(first >= j * bucket, 1, 0).astype(jnp.int32)
        segs.append(seg)
        starts.append(first - seg * bucket)
    iota = lax.broadcasted_iota(jnp.int32, (1, half), 1)
    rows = []
    for query_part in range(2):
        cols = []
        for key_part in range(2):
            same = segs[query_part] == segs[key_part]
            limit = jnp.where(same, ids_ref[3 + segs[key_part]] - starts[key_part], 0)
            cols.append(jnp.where(iota < limit, 0.0, MASKED).astype(F32))
        rows.append(jnp.concatenate(cols, axis=1))
    return rows


def bias_band(rel_row):
    return pltpu.roll(jnp.broadcast_to(rel_row, (TILE, SPAN)), 0, 1, stride=1, stride_axis=0)


def masked_bias(i, near, rel_row, mask):
    tiles = []
    for j in range(BIG // TILE):
        keys = mask[:, j * TILE : (j + 1) * TILE]
        if abs(j - i) <= 1:
            tiles.append(near[:, (j - i + 2) * TILE : (j - i + 3) * TILE] + keys)
        else:
            far = rel_row[:, SPAN - 1 :] if j > i else rel_row[:, :1]
            tiles.append(jnp.broadcast_to(far + keys, (TILE, TILE)))
    return jnp.concatenate(tiles, axis=1)


def row_block(low, bits):
    return ((low & 1) << (bits - 1)) | (low >> 1)


def side_of(ids_ref, bit):
    return (ids_ref[0] >> bit) & 1


def block_rows(ids_ref, mask, bits, rows):
    return pl.ds(pl.multiple_of(row_block(ids_ref[0] ^ mask, bits) * rows, rows), rows)


class Mover:
    def __init__(self, sems):
        self.sems, self.used, self.out = sems, 0, []

    def copy(self, source, target):
        one = pltpu.make_async_copy(source, target, self.sems.at[self.used])
        self.used += 1
        one.start()
        return one

    def load(self, source, target):
        return [self.copy(source, target)]

    def blocks(self, ids_ref, masks, part_refs, mat, which):
        copies, j, first = [], 0, 0
        for part in part_refs:
            if masks is None:
                copies.append(self.copy(part, mat.at[pl.ds(first, part.shape[0])]))
                first += part.shape[0]
                continue
            bits = (len(masks) - 1).bit_length()
            for e in range(part.shape[0]):
                copies.append(self.copy(part.at[e, which], mat.at[block_rows(ids_ref, masks[j], bits, part.shape[2])]))
                j += 1
        return copies

    def store(self, source, target):
        self.out.append(self.copy(source, target))

    def halves(self, ids_ref, source, send, keep):
        size = source.shape[0] // 2
        for ref, side in ((send, 1 - side_of(ids_ref, 0)), (keep, side_of(ids_ref, 0))):
            self.store(source.at[pl.ds(pl.multiple_of(side * size, size), size)], ref)

    def finish(self):
        wait(self.out)


def wait(copies):
    for one in copies:
        one.wait()


def put_blocks(ids_ref, masks, part_refs, mat, which):
    j, bits = 0, (len(masks) - 1).bit_length()
    for part in part_refs:
        for e in range(part.shape[0]):
            mat[block_rows(ids_ref, masks[j], bits, part.shape[2]), :] = part[e, which].astype(mat.dtype)
            j += 1


def rms(values):
    root = lax.rsqrt(jnp.mean(values * values, axis=1, keepdims=True) + EPS)
    return values * root, root


def rms_back(grad, unit, root, gain):
    scaled = grad * gain
    centred = scaled - unit * jnp.mean(scaled * unit, axis=1, keepdims=True)
    return root * centred, jnp.sum(grad * unit, axis=0, keepdims=True)


def head_slices(qkv_ref, heads, h):
    width = heads * HEAD
    return [qkv_ref[:, j * width + h * HEAD : j * width + (h + 1) * HEAD] for j in (1, 2, 3)]


def forward_scores(h, band, rel, masks, scores, lse_ref):
    probs = []
    for i in range(BIG // TILE):
        rows = slice(i * TILE, (i + 1) * TILE)
        s = scores[h, rows, :] + masked_bias(i, band[h], rel[h : h + 1], masks[i // 2])
        top = jnp.max(s, axis=1, keepdims=True)
        e = jnp.exp(s - top)
        total = jnp.sum(e, axis=1, keepdims=True)
        probs.append((e * (1.0 / total)).astype(BF))
        lse_ref[rows, h : h + 1] = top + jnp.log(total)
    return jnp.concatenate(probs, axis=0)


def attn_fwd_kernel(slots, heads, parts, masks, start, shards, last, ids_ref, *refs):
    refs = list(refs)
    take = lambda n: [refs.pop(0) for _ in range(n)]
    n1_hbm = take(1)[0]
    a_parts = take(parts)
    tab_hbm, hot_hbm, prior_hbm = take(3)
    gain_hbm = take(1)[0] if last else None
    qkv_out, o_out, lse_out, hid_out = take(4)
    n2_out = take(1)[0] if last else None
    n1_ref, mat, tab_ref, hot_ref, prior_ref, gain_ref, qkv_ref, o_ref, lse_ref, hid_ref, n2_ref, band, scores, sems = refs
    move = Mover(sems)
    width = heads * HEAD
    half = BIG // 2
    got_mat = [move.blocks(ids_ref, masks, a_parts, mat.at[0], start)]
    got_n1 = move.load(n1_hbm, n1_ref)
    got_tab = move.load(tab_hbm.at[pl.ds(start, shards)], tab_ref) + move.load(hot_hbm, hot_ref)
    allowed = mask_rows(ids_ref, slots)
    wait(got_tab)
    wait(got_n1)
    for s in range(shards):
        rel = dot_nn(tab_ref[s], hot_ref[...])
        for h in range(heads):
            band[h] = bias_band(rel[h : h + 1])
        wait(got_mat[s])
        if s == 0:
            got_mat += [move.blocks(ids_ref, masks, a_parts, mat.at[t], start + t) for t in range(1, shards)]
            got_prior = move.load(prior_hbm, prior_ref)
            if last:
                got_prior += move.load(gain_hbm, gain_ref)
        qkv_ref[s] = dot_nt(n1_ref[...], mat[s]).astype(BF)
        move.store(qkv_ref.at[s], qkv_out.at[s])
        for h in range(heads):
            q, k, _ = head_slices(qkv_ref.at[s], heads, h)
            scores[h] = dot_nt(q, k)
        for h in range(heads):
            v = head_slices(qkv_ref.at[s], heads, h)[2]
            pb = forward_scores(h, band, rel, allowed, scores, lse_ref.at[s])
            o_ref[s, :, h * HEAD : (h + 1) * HEAD] = dot_nn(pb, v).astype(BF)
        move.store(o_ref.at[s], o_out.at[s])
        move.store(lse_ref.at[s], lse_out.at[s])
        if s == 0:
            wait(got_prior)
        for part in range(2):
            rows = pl.ds(part * half, half)
            before = prior_ref[rows, :].astype(F32) if s == 0 else hid_ref[rows, :]
            hidden = before + dot_nn(o_ref[s, rows, :], mat[s, :width, :])
            hid_ref[rows, :] = hidden
            if s == shards - 1:
                move.store(hid_ref.at[rows], hid_out.at[rows])
                if last:
                    n2_ref[rows, :] = (rms(hidden)[0] * gain_ref[...].astype(F32)).astype(BF)
                    move.store(n2_ref.at[rows], n2_out.at[rows])
    move.finish()


HBM = pl.BlockSpec(memory_space=pltpu.HBM)


def attn_fwd(ids, masks, n1, a_parts, start, shards, tab, hot, prior, gain, slots, heads):
    last = gain is not None
    rows, depth = n1.shape
    width = heads * HEAD
    cols = 4 * width
    args = [n1, *a_parts, tab, hot, prior] + ([gain] if last else [])
    out_shape = [
        like((shards, rows, cols), BF),
        like((shards, rows, width), BF),
        like((shards, rows, TILE), F32),
        like((rows, depth), F32),
    ]
    if last:
        out_shape.append(like((rows, depth), BF))
    return pl.pallas_call(
        functools.partial(attn_fwd_kernel, slots, heads, len(a_parts), masks, start, shards, last),
        in_specs=[SMEM] + [ANY] * len(args),
        out_specs=[HBM] * len(out_shape),
        out_shape=out_shape,
        scratch_shapes=[
            pltpu.VMEM((rows, depth), BF),
            pltpu.VMEM((shards, cols, depth), BF),
            pltpu.VMEM((shards,) + tab.shape[1:], BF),
            pltpu.VMEM(hot.shape, BF),
            pltpu.VMEM(prior.shape, prior.dtype),
            pltpu.VMEM((1, depth), BF),
            pltpu.VMEM((shards, rows, cols), BF),
            pltpu.VMEM((shards, rows, width), BF),
            pltpu.VMEM((shards, rows, TILE), F32),
            pltpu.VMEM((rows, depth), F32),
            pltpu.VMEM((rows, depth), BF),
            pltpu.VMEM((heads, TILE, SPAN), F32),
            pltpu.VMEM((heads, BIG, BIG), F32),
            pltpu.SemaphoreType.DMA((12 + 12 * shards,)),
        ],
        compiler_params=params(LIMIT),
        cost_estimate=cost(16 * shards),
        name="attn_fwd",
    )(ids, *args)


def attn_bwd_kernel(slots, heads, masks, shards, rest, sources, own, first, befores, ids_ref, *refs):
    refs = list(refs)
    take = lambda n: [refs.pop(0) for _ in range(n)]
    last = None in shards
    count = len(shards)
    n1_hbm, gh_hbm, hot_hbm = take(3)
    rest_parts = take(rest)
    rest_tab = take(1)[0]
    rest_kept, rest_at = {}, {}
    for places in sources:
        kept = take(3) + [rest_tab]
        for base, which in enumerate(places):
            rest_kept[which], rest_at[which] = kept, base
    own_parts, own_kept = (take(own), take(4)) if last else ([], [])
    prior_hbm = None if first else take(1)[0]
    if last:
        x_hbm, gain_hbm, ghid_hbm, gain2_hbm = take(4)
        tabs_hbm = take(befores)
        send_out, keep_out, gin_out = take(3)
    else:
        send_out, keep_out, gn_out, tabs_out = take(4)
    n1_ref, gh_ref, hot_ref, mat, qkv_ref, o_ref, lse_ref, tab_ref, gn_ref = take(9)
    band, acc, gs_all, pb_all, gq_all, grads_mat, tabs_ref, sems = take(8)
    move = Mover(sems)
    width = heads * HEAD
    half = BIG // 2
    if last:
        x_ref, gain_ref, ghid_ref, gain2_ref, before_ref, small, packed = take(7)

    def load(c):
        which = shards[c]
        parts, kept = (own_parts, own_kept) if which is None else (rest_parts, rest_kept[which])
        at = 0 if which is None else which
        base = 0 if which is None else rest_at[which]
        got_tab = move.load(kept[3].at[at], tab_ref.at[c])
        got_mat = move.blocks(ids_ref, None if which is None else masks, parts, mat.at[c], at)
        got_kept = move.load(kept[0].at[base], qkv_ref.at[c]) + move.load(kept[2].at[base], lse_ref.at[c])
        return got_tab, got_mat, got_kept, move.load(kept[1].at[base], o_ref.at[c])

    got_first = move.load(hot_hbm, hot_ref) + move.load(gh_hbm, gh_ref)
    got = [load(0)]
    got_n1 = move.load(n1_hbm, n1_ref)
    allowed = mask_rows(ids_ref, slots)
    lane = lax.broadcasted_iota(jnp.int32, (1, SPAN), 1)
    wait(got_first)
    gh = gh_ref[...]
    for c in range(count):
        got_tab, got_mat, got_kept, got_late = got[c]
        acc[...] = jnp.zeros(acc.shape, F32)
        gq_all[c, :, :width] = jnp.zeros((gq_all.shape[1], width), BF)
        wait(got_tab)
        rel = dot_nn(tab_ref[c], hot_ref[...])
        for h in range(heads):
            band[h] = bias_band(rel[h : h + 1])
        wait(got_mat)
        go_all = dot_nt(gh, mat[c, :width, :]).astype(BF)
        wait(got_kept)
        if c == 0:
            got += [load(t) for t in range(1, count)]
            got_prior = [] if first else move.load(prior_hbm, gn_ref)
            if last:
                got_prior += move.load(x_hbm, x_ref) + move.load(gain_hbm, gain_ref)
                got_prior += move.load(ghid_hbm, ghid_ref) + move.load(gain2_hbm, gain2_ref)
                done = 0
                for ref in tabs_hbm:
                    got_prior += move.load(ref, before_ref.at[pl.ds(done, ref.shape[0])])
                    done += ref.shape[0]
        far = []
        for h in range(heads):
            q, k, v = head_slices(qkv_ref.at[c], heads, h)
            go = go_all[:, h * HEAD : (h + 1) * HEAD]
            low = jnp.zeros((1, TILE), F32)
            high = jnp.zeros((1, TILE), F32)
            for i in range(BIG // TILE):
                rows = slice(i * TILE, (i + 1) * TILE)
                s = dot_nt(q[rows], k) + masked_bias(i, band[h], rel[h : h + 1], allowed[i // 2])
                p = jnp.exp(s - lse_ref[c, rows, h : h + 1])
                dp = dot_nt(go[rows], v)
                inner = jnp.sum(p * dp, axis=1, keepdims=True)
                gs = (p * (dp - inner)).astype(BF)
                gs_all[h, rows, :] = gs
                pb_all[h, rows, :] = p.astype(BF)
                wide = gs.astype(F32)
                for j in range(BIG // TILE):
                    tile = wide[:, j * TILE : (j + 1) * TILE]
                    if abs(j - i) <= 1:
                        acc[h, :, (j - i + 2) * TILE : (j - i + 3) * TILE] += tile
                    elif j > i:
                        high = high + jnp.sum(tile, axis=0, keepdims=True)
                    else:
                        low = low + jnp.sum(tile, axis=0, keepdims=True)
            at = lambda j: slice(j * width + h * HEAD, j * width + (h + 1) * HEAD)
            gq_all[c, :, at(1)] = dot_nn(gs_all[h], k).astype(BF)
            gq_all[c, :, at(2)] = dot_tn(gs_all[h], q).astype(BF)
            gq_all[c, :, at(3)] = dot_tn(pb_all[h], go).astype(BF)
            far.append((low, high))
        wait(got_late)
        if c == 0:
            wait(got_n1)
        grads_mat[c] = dot_tn(gq_all[c], n1_ref[...]).astype(BF)
        grads_mat[c, :width, :] = dot_tn(o_ref[c], gh).astype(BF)
        size = pl.ds(0, grads_mat.shape[1] // 2)
        move.halves(ids_ref, grads_mat.at[c], send_out.at[c, size], keep_out.at[c, size])
        near = acc[...]
        n = TILE // 2
        while n >= 8:
            near = near[:, :n] + pltpu.roll(near[:, n:], SPAN - n, 2)
            n //= 2
        line = near[:, 0:1]
        for j in range(1, 8):
            line = line + pltpu.roll(near[:, j : j + 1], SPAN - j, 2)
        lines = []
        for h, (low, high) in enumerate(far):
            ends = jnp.where(lane == 0, jnp.sum(low, axis=1, keepdims=True), 0.0)
            ends = ends + jnp.where(lane == SPAN - 1, jnp.sum(high, axis=1, keepdims=True), 0.0)
            lines.append(line[h] + ends)
        lines = jnp.concatenate(lines + [jnp.zeros((8 - heads, SPAN), F32)], axis=0)
        tabs_ref[c] = lax.dot_general(
            lines, hot_ref[...].astype(F32), (((1,), (1,)), ((), ())),
            precision=lax.Precision.HIGHEST, preferred_element_type=F32,
        )
        if c == 0:
            wait(got_prior)
        for part in range(2):
            rows = pl.ds(part * half, half)
            gn = dot_nn(gq_all[c, rows, :], mat[c])
            if not (first and c == 0):
                gn = gn + gn_ref[rows, :]
            gn_ref[rows, :] = gn
            if c == count - 1 and not last:
                move.store(gn_ref.at[rows], gn_out.at[rows])
    if not last:
        move.store(tabs_ref, tabs_out)
        move.finish()
        return
    unit, root = rms(x_ref[...].astype(F32))
    back, gain_grad = rms_back(gn_ref[...], unit, root, gain_ref[...].astype(F32))
    small[...] = jnp.zeros_like(small)
    total = before_ref.shape[0] + count
    tables = [tabs_ref[count - 1]] + [before_ref[j] for j in range(total - count)]
    tables += [tabs_ref[c] for c in range(count - 1)]
    for row, value in enumerate(tables):
        for h in range(heads):
            small[row : row + 1, h * TILE : (h + 1) * TILE] = value[h : h + 1]
    small[total : total + 1, :] = gain_grad
    small[total + 1 : total + 2, :] = gain2_ref[0:1, :]
    packed[...] = split_small(small[...])
    tail = pl.ds(grads_mat.shape[1] // 2, EXTRA)
    for c in range(count):
        move.store(packed, send_out.at[c, tail])
        move.store(packed, keep_out.at[c, tail])
    gh_ref[...] = (ghid_ref[...] + back).astype(BF)
    move.store(gh_ref, gin_out)
    move.finish()


def split_small(value):
    high = value.astype(BF)
    low = (value - high.astype(F32)).astype(BF)
    return jnp.concatenate([high.astype(F32), low.astype(F32)], axis=0).astype(BF)


def join_small(packed):
    wide = packed.astype(F32)
    return wide[: EXTRA // 2] + wide[EXTRA // 2 :]


def attn_bwd(ids, masks, n1, gh, hot, shards, rest, own, prior, final, slots, heads):
    last, first = None in shards, prior is None
    count = len(shards)
    rows, depth = n1.shape
    width = heads * HEAD
    cols = 4 * width
    parts, tab, sources = rest
    sources = [(places, kept) for places, kept in sources if set(places) & set(shards)]
    args = [n1, gh, hot, *parts, tab] + [k for _, kept in sources for k in kept]
    args += [*own[0], *own[1]] if last else []
    args += ([] if first else [prior]) + (list(final) if last else [])
    befores = len(final) - 4 if last else 0
    half = like((count, cols // 2 + (EXTRA if last else 0), depth), BF)
    if last:
        out_shape = [half, half, like((rows, depth), BF)]
    else:
        out_shape = [half, half, like((rows, depth), F32), like((count, 8, TILE), F32)]
    scratch = [
        pltpu.VMEM((rows, depth), BF),
        pltpu.VMEM((rows, depth), BF),
        pltpu.VMEM(hot.shape, BF),
        pltpu.VMEM((count, cols, depth), BF),
        pltpu.VMEM((count, rows, cols), BF),
        pltpu.VMEM((count, rows, width), BF),
        pltpu.VMEM((count, rows, TILE), F32),
        pltpu.VMEM((count,) + tab.shape[1:], BF),
        pltpu.VMEM((rows, depth), F32),
        pltpu.VMEM((heads, TILE, SPAN), F32),
        pltpu.VMEM((heads, TILE, SPAN), F32),
        pltpu.VMEM((heads, BIG, BIG), BF),
        pltpu.VMEM((heads, BIG, BIG), BF),
        pltpu.VMEM((count, rows, cols), BF),
        pltpu.VMEM((count, cols, depth), BF),
        pltpu.VMEM((count, 8, TILE), F32),
        pltpu.SemaphoreType.DMA((16 + 18 * count,)),
    ]
    if last:
        scratch += [
            pltpu.VMEM((rows, depth), BF),
            pltpu.VMEM((1, depth), BF),
            pltpu.VMEM((rows, depth), F32),
            pltpu.VMEM((8, depth), F32),
            pltpu.VMEM((sum(f.shape[0] for f in final[4:]), 8, TILE), F32),
            pltpu.VMEM((8, depth), F32),
            pltpu.VMEM((EXTRA, depth), BF),
        ]
    return pl.pallas_call(
        functools.partial(
            attn_bwd_kernel, slots, heads, masks, tuple(shards), len(parts), tuple(p for p, _ in sources),
            len(own[0]) if last else 0, first, befores,
        ),
        in_specs=[SMEM] + [ANY] * len(args),
        out_specs=[HBM] * len(out_shape),
        out_shape=out_shape,
        scratch_shapes=scratch,
        compiler_params=params(LIMIT),
        cost_estimate=cost(32 * count),
        name="attn_bwd",
    )(ids, *args)


def ffn_kernel(parts, masks, first, last, ids_ref, *refs):
    refs = list(refs)
    take = lambda n: [refs.pop(0) for _ in range(n)]
    count = len(parts)
    n2_hbm, cot_hbm = take(2)
    f_parts = [take(n or 2) for n in parts]
    out_in, gn_in = (None, None) if first else take(2)
    if last:
        hid_in, gain_in = take(2)
        out_out, send_out, keep_out, ghid_out, gh_out, gg_out = take(6)
    else:
        out_out, gn_out, send_out, keep_out = take(4)
    n2_ref, cot_ref, i_mat, w_mat, act_ref, gp_ref, gi_mat, gw_mat, out_ref, gn_ref, sems = take(11)
    move = Mover(sems)
    hid_ref, gain_ref, y_ref, gg_ref = take(4) if last else [None] * 4

    def load(c):
        if not parts[c]:
            return move.load(f_parts[c][0], i_mat.at[c]), move.load(f_parts[c][1], w_mat.at[c])
        return tuple(move.blocks(ids_ref, masks[c], f_parts[c], mat.at[c], j) for j, mat in enumerate((i_mat, w_mat)))

    got_n2 = move.load(n2_hbm, n2_ref)
    got = [load(0)]
    got_cot = move.load(cot_hbm, cot_ref)
    c0 = 0.7978845608028654
    c1 = 0.044715
    size = n2_ref.shape[0] // 2
    gain_grad = None
    for c in range(count):
        wait(got[c][0])
        if c == 0:
            wait(got_n2)
            got += [load(t) for t in range(1, count)]
            got_sums = [] if first else move.load(out_in, out_ref) + move.load(gn_in, gn_ref)
            if last:
                got_sums += move.load(hid_in, hid_ref) + move.load(gain_in, gain_ref)
        pre = dot_nn(n2_ref[...], i_mat[c])
        square = pre * pre
        th = jnp.tanh(pre * (c0 + (c0 * c1) * square))
        half = 0.5 * (1.0 + th)
        act_ref[c] = (pre * half).astype(BF)
        slope = half + (0.5 * pre) * (1.0 - th * th) * (c0 + (3.0 * c0 * c1) * square)
        wait(got[c][1])
        if c == 0:
            wait(got_cot)
        cot = cot_ref[...]
        gp_ref[c] = (dot_nt(cot, w_mat[c]) * slope).astype(BF)
        gw_mat[c] = dot_tn(act_ref[c], cot).astype(BF)
        move.halves(ids_ref, gw_mat.at[c], send_out.at[2 * c + 1], keep_out.at[2 * c + 1])
        gi_mat[c] = dot_tn(n2_ref[...], gp_ref[c]).astype(BF)
        move.halves(ids_ref, gi_mat.at[c], send_out.at[2 * c], keep_out.at[2 * c])
        if c == 0:
            wait(got_sums)
        ending = c == count - 1
        for part in range(2):
            rows = pl.ds(part * size, size)
            gn = dot_nt(gp_ref[c, rows, :], i_mat[c])
            out = dot_nn(act_ref[c, rows, :], w_mat[c])
            if not (first and c == 0):
                out = out + out_ref[rows, :]
                gn = gn + gn_ref[rows, :]
            if not (last and ending):
                gn_ref[rows, :] = gn
                out_ref[rows, :] = out
                if ending:
                    move.store(gn_ref.at[rows], gn_out.at[rows])
                    move.store(out_ref.at[rows], out_out.at[rows])
                continue
            hidden = hid_ref[rows, :]
            y_ref[rows, :] = (hidden + out).astype(BF)
            move.store(y_ref.at[rows], out_out.at[rows])
            unit, root = rms(hidden)
            back, gain_part = rms_back(gn, unit, root, gain_ref[...].astype(F32))
            gain_grad = gain_part if gain_grad is None else gain_grad + gain_part
            grad_hidden = cot_ref[rows, :].astype(F32) + back
            gn_ref[rows, :] = grad_hidden
            move.store(gn_ref.at[rows], ghid_out.at[rows])
            n2_ref[rows, :] = grad_hidden.astype(BF)
            move.store(n2_ref.at[rows], gh_out.at[rows])
    if last:
        gg_ref[...] = jnp.broadcast_to(gain_grad, gg_ref.shape)
        move.store(gg_ref, gg_out)
    move.finish()


def ffn(ids, n2, cot, shards, sums, final):
    first, last = sums is None, final is not None
    rows, depth = n2.shape
    count = len(shards)
    units = shards[-1][1][0].shape[-1]
    half = like((2 * count, depth // 2, units), BF)
    total = like((rows, depth), F32)
    args = [n2, cot] + [p for _, ps in shards for p in ps]
    args += ([] if first else list(sums)) + ([] if not last else list(final))
    if last:
        out_shape = [like((rows, depth), BF), half, half, total, like((rows, depth), BF), like((8, depth), F32)]
    else:
        out_shape = [total, total, half, half]
    scratch = [
        pltpu.VMEM((rows, depth), BF),
        pltpu.VMEM((rows, depth), BF),
        pltpu.VMEM((count, depth, units), BF),
        pltpu.VMEM((count, units, depth), BF),
        pltpu.VMEM((count, rows, units), BF),
        pltpu.VMEM((count, rows, units), BF),
        pltpu.VMEM((count, depth, units), BF),
        pltpu.VMEM((count, units, depth), BF),
        pltpu.VMEM((rows, depth), F32),
        pltpu.VMEM((rows, depth), F32),
        pltpu.SemaphoreType.DMA((20 + 20 * count,)),
    ]
    if last:
        scratch += [
            pltpu.VMEM((rows, depth), F32),
            pltpu.VMEM((1, depth), BF),
            pltpu.VMEM((rows, depth), BF),
            pltpu.VMEM((8, depth), F32),
        ]
    return pl.pallas_call(
        functools.partial(
            ffn_kernel, tuple(0 if m is None else len(p) for m, p in shards), [m for m, _ in shards], first, last
        ),
        in_specs=[SMEM] + [ANY] * len(args),
        out_specs=[HBM] * len(out_shape),
        out_shape=out_shape,
        scratch_shapes=scratch,
        compiler_params=params(LIMIT),
        cost_estimate=cost(32 * count),
        name="ffn",
    )(ids, *args)


def prep_kernel(rows, bits, count, ids_ref, *refs):
    mats, (tab_ref, in_ref, down_ref, a_ref, f_ref, wide_ref, sems) = refs[:count], refs[count:]
    block = row_block(ids_ref[0], bits)
    first = pl.ds(pl.multiple_of(block * rows, rows), rows)
    copies = [
        pltpu.make_async_copy(in_ref.at[first], f_ref.at[0], sems.at[0]),
        pltpu.make_async_copy(down_ref.at[first], f_ref.at[1], sems.at[1]),
    ]
    per = mats[0].shape[0] // rows

    def piece(j, mat):
        at = pl.ds(pl.multiple_of((block - j * per) * rows, rows), rows)
        return pltpu.make_async_copy(mat.at[at], a_ref.at[pl.ds(0, rows)], sems.at[2])

    for j, mat in enumerate(mats):
        @pl.when(block // per == j)
        def _():
            piece(j, mat).start()

    for copy in copies:
        copy.start()
    tab = tab_ref[...].astype(F32)
    heads, buckets = tab.shape
    tab = jnp.concatenate([tab, jnp.zeros((heads, TILE - buckets), F32)], axis=1)
    tab = jnp.concatenate([tab, jnp.zeros((EXTRA - heads, TILE), F32)], axis=0).astype(BF)
    wide_ref[0] = tab
    a_ref[rows:, :] = jnp.zeros((EXTRA, a_ref.shape[1]), BF)
    a_ref[rows:, :TILE] = tab
    for j, mat in enumerate(mats):
        @pl.when(block // per == j)
        def _():
            piece(j, mat).wait()

    for copy in copies:
        copy.wait()


def prep(ids, mats, tab, w_in, w_down, rows, bits):
    depth = w_in.shape[0]
    return pl.pallas_call(
        functools.partial(prep_kernel, rows, bits, len(mats)),
        in_specs=[SMEM] + [ANY] * len(mats) + [VMEM, ANY, ANY],
        out_specs=[VMEM, VMEM, VMEM],
        out_shape=[like((rows + EXTRA, depth), BF), like((2, rows, depth), BF), like((1, EXTRA, TILE), BF)],
        scratch_shapes=[pltpu.SemaphoreType.DMA((3,))],
        compiler_params=params(60),
        cost_estimate=cost(0),
        name="prep",
    )(ids, *mats, tab, w_in, w_down)


def join_kernel(count, *refs):
    parts, (a_ref, tab_ref) = refs[:count], refs[count:]
    rows = a_ref.shape[1]
    for j, part in enumerate(parts):
        a_ref[j] = part[:rows, :]
        tab_ref[j] = part[rows:, :TILE]


def join(parts):
    rows, depth = parts[0].shape
    return pl.pallas_call(
        functools.partial(join_kernel, len(parts)),
        in_specs=[VMEM] * len(parts),
        out_specs=[VMEM, VMEM],
        out_shape=[like((len(parts), rows - EXTRA, depth), BF), like((len(parts), EXTRA, TILE), BF)],
        compiler_params=params(16),
        cost_estimate=cost(0),
        name="join",
    )(*parts)


def row_runs(left, bit, rows):
    inner = rows
    for b in left[left.index(bit) + 1 :]:
        inner *= 2
    outer = 1
    for b in left[: left.index(bit)]:
        outer *= 2
    return [(o * 2 * inner, inner, o * inner) for o in range(outer)]


def fold_kernel(runs, extra, joined, ids_ref, *refs):
    if joined:
        keep_ref, recv_ref = refs[:2]
        n = keep_ref.shape[0] // 2
        ins = [(keep_ref.at[pl.ds(g * n, n)], recv_ref.at[pl.ds(g * n, n)]) for g in range(2)]
        outs = refs[2:]
    else:
        ins, outs = [refs[0:2], refs[2:4]], refs[4:]
    packed = None
    if extra:
        keep, recv = ins[1]
        tail = pl.ds(keep.shape[1] - extra, extra)
        packed = split_small(join_small(keep[0, tail, :]) + join_small(recv[0, tail, :]))
    for g, (keep, recv) in enumerate(ins):
        def total(rows):
            return (keep[:, rows, :].astype(F32) + recv[:, rows, :].astype(F32)).astype(BF)

        if runs is None:
            rows, n = outs[0].shape[1], outs[0].shape[0] // 2
            outs[0][g * n : (g + 1) * n] = total(pl.ds(0, rows))
            continue
        bit, group_runs = runs[g]
        mine = side_of(ids_ref, bit)
        for ref, side in ((outs[2 * g], 1 - mine), (outs[2 * g + 1], mine)):
            for source, length, target in group_runs:
                ref[:, target : target + length, :] = total(pl.ds(pl.multiple_of(source + side * length, length), length))
            if extra and g == 1:
                done = sum(length for _, length, _ in group_runs)
                for m in range(ref.shape[0]):
                    ref[m, done:, :] = packed
    if extra and runs is None:
        outs[1][...] = packed


def fold(ids, groups, runs, extra):
    joined = len(groups) == 1
    arrays = [a for group in groups for a in group]
    if joined:
        count = arrays[0].shape[0] // 2
        bodies = [arrays[0].shape[1] - extra] * 2
    else:
        count = arrays[0].shape[0]
        bodies = [arrays[0].shape[1], arrays[2].shape[1] - extra]
    cols = arrays[0].shape[2]
    if runs is None:
        out_shape = [like((2 * count, bodies[0], cols), BF)] + ([like((extra, cols), BF)] if extra else [])
    else:
        tails = (0, extra)
        out_shape = [like((count, bodies[g] // 2 + tails[g], cols), BF) for g in (0, 0, 1, 1)]
    return pl.pallas_call(
        functools.partial(fold_kernel, runs, extra, joined),
        in_specs=[SMEM] + [VMEM] * len(arrays),
        out_specs=[VMEM] * len(out_shape),
        out_shape=out_shape,
        compiler_params=params(24),
        cost_estimate=cost(0),
        name="fold",
    )(ids, *arrays)


def add_kernel(a_ref, b_ref, out_ref):
    out_ref[...] = (a_ref[...].astype(F32) + b_ref[...].astype(F32)).astype(BF)


def add(a, b):
    return pl.pallas_call(
        add_kernel, in_specs=[VMEM, VMEM], out_specs=VMEM, out_shape=like(a.shape, BF),
        compiler_params=params(16), cost_estimate=cost(0), name="add",
    )(a, b)


def add_small_kernel(a_ref, b_ref, out_ref):
    out_ref[...] = split_small(join_small(a_ref[...]) + join_small(b_ref[...]))


def add_small(a, b):
    return pl.pallas_call(
        add_small_kernel, in_specs=[VMEM, VMEM], out_specs=VMEM, out_shape=like(a.shape, BF),
        compiler_params=params(16), cost_estimate=cost(0), name="add_small",
    )(a, b)


def total_kernel(count, *refs):
    parts, out_ref = refs[:count], refs[count]
    total = parts[0][...].astype(F32)
    for part in parts[1:]:
        total = total + part[...].astype(F32)
    out_ref[...] = total.astype(BF)


def total_of(parts):
    return pl.pallas_call(
        functools.partial(total_kernel, len(parts)),
        in_specs=[VMEM] * len(parts),
        out_specs=VMEM,
        out_shape=like(parts[0].shape, BF),
        compiler_params=params(16),
        cost_estimate=cost(0),
        name="total",
    )(*parts)


def pack_kernel(places, count, *refs):
    parts, small_ref, outs = refs[:count], refs[count], refs[count + 1 :]
    for (j, m), ref in zip(places, outs):
        rows = parts[j].shape[1]
        ref[:rows, :] = parts[j][m]
        ref[rows:, :] = small_ref[...]


def pack(places, parts, small):
    rows, cols = parts[0].shape[1:]
    return pl.pallas_call(
        functools.partial(pack_kernel, places, len(parts)),
        in_specs=[VMEM] * (len(parts) + 1),
        out_specs=[VMEM] * len(places),
        out_shape=[like((rows + EXTRA, cols), BF)] * len(places),
        compiler_params=params(16),
        cost_estimate=cost(0),
        name="pack",
    )(*parts, small)


def unpack_kernel(count, *refs):
    parts, (out_ref, tab_ref, gains_ref) = refs[:count], refs[count:]
    rows = out_ref.shape[1]
    total, table, gains = None, None, None
    for j, part in enumerate(parts):
        piece = part[:rows, :].astype(F32)
        wide = join_small(part[rows:, :])
        total = piece if total is None else total + piece
        table = wide[j : j + 1] if table is None else table + wide[j : j + 1]
        gains = wide if gains is None else gains + wide
    out_ref[0] = total.astype(BF)
    tab_ref[...] = jnp.broadcast_to(table, tab_ref.shape)
    gains_ref[...] = gains


def unpack(parts):
    rows, cols = parts[0].shape
    shape = like((EXTRA // 2, cols), F32)
    return pl.pallas_call(
        functools.partial(unpack_kernel, len(parts)),
        in_specs=[VMEM] * len(parts),
        out_specs=[VMEM] * 3,
        out_shape=[like((1, rows - EXTRA, cols), BF), shape, shape],
        compiler_params=params(16),
        cost_estimate=cost(0),
        name="unpack",
    )(*parts)


def cat_kernel(count, *refs):
    for j in range(count):
        refs[count][j] = refs[j][...]


def cat(parts):
    return pl.pallas_call(
        functools.partial(cat_kernel, len(parts)),
        in_specs=[VMEM] * len(parts),
        out_specs=VMEM,
        out_shape=like((len(parts),) + parts[0].shape, BF),
        compiler_params=params(16),
        cost_estimate=cost(0),
        name="cat",
    )(*parts)


def finish_kernel(count, split, masks, ids_ref, *refs):
    parts, out_refs, mat = refs[:count], refs[count:-1], refs[-1]
    for j in range(parts[0].shape[1]):
        if split:
            put_blocks(ids_ref, masks, parts, mat, j)
            rows = mat.shape[0] // len(out_refs)
            for i, ref in enumerate(out_refs):
                ref[...] = mat[i * rows : (i + 1) * rows, :].astype(F32)
        else:
            put_blocks(ids_ref, masks, parts, out_refs[j], j)


def finish(ids, masks, parts, outs, rows):
    depth = parts[0].shape[-1]
    split = parts[0].shape[1] != outs
    return pl.pallas_call(
        functools.partial(finish_kernel, len(parts), split, masks),
        in_specs=[SMEM] + [VMEM] * len(parts),
        out_specs=[VMEM] * outs,
        out_shape=[like((rows, depth), F32)] * outs,
        scratch_shapes=[pltpu.VMEM((depth, depth), BF)],
        compiler_params=params(24),
        cost_estimate=cost(0),
        name="finish",
    )(ids, *parts)


def bar(*values):
    return list(lax.optimization_barrier(values))


def after(x, *deps):
    return lax.optimization_barrier((x,) + deps)[0]


class Ring:
    def __init__(self, n_dp, n_mp, depth, ids):
        self.n_dp, self.n_mp = n_dp, n_mp
        self.all_bits = (n_dp - 1).bit_length()
        self.bits = min(3, self.all_bits)
        self.rows = depth // (1 << self.bits)
        self.ids = ids
        self.masks = {flip: self.block_masks(flip) for flip in (False, True)}

    def block_masks(self, flip):
        masks, high = [0], list(range(1, self.bits))
        for bit in (high[::-1] if flip else high) + [0]:
            masks = masks + [m | (1 << bit) for m in masks]
        return masks

    def swap(self, x, mask):
        return lax.ppermute(x, "dp", [(i, i ^ mask) for i in range(self.n_dp)])

    def pull(self, x, shift):
        return lax.ppermute(x, "mp", [(i, (i - shift) % self.n_mp) for i in range(self.n_mp)])

    def push(self, x, shift):
        return lax.ppermute(x, "mp", [(i, (i + shift) % self.n_mp) for i in range(self.n_mp)])


class Reduce:
    def __init__(self, ring, send, keep, extra=0):
        self.ring, self.extra = ring, extra
        order = list(range(1, ring.bits))
        self.orders = [order, order[::-1]]
        self.left = [order[::-1], order[::-1]]
        self.groups = [[keep, ring.swap(send, 1)]]
        self.done = False

    def received(self):
        return [group[1] for group in self.groups]

    def set_received(self, values):
        for group, value in zip(self.groups, values):
            group[1] = value

    def step(self):
        ring = self.ring
        if not self.orders[0]:
            out = fold(ring.ids, self.groups, None, self.extra)
            self.out, self.small = out[0], out[1] if self.extra else None
            for bit in range(ring.bits, ring.all_bits):
                self.out = add(self.out, ring.swap(self.out, 1 << bit))
                if self.extra:
                    self.small = add_small(self.small, ring.swap(self.small, 1 << bit))
            self.done = True
            return [self.out]
        runs, bits = [], []
        for g in range(2):
            bit = self.orders[g].pop(0)
            runs.append((bit, row_runs(self.left[g], bit, ring.rows)))
            self.left[g] = [b for b in self.left[g] if b != bit]
            bits.append(bit)
        outs = fold(ring.ids, self.groups, runs, self.extra)
        self.groups = [[outs[2 * g + 1], ring.swap(outs[2 * g], 1 << bits[g])] for g in range(2)]
        return [outs[1], outs[3]]


def body(
    n_dp, n_mp, inputs, gain_attn, w_query, w_key, w_value, w_out, rel_table, gain_ffn, w_in, w_down,
    cotangent, bucket, lengths,
):
    rows, depth = inputs.shape
    buckets, heads = rel_table.shape
    width = heads * HEAD
    slots = lengths.shape[1]
    low = lax.axis_index("dp") & ((1 << min(3, (n_dp - 1).bit_length())) - 1)
    first_row = lax.axis_index("mp") * BIG
    ids = jnp.concatenate([low[None].astype(jnp.int32), bucket, first_row[None].astype(jnp.int32), lengths[0]])
    ring = Ring(n_dp, n_mp, depth, ids)
    shifts = list(range(1, n_mp))
    hot = jnp.asarray(offset_one_hot(buckets), BF)
    gain_one, gain_two = gain_attn[None], gain_ffn[None]

    a_own = [w_out, w_query.T, w_key.T, w_value.T]
    a_piece, f_piece, tab_own = prep(ids, a_own, rel_table.T, w_in, w_down, ring.rows, ring.bits)
    v = {}

    def close(*keys):
        v.update(zip(keys, bar(*[v[key] for key in keys])))

    def swap(new, old, mask):
        v[new] = ring.swap(v[old], mask)

    f3 = n_mp // 2
    f1, f2 = [s for s in shifts if s != f3]
    masks = ring.masks[False]
    v["piece"] = f_piece
    for s in shifts:
        v["z", s] = ring.pull(a_piece, s)
    x_value = inputs.astype(F32)
    n1 = (rms(x_value)[0] * gain_attn.astype(F32)).astype(BF)
    *kept_own, v["hidden"] = attn_fwd(ids, None, n1, a_own, 0, 1, tab_own, hot, inputs, None, slots, heads)
    close(*[("z", s) for s in shifts], "hidden")
    v["a"], tab_rest = join([v["z", s] for s in shifts])
    close("a", "piece")
    swap("ax", "a", 2)
    swap("ay", "a", 4)
    v["f", f1] = ring.pull(v["piece"], f1)
    close("ax", "ay", "a", ("f", f1), "piece")
    swap("ayx", "ax", 4)
    v["a3"] = cat([v["a"], v["ax"], v["ay"]])
    swap("a3c", "a3", 1)
    swap(("fx", f1), ("f", f1), 2)
    v["f", f2] = ring.pull(v["piece"], f2)
    close("ayx", "a3c", ("fx", f1), ("f", f2), "piece")
    v["a1"] = v["ayx"][None]
    swap("a1c", "a1", 1)
    close("a1c", "hidden")
    v["cat", f1] = cat([v["f", f1], v["fx", f1]])
    swap(("far", f1), ("cat", f1), 4)
    swap(("fx", f2), ("f", f2), 2)
    v["f", f3] = ring.pull(v["piece"], f3)
    a_parts = [v["a3"], v["a1"], v["a3c"], v["a1c"]]
    cut = n_mp - 2
    *kept_one, v["hidden"] = attn_fwd(
        ids, masks, n1, a_parts, 0, cut, tab_rest, hot, v["hidden"], None, slots, heads
    )
    close("hidden", ("fx", f2), ("f", f3), ("far", f1))
    v["cat", f2] = cat([v["f", f2], v["fx", f2]])
    swap(("far", f2), ("cat", f2), 4)
    swap(("fx", f3), ("f", f3), 2)
    swap(("catc", f1), ("cat", f1), 1)
    swap(("farc", f1), ("far", f1), 1)
    *kept_two, v["hidden"], v["n2"] = attn_fwd(
        ids, masks, n1, a_parts, cut, 1, tab_rest, hot, v["hidden"], gain_two, slots, heads
    )
    close("hidden", "n2", ("fx", f3), ("catc", f1), ("farc", f1))
    v["cat", f3] = cat([v["f", f3], v["fx", f3]])
    swap(("far", f3), ("cat", f3), 4)
    swap(("catc", f2), ("cat", f2), 1)
    swap(("catc", f3), ("cat", f3), 1)

    def parts_of(s):
        return masks, [v["cat", s], v["far", s], v["catc", s], v["farc", s]]

    v["out"], v["gn"], v["send"], v["keep"] = ffn(
        ids, v["n2"], cotangent, [(None, [w_in, w_down]), parts_of(f1)], None, None
    )
    close("out", "gn", "n2", "send", "keep", ("far", f3), ("far", f2), ("catc", f3), ("catc", f2))
    red = {}

    def reduce(name, extra=0):
        red[name] = Reduce(ring, v["send"], v["keep"], extra)

    def close_with(names, *keys):
        groups = [group for name in names for group in red[name].groups]
        values = bar(*[group[1] for group in groups], *[v[key] for key in keys])
        for group, value in zip(groups, values):
            group[1] = value
        v.update(zip(keys, values[len(groups) :]))

    def folded(names, *keys):
        outs = [out for name in names for out in red[name].step()]
        v.update(zip(keys, bar(*[v[key] for key in keys], *outs)))

    swap(("farc", f2), ("far", f2), 1)
    swap(("farc", f3), ("far", f3), 1)
    reduce("a")
    close_with(["a"], "n2", "out", "gn", ("farc", f3), ("farc", f2))
    folded(["a"], "n2", "out", "gn")
    outputs, v["send"], v["keep"], grad_hidden, v["gh"], gg = ffn(
        ids, v["n2"], cotangent, [parts_of(f2), parts_of(f3)], (v["out"], v["gn"]), (v["hidden"], gain_two)
    )
    close_with(["a"], "send", "keep", "gh")
    reduce("b")
    folded(["a"], "gh")
    close_with(["b"], "gh")
    folded(["b"], "gh")

    places = [(tuple(range(cut)), kept_one), ((cut,), kept_two)]
    rest = (a_parts, tab_rest, places)
    own = (a_own, [*kept_own, tab_own])
    v["send"], v["keep"], v["gn"], tabs = attn_bwd(
        ids, masks, n1, v["gh"], hot, list(range(cut)), rest, None, None, None, slots, heads
    )
    close_with(["a", "b"], "send", "keep", "gh", "gn")
    reduce("c")
    folded(["b", "a"], "gh", "gn")
    v["f1"] = ring.push(red["a"].out[2:], f1)
    close_with(["c"], "gh", "gn")
    folded(["c"], "gh", "gn")
    final = (inputs, gain_one, grad_hidden, gg, tabs)
    v["send"], v["keep"], v["gin"] = attn_bwd(
        ids, masks, n1, v["gh"], hot, [cut, None], rest, own, v["gn"], final, slots, heads
    )
    close_with(["b", "c"], "send", "keep", "gin", "f1")
    reduce("d", EXTRA)
    folded(["b", "c"], "gin")
    v["f2"] = ring.push(red["b"].out[:2], f2)
    v["f3"] = ring.push(red["b"].out[2:], f3)
    close_with(["d"], "gin")
    folded(["d"], "gin")
    close_with(["c"], "gin")
    folded(["c"], "gin")
    close_with(["d"], "gin")
    folded(["d"], "gin")
    close_with(["d"], "gin")
    folded(["d"], "gin")
    packed = pack(((1, 1), (0, 0), (0, 1), (1, 0)), [red["c"].out, red["d"].out], red["d"].small)
    for s in shifts:
        v["a", s] = ring.push(packed[s], s)
    close("f2", "f3", "gin")

    def spread(name, piece):
        v[name, 0] = piece
        for mask in (2, 4, 6):
            v[name, mask] = ring.swap(piece, mask)

    def gathered(name):
        v[name] = cat([v[name, mask] for mask in (0, 2, 4, 6)])
        v[name, 1] = ring.swap(v[name], 1)

    spread("f", total_of([red["a"].out[:2], v["f1"], v["f2"], v["f3"]]))
    close(*[("a", s) for s in shifts], "gin")
    a_total, table, gains = unpack([packed[0]] + [v["a", s] for s in shifts])
    spread("a", a_total)
    close(("f", 2), ("f", 4), ("f", 6), "gin")
    gathered("f")
    close(("f", 1), "gin")
    v["in"], v["down"] = finish(ids, masks, [v["f"], v["f", 1]], 2, depth)
    close("in", "down", ("a", 2), ("a", 4), ("a", 6), "gin")
    gathered("a")
    grad_in, grad_down, grad_inputs = v["in"], v["down"], v["gin"]
    grads = finish(ids, masks, [v["a"], v["a", 1]], 4, width)
    grad_out, grad_query, grad_key, grad_value = grads[0], grads[1].T, grads[2].T, grads[3].T

    grad_table = table[0, : heads * TILE].reshape(heads, TILE)[:, :buckets].T
    return (
        outputs, grad_inputs, grad_query, grad_key, grad_value, grad_out, grad_table,
        gains[n_mp], gains[n_mp + 1], grad_in, grad_down,
    )


def solution(mesh):
    placed = (
        P(("dp", "mp"), None), P(), P(None, "mp"), P(None, "mp"), P(None, "mp"), P("mp", None),
        P(None, "mp"), P(), P(None, "mp"), P("mp", None), P(("dp", "mp"), None), P("dp"), P("dp", None),
    )
    return jax.shard_map(
        functools.partial(body, mesh.shape["dp"], mesh.shape["mp"]),
        mesh=mesh,
        in_specs=placed,
        out_specs=(
            P(("dp", "mp"), None), P(("dp", "mp"), None), P(None, "mp"), P(None, "mp"), P(None, "mp"),
            P("mp", None), P(None, "mp"), P(), P(), P(None, "mp"), P("mp", None),
        ),
        check_vma=False,
    )
```

```python
import functools

import jax
import jax.numpy as jnp
import numpy as np
from jax import lax
from jax.experimental import pallas as pl
from jax.experimental.pallas import tpu as pltpu
from jax.sharding import PartitionSpec as P

BIG = 512
HEAD = 64
EPS = 1e-06
THRESHOLDS = (12, 16, 23, 32, 46, 64, 91)
MASKED = -1e30
TILE = 128
SPAN = 512
EXTRA = 16
BF = jnp.bfloat16
F32 = jnp.float32
MIB = 1024 * 1024
LIMIT = 56
SMEM = pl.BlockSpec(memory_space=pltpu.SMEM)
VMEM = pl.BlockSpec(memory_space=pltpu.VMEM)
ANY = pl.BlockSpec(memory_space=pl.ANY)


def offset_one_hot(buckets):
    offsets = np.arange(SPAN) - SPAN // 2
    distance = np.abs(offsets)
    far = 8 + sum((distance >= t).astype(np.int32) for t in THRESHOLDS)
    bucket = np.where(distance < 8, distance, far) + np.where(offsets > 0, buckets // 2, 0)
    return (np.arange(TILE)[:, None] == bucket[None, :]).astype(np.float32)


def dot_nn(a, b):
    return lax.dot_general(a, b, (((1,), (0,)), ((), ())), preferred_element_type=F32)


def dot_nt(a, b):
    return lax.dot_general(a, b, (((1,), (1,)), ((), ())), preferred_element_type=F32)


def dot_tn(a, b):
    return lax.dot_general(a, b, (((0,), (0,)), ((), ())), preferred_element_type=F32)


def like(shape, dtype):
    return jax.ShapeDtypeStruct(shape, dtype)


def params(mib):
    return pltpu.CompilerParams(vmem_limit_bytes=mib * MIB)


def cost(micros):
    return pl.CostEstimate(flops=micros * 10**9, bytes_accessed=micros * 10**6, transcendentals=0)


def mask_rows(ids_ref, slots):
    bucket = ids_ref[1]
    half = BIG // 2
    segs, starts = [], []
    for part in range(2):
        first = ids_ref[2] + part * half
        seg = jnp.int32(0)
        for j in range(1, slots):
            seg = seg + jnp.where(first >= j * bucket, 1, 0).astype(jnp.int32)
        segs.append(seg)
        starts.append(first - seg * bucket)
    iota = lax.broadcasted_iota(jnp.int32, (1, half), 1)
    rows = []
    for query_part in range(2):
        cols = []
        for key_part in range(2):
            same = segs[query_part] == segs[key_part]
            limit = jnp.where(same, ids_ref[3 + segs[key_part]] - starts[key_part], 0)
            cols.append(jnp.where(iota < limit, 0.0, MASKED).astype(F32))
        rows.append(jnp.concatenate(cols, axis=1))
    return rows


def bias_band(rel_row):
    return pltpu.roll(jnp.broadcast_to(rel_row, (TILE, SPAN)), 0, 1, stride=1, stride_axis=0)


def masked_bias(i, near, rel_row, mask):
    tiles = []
    for j in range(BIG // TILE):
        keys = mask[:, j * TILE : (j + 1) * TILE]
        if abs(j - i) <= 1:
            tiles.append(near[:, (j - i + 2) * TILE : (j - i + 3) * TILE] + keys)
        else:
            far = rel_row[:, SPAN - 1 :] if j > i else rel_row[:, :1]
            tiles.append(jnp.broadcast_to(far + keys, (TILE, TILE)))
    return jnp.concatenate(tiles, axis=1)


def row_block(low, bits):
    return ((low & 1) << (bits - 1)) | (low >> 1)


def side_of(ids_ref, bit):
    return (ids_ref[0] >> bit) & 1


def block_rows(ids_ref, mask, bits, rows):
    return pl.ds(pl.multiple_of(row_block(ids_ref[0] ^ mask, bits) * rows, rows), rows)


class Mover:
    def __init__(self, sems):
        self.sems, self.used, self.out = sems, 0, []

    def copy(self, source, target):
        one = pltpu.make_async_copy(source, target, self.sems.at[self.used])
        self.used += 1
        one.start()
        return one

    def load(self, source, target):
        return [self.copy(source, target)]

    def blocks(self, ids_ref, masks, part_refs, mat, which):
        copies, j, first = [], 0, 0
        for part in part_refs:
            if masks is None:
                copies.append(self.copy(part, mat.at[pl.ds(first, part.shape[0])]))
                first += part.shape[0]
                continue
            bits = (len(masks) - 1).bit_length()
            for e in range(part.shape[0]):
                copies.append(self.copy(part.at[e, which], mat.at[block_rows(ids_ref, masks[j], bits, part.shape[2])]))
                j += 1
        return copies

    def store(self, source, target):
        self.out.append(self.copy(source, target))

    def halves(self, ids_ref, source, send, keep):
        size = source.shape[0] // 2
        for ref, side in ((send, 1 - side_of(ids_ref, 0)), (keep, side_of(ids_ref, 0))):
            self.store(source.at[pl.ds(pl.multiple_of(side * size, size), size)], ref)

    def finish(self):
        wait(self.out)


def wait(copies):
    for one in copies:
        one.wait()


def put_blocks(ids_ref, masks, part_refs, mat, which):
    j, bits = 0, (len(masks) - 1).bit_length()
    for part in part_refs:
        for e in range(part.shape[0]):
            mat[block_rows(ids_ref, masks[j], bits, part.shape[2]), :] = part[e, which].astype(mat.dtype)
            j += 1


def rms(values):
    root = lax.rsqrt(jnp.mean(values * values, axis=1, keepdims=True) + EPS)
    return values * root, root


def rms_back(grad, unit, root, gain):
    scaled = grad * gain
    centred = scaled - unit * jnp.mean(scaled * unit, axis=1, keepdims=True)
    return root * centred, jnp.sum(grad * unit, axis=0, keepdims=True)


def head_slices(qkv_ref, heads, h):
    width = heads * HEAD
    return [qkv_ref[:, j * width + h * HEAD : j * width + (h + 1) * HEAD] for j in (1, 2, 3)]


def forward_scores(h, band, rel, masks, scores, lse_ref):
    probs = []
    for i in range(BIG // TILE):
        rows = slice(i * TILE, (i + 1) * TILE)
        s = scores[h, rows, :] + masked_bias(i, band[h], rel[h : h + 1], masks[i // 2])
        top = jnp.max(s, axis=1, keepdims=True)
        e = jnp.exp(s - top)
        total = jnp.sum(e, axis=1, keepdims=True)
        probs.append((e * (1.0 / total)).astype(BF))
        lse_ref[rows, h : h + 1] = top + jnp.log(total)
    return jnp.concatenate(probs, axis=0)


def attn_fwd_kernel(slots, heads, parts, masks, start, shards, last, ids_ref, *refs):
    refs = list(refs)
    take = lambda n: [refs.pop(0) for _ in range(n)]
    n1_hbm = take(1)[0]
    a_parts = take(parts)
    tab_hbm, hot_hbm, prior_hbm = take(3)
    gain_hbm = take(1)[0] if last else None
    qkv_out, o_out, lse_out, hid_out = take(4)
    n2_out = take(1)[0] if last else None
    n1_ref, mat, tab_ref, hot_ref, prior_ref, gain_ref, qkv_ref, o_ref, lse_ref, hid_ref, n2_ref, band, scores, sems = refs
    move = Mover(sems)
    width = heads * HEAD
    half = BIG // 2
    got_mat = [move.blocks(ids_ref, masks, a_parts, mat.at[0], start)]
    got_n1 = move.load(n1_hbm, n1_ref)
    got_tab = move.load(tab_hbm.at[pl.ds(start, shards)], tab_ref) + move.load(hot_hbm, hot_ref)
    allowed = mask_rows(ids_ref, slots)
    wait(got_tab)
    wait(got_n1)
    for s in range(shards):
        rel = dot_nn(tab_ref[s], hot_ref[...])
        for h in range(heads):
            band[h] = bias_band(rel[h : h + 1])
        wait(got_mat[s])
        if s == 0:
            got_mat += [move.blocks(ids_ref, masks, a_parts, mat.at[t], start + t) for t in range(1, shards)]
            got_prior = move.load(prior_hbm, prior_ref)
            if last:
                got_prior += move.load(gain_hbm, gain_ref)
        qkv_ref[s] = dot_nt(n1_ref[...], mat[s]).astype(BF)
        move.store(qkv_ref.at[s], qkv_out.at[s])
        for h in range(heads):
            q, k, _ = head_slices(qkv_ref.at[s], heads, h)
            scores[h] = dot_nt(q, k)
        for h in range(heads):
            v = head_slices(qkv_ref.at[s], heads, h)[2]
            pb = forward_scores(h, band, rel, allowed, scores, lse_ref.at[s])
            o_ref[s, :, h * HEAD : (h + 1) * HEAD] = dot_nn(pb, v).astype(BF)
        move.store(o_ref.at[s], o_out.at[s])
        move.store(lse_ref.at[s], lse_out.at[s])
        if s == 0:
            wait(got_prior)
        for part in range(2):
            rows = pl.ds(part * half, half)
            before = prior_ref[rows, :].astype(F32) if s == 0 else hid_ref[rows, :]
            hidden = before + dot_nn(o_ref[s, rows, :], mat[s, :width, :])
            hid_ref[rows, :] = hidden
            if s == shards - 1:
                move.store(hid_ref.at[rows], hid_out.at[rows])
                if last:
                    n2_ref[rows, :] = (rms(hidden)[0] * gain_ref[...].astype(F32)).astype(BF)
                    move.store(n2_ref.at[rows], n2_out.at[rows])
    move.finish()


HBM = pl.BlockSpec(memory_space=pltpu.HBM)


def attn_fwd(ids, masks, n1, a_parts, start, shards, tab, hot, prior, gain, slots, heads):
    last = gain is not None
    rows, depth = n1.shape
    width = heads * HEAD
    cols = 4 * width
    args = [n1, *a_parts, tab, hot, prior] + ([gain] if last else [])
    out_shape = [
        like((shards, rows, cols), BF),
        like((shards, rows, width), BF),
        like((shards, rows, TILE), F32),
        like((rows, depth), F32),
    ]
    if last:
        out_shape.append(like((rows, depth), BF))
    return pl.pallas_call(
        functools.partial(attn_fwd_kernel, slots, heads, len(a_parts), masks, start, shards, last),
        in_specs=[SMEM] + [ANY] * len(args),
        out_specs=[HBM] * len(out_shape),
        out_shape=out_shape,
        scratch_shapes=[
            pltpu.VMEM((rows, depth), BF),
            pltpu.VMEM((shards, cols, depth), BF),
            pltpu.VMEM((shards,) + tab.shape[1:], BF),
            pltpu.VMEM(hot.shape, BF),
            pltpu.VMEM(prior.shape, prior.dtype),
            pltpu.VMEM((1, depth), BF),
            pltpu.VMEM((shards, rows, cols), BF),
            pltpu.VMEM((shards, rows, width), BF),
            pltpu.VMEM((shards, rows, TILE), F32),
            pltpu.VMEM((rows, depth), F32),
            pltpu.VMEM((rows, depth), BF),
            pltpu.VMEM((heads, TILE, SPAN), F32),
            pltpu.VMEM((heads, BIG, BIG), F32),
            pltpu.SemaphoreType.DMA((12 + 12 * shards,)),
        ],
        compiler_params=params(LIMIT),
        cost_estimate=cost(16 * shards),
        name="attn_fwd",
    )(ids, *args)


def attn_bwd_kernel(slots, heads, masks, shards, rest, sources, own, first, befores, ids_ref, *refs):
    refs = list(refs)
    take = lambda n: [refs.pop(0) for _ in range(n)]
    last = None in shards
    count = len(shards)
    n1_hbm, gh_hbm, hot_hbm = take(3)
    rest_parts = take(rest)
    rest_tab = take(1)[0]
    rest_kept, rest_at = {}, {}
    for places in sources:
        kept = take(3) + [rest_tab]
        for base, which in enumerate(places):
            rest_kept[which], rest_at[which] = kept, base
    own_parts, own_kept = (take(own), take(4)) if last else ([], [])
    prior_hbm = None if first else take(1)[0]
    if last:
        x_hbm, gain_hbm, ghid_hbm, gain2_hbm = take(4)
        tabs_hbm = take(befores)
        send_out, keep_out, gin_out = take(3)
    else:
        send_out, keep_out, gn_out, tabs_out = take(4)
    n1_ref, gh_ref, hot_ref, mat, qkv_ref, o_ref, lse_ref, tab_ref, gn_ref = take(9)
    band, acc, gs_all, pb_all, gq_all, grads_mat, tabs_ref, sems = take(8)
    move = Mover(sems)
    width = heads * HEAD
    half = BIG // 2
    if last:
        x_ref, gain_ref, ghid_ref, gain2_ref, before_ref, small, packed = take(7)

    def load(c):
        which = shards[c]
        parts, kept = (own_parts, own_kept) if which is None else (rest_parts, rest_kept[which])
        at = 0 if which is None else which
        base = 0 if which is None else rest_at[which]
        got_tab = move.load(kept[3].at[at], tab_ref.at[c])
        got_mat = move.blocks(ids_ref, None if which is None else masks, parts, mat.at[c], at)
        got_kept = move.load(kept[0].at[base], qkv_ref.at[c]) + move.load(kept[2].at[base], lse_ref.at[c])
        return got_tab, got_mat, got_kept, move.load(kept[1].at[base], o_ref.at[c])

    got_first = move.load(hot_hbm, hot_ref) + move.load(gh_hbm, gh_ref)
    got = [load(0)]
    got_n1 = move.load(n1_hbm, n1_ref)
    allowed = mask_rows(ids_ref, slots)
    lane = lax.broadcasted_iota(jnp.int32, (1, SPAN), 1)
    wait(got_first)
    gh = gh_ref[...]
    for c in range(count):
        got_tab, got_mat, got_kept, got_late = got[c]
        acc[...] = jnp.zeros(acc.shape, F32)
        gq_all[c, :, :width] = jnp.zeros((gq_all.shape[1], width), BF)
        wait(got_tab)
        rel = dot_nn(tab_ref[c], hot_ref[...])
        for h in range(heads):
            band[h] = bias_band(rel[h : h + 1])
        wait(got_mat)
        go_all = dot_nt(gh, mat[c, :width, :]).astype(BF)
        wait(got_kept)
        if c == 0:
            got += [load(t) for t in range(1, count)]
            got_prior = [] if first else move.load(prior_hbm, gn_ref)
            if last:
                got_prior += move.load(x_hbm, x_ref) + move.load(gain_hbm, gain_ref)
                got_prior += move.load(ghid_hbm, ghid_ref) + move.load(gain2_hbm, gain2_ref)
                done = 0
                for ref in tabs_hbm:
                    got_prior += move.load(ref, before_ref.at[pl.ds(done, ref.shape[0])])
                    done += ref.shape[0]
        far = []
        for h in range(heads):
            q, k, v = head_slices(qkv_ref.at[c], heads, h)
            go = go_all[:, h * HEAD : (h + 1) * HEAD]
            low = jnp.zeros((1, TILE), F32)
            high = jnp.zeros((1, TILE), F32)
            for i in range(BIG // TILE):
                rows = slice(i * TILE, (i + 1) * TILE)
                s = dot_nt(q[rows], k) + masked_bias(i, band[h], rel[h : h + 1], allowed[i // 2])
                p = jnp.exp(s - lse_ref[c, rows, h : h + 1])
                dp = dot_nt(go[rows], v)
                inner = jnp.sum(p * dp, axis=1, keepdims=True)
                gs = (p * (dp - inner)).astype(BF)
                gs_all[h, rows, :] = gs
                pb_all[h, rows, :] = p.astype(BF)
                wide = gs.astype(F32)
                for j in range(BIG // TILE):
                    tile = wide[:, j * TILE : (j + 1) * TILE]
                    if abs(j - i) <= 1:
                        acc[h, :, (j - i + 2) * TILE : (j - i + 3) * TILE] += tile
                    elif j > i:
                        high = high + jnp.sum(tile, axis=0, keepdims=True)
                    else:
                        low = low + jnp.sum(tile, axis=0, keepdims=True)
            at = lambda j: slice(j * width + h * HEAD, j * width + (h + 1) * HEAD)
            gq_all[c, :, at(1)] = dot_nn(gs_all[h], k).astype(BF)
            gq_all[c, :, at(2)] = dot_tn(gs_all[h], q).astype(BF)
            gq_all[c, :, at(3)] = dot_tn(pb_all[h], go).astype(BF)
            far.append((low, high))
        wait(got_late)
        if c == 0:
            wait(got_n1)
        grads_mat[c] = dot_tn(gq_all[c], n1_ref[...]).astype(BF)
        grads_mat[c, :width, :] = dot_tn(o_ref[c], gh).astype(BF)
        size = pl.ds(0, grads_mat.shape[1] // 2)
        move.halves(ids_ref, grads_mat.at[c], send_out.at[c, size], keep_out.at[c, size])
        near = acc[...]
        n = TILE // 2
        while n >= 8:
            near = near[:, :n] + pltpu.roll(near[:, n:], SPAN - n, 2)
            n //= 2
        line = near[:, 0:1]
        for j in range(1, 8):
            line = line + pltpu.roll(near[:, j : j + 1], SPAN - j, 2)
        lines = []
        for h, (low, high) in enumerate(far):
            ends = jnp.where(lane == 0, jnp.sum(low, axis=1, keepdims=True), 0.0)
            ends = ends + jnp.where(lane == SPAN - 1, jnp.sum(high, axis=1, keepdims=True), 0.0)
            lines.append(line[h] + ends)
        lines = jnp.concatenate(lines + [jnp.zeros((8 - heads, SPAN), F32)], axis=0)
        tabs_ref[c] = lax.dot_general(
            lines, hot_ref[...].astype(F32), (((1,), (1,)), ((), ())),
            precision=lax.Precision.HIGHEST, preferred_element_type=F32,
        )
        if c == 0:
            wait(got_prior)
        for part in range(2):
            rows = pl.ds(part * half, half)
            gn = dot_nn(gq_all[c, rows, :], mat[c])
            if not (first and c == 0):
                gn = gn + gn_ref[rows, :]
            gn_ref[rows, :] = gn
            if c == count - 1 and not last:
                move.store(gn_ref.at[rows], gn_out.at[rows])
    if not last:
        move.store(tabs_ref, tabs_out)
        move.finish()
        return
    unit, root = rms(x_ref[...].astype(F32))
    back, gain_grad = rms_back(gn_ref[...], unit, root, gain_ref[...].astype(F32))
    small[...] = jnp.zeros_like(small)
    total = before_ref.shape[0] + count
    tables = [tabs_ref[count - 1]] + [before_ref[j] for j in range(total - count)]
    tables += [tabs_ref[c] for c in range(count - 1)]
    for row, value in enumerate(tables):
        for h in range(heads):
            small[row : row + 1, h * TILE : (h + 1) * TILE] = value[h : h + 1]
    small[total : total + 1, :] = gain_grad
    small[total + 1 : total + 2, :] = gain2_ref[0:1, :]
    packed[...] = split_small(small[...])
    tail = pl.ds(grads_mat.shape[1] // 2, EXTRA)
    for c in range(count):
        move.store(packed, send_out.at[c, tail])
        move.store(packed, keep_out.at[c, tail])
    gh_ref[...] = (ghid_ref[...] + back).astype(BF)
    move.store(gh_ref, gin_out)
    move.finish()


def split_small(value):
    high = value.astype(BF)
    low = (value - high.astype(F32)).astype(BF)
    return jnp.concatenate([high.astype(F32), low.astype(F32)], axis=0).astype(BF)


def join_small(packed):
    wide = packed.astype(F32)
    return wide[: EXTRA // 2] + wide[EXTRA // 2 :]


def attn_bwd(ids, masks, n1, gh, hot, shards, rest, own, prior, final, slots, heads):
    last, first = None in shards, prior is None
    count = len(shards)
    rows, depth = n1.shape
    width = heads * HEAD
    cols = 4 * width
    parts, tab, sources = rest
    sources = [(places, kept) for places, kept in sources if set(places) & set(shards)]
    args = [n1, gh, hot, *parts, tab] + [k for _, kept in sources for k in kept]
    args += [*own[0], *own[1]] if last else []
    args += ([] if first else [prior]) + (list(final) if last else [])
    befores = len(final) - 4 if last else 0
    half = like((count, cols // 2 + (EXTRA if last else 0), depth), BF)
    if last:
        out_shape = [half, half, like((rows, depth), BF)]
    else:
        out_shape = [half, half, like((rows, depth), F32), like((count, 8, TILE), F32)]
    scratch = [
        pltpu.VMEM((rows, depth), BF),
        pltpu.VMEM((rows, depth), BF),
        pltpu.VMEM(hot.shape, BF),
        pltpu.VMEM((count, cols, depth), BF),
        pltpu.VMEM((count, rows, cols), BF),
        pltpu.VMEM((count, rows, width), BF),
        pltpu.VMEM((count, rows, TILE), F32),
        pltpu.VMEM((count,) + tab.shape[1:], BF),
        pltpu.VMEM((rows, depth), F32),
        pltpu.VMEM((heads, TILE, SPAN), F32),
        pltpu.VMEM((heads, TILE, SPAN), F32),
        pltpu.VMEM((heads, BIG, BIG), BF),
        pltpu.VMEM((heads, BIG, BIG), BF),
        pltpu.VMEM((count, rows, cols), BF),
        pltpu.VMEM((count, cols, depth), BF),
        pltpu.VMEM((count, 8, TILE), F32),
        pltpu.SemaphoreType.DMA((16 + 18 * count,)),
    ]
    if last:
        scratch += [
            pltpu.VMEM((rows, depth), BF),
            pltpu.VMEM((1, depth), BF),
            pltpu.VMEM((rows, depth), F32),
            pltpu.VMEM((8, depth), F32),
            pltpu.VMEM((sum(f.shape[0] for f in final[4:]), 8, TILE), F32),
            pltpu.VMEM((8, depth), F32),
            pltpu.VMEM((EXTRA, depth), BF),
        ]
    return pl.pallas_call(
        functools.partial(
            attn_bwd_kernel, slots, heads, masks, tuple(shards), len(parts), tuple(p for p, _ in sources),
            len(own[0]) if last else 0, first, befores,
        ),
        in_specs=[SMEM] + [ANY] * len(args),
        out_specs=[HBM] * len(out_shape),
        out_shape=out_shape,
        scratch_shapes=scratch,
        compiler_params=params(LIMIT),
        cost_estimate=cost(32 * count),
        name="attn_bwd",
    )(ids, *args)


def ffn_kernel(parts, masks, first, last, ids_ref, *refs):
    refs = list(refs)
    take = lambda n: [refs.pop(0) for _ in range(n)]
    count = len(parts)
    n2_hbm, cot_hbm = take(2)
    f_parts = [take(n or 2) for n in parts]
    out_in, gn_in = (None, None) if first else take(2)
    if last:
        hid_in, gain_in = take(2)
        out_out, send_out, keep_out, ghid_out, gh_out, gg_out = take(6)
    else:
        out_out, gn_out, send_out, keep_out = take(4)
    n2_ref, cot_ref, i_mat, w_mat, act_ref, gp_ref, gi_mat, gw_mat, out_ref, gn_ref, sems = take(11)
    move = Mover(sems)
    hid_ref, gain_ref, y_ref, gg_ref = take(4) if last else [None] * 4

    def load(c):
        if not parts[c]:
            return move.load(f_parts[c][0], i_mat.at[c]), move.load(f_parts[c][1], w_mat.at[c])
        return tuple(move.blocks(ids_ref, masks[c], f_parts[c], mat.at[c], j) for j, mat in enumerate((i_mat, w_mat)))

    got_n2 = move.load(n2_hbm, n2_ref)
    got = [load(0)]
    got_cot = move.load(cot_hbm, cot_ref)
    c0 = 0.7978845608028654
    c1 = 0.044715
    size = n2_ref.shape[0] // 2
    gain_grad = None
    for c in range(count):
        wait(got[c][0])
        if c == 0:
            wait(got_n2)
            got += [load(t) for t in range(1, count)]
            got_sums = [] if first else move.load(out_in, out_ref) + move.load(gn_in, gn_ref)
            if last:
                got_sums += move.load(hid_in, hid_ref) + move.load(gain_in, gain_ref)
        pre = dot_nn(n2_ref[...], i_mat[c])
        square = pre * pre
        th = jnp.tanh(pre * (c0 + (c0 * c1) * square))
        half = 0.5 * (1.0 + th)
        act_ref[c] = (pre * half).astype(BF)
        slope = half + (0.5 * pre) * (1.0 - th * th) * (c0 + (3.0 * c0 * c1) * square)
        wait(got[c][1])
        if c == 0:
            wait(got_cot)
        cot = cot_ref[...]
        gp_ref[c] = (dot_nt(cot, w_mat[c]) * slope).astype(BF)
        gw_mat[c] = dot_tn(act_ref[c], cot).astype(BF)
        move.halves(ids_ref, gw_mat.at[c], send_out.at[2 * c + 1], keep_out.at[2 * c + 1])
        gi_mat[c] = dot_tn(n2_ref[...], gp_ref[c]).astype(BF)
        move.halves(ids_ref, gi_mat.at[c], send_out.at[2 * c], keep_out.at[2 * c])
        if c == 0:
            wait(got_sums)
        ending = c == count - 1
        for part in range(2):
            rows = pl.ds(part * size, size)
            gn = dot_nt(gp_ref[c, rows, :], i_mat[c])
            out = dot_nn(act_ref[c, rows, :], w_mat[c])
            if not (first and c == 0):
                out = out + out_ref[rows, :]
                gn = gn + gn_ref[rows, :]
            if not (last and ending):
                gn_ref[rows, :] = gn
                out_ref[rows, :] = out
                if ending:
                    move.store(gn_ref.at[rows], gn_out.at[rows])
                    move.store(out_ref.at[rows], out_out.at[rows])
                continue
            hidden = hid_ref[rows, :]
            y_ref[rows, :] = (hidden + out).astype(BF)
            move.store(y_ref.at[rows], out_out.at[rows])
            unit, root = rms(hidden)
            back, gain_part = rms_back(gn, unit, root, gain_ref[...].astype(F32))
            gain_grad = gain_part if gain_grad is None else gain_grad + gain_part
            grad_hidden = cot_ref[rows, :].astype(F32) + back
            gn_ref[rows, :] = grad_hidden
            move.store(gn_ref.at[rows], ghid_out.at[rows])
            n2_ref[rows, :] = grad_hidden.astype(BF)
            move.store(n2_ref.at[rows], gh_out.at[rows])
    if last:
        gg_ref[...] = jnp.broadcast_to(gain_grad, gg_ref.shape)
        move.store(gg_ref, gg_out)
    move.finish()


def ffn(ids, n2, cot, shards, sums, final):
    first, last = sums is None, final is not None
    rows, depth = n2.shape
    count = len(shards)
    units = shards[-1][1][0].shape[-1]
    half = like((2 * count, depth // 2, units), BF)
    total = like((rows, depth), F32)
    args = [n2, cot] + [p for _, ps in shards for p in ps]
    args += ([] if first else list(sums)) + ([] if not last else list(final))
    if last:
        out_shape = [like((rows, depth), BF), half, half, total, like((rows, depth), BF), like((8, depth), F32)]
    else:
        out_shape = [total, total, half, half]
    scratch = [
        pltpu.VMEM((rows, depth), BF),
        pltpu.VMEM((rows, depth), BF),
        pltpu.VMEM((count, depth, units), BF),
        pltpu.VMEM((count, units, depth), BF),
        pltpu.VMEM((count, rows, units), BF),
        pltpu.VMEM((count, rows, units), BF),
        pltpu.VMEM((count, depth, units), BF),
        pltpu.VMEM((count, units, depth), BF),
        pltpu.VMEM((rows, depth), F32),
        pltpu.VMEM((rows, depth), F32),
        pltpu.SemaphoreType.DMA((20 + 20 * count,)),
    ]
    if last:
        scratch += [
            pltpu.VMEM((rows, depth), F32),
            pltpu.VMEM((1, depth), BF),
            pltpu.VMEM((rows, depth), BF),
            pltpu.VMEM((8, depth), F32),
        ]
    return pl.pallas_call(
        functools.partial(
            ffn_kernel, tuple(0 if m is None else len(p) for m, p in shards), [m for m, _ in shards], first, last
        ),
        in_specs=[SMEM] + [ANY] * len(args),
        out_specs=[HBM] * len(out_shape),
        out_shape=out_shape,
        scratch_shapes=scratch,
        compiler_params=params(LIMIT),
        cost_estimate=cost(32 * count),
        name="ffn",
    )(ids, *args)


def prep_kernel(rows, bits, count, *refs):
    mats, (tab_ref, in_ref, down_ref, a_ref, f_ref, wide_ref, sems) = refs[:count], refs[count:]
    block = row_block(lax.axis_index("dp") & ((1 << bits) - 1), bits)
    first = pl.ds(pl.multiple_of(block * rows, rows), rows)
    copies = [
        pltpu.make_async_copy(in_ref.at[first], f_ref.at[0], sems.at[0]),
        pltpu.make_async_copy(down_ref.at[first], f_ref.at[1], sems.at[1]),
    ]
    per = mats[0].shape[0] // rows

    def piece(j, mat):
        at = pl.ds(pl.multiple_of((block - j * per) * rows, rows), rows)
        return pltpu.make_async_copy(mat.at[at], a_ref.at[pl.ds(0, rows)], sems.at[2])

    for j, mat in enumerate(mats):
        @pl.when(block // per == j)
        def _():
            piece(j, mat).start()

    for copy in copies:
        copy.start()
    tab = tab_ref[...].astype(F32)
    heads, buckets = tab.shape
    tab = jnp.concatenate([tab, jnp.zeros((heads, TILE - buckets), F32)], axis=1)
    tab = jnp.concatenate([tab, jnp.zeros((EXTRA - heads, TILE), F32)], axis=0).astype(BF)
    wide_ref[0] = tab
    a_ref[rows:, :] = jnp.zeros((EXTRA, a_ref.shape[1]), BF)
    a_ref[rows:, :TILE] = tab
    for j, mat in enumerate(mats):
        @pl.when(block // per == j)
        def _():
            piece(j, mat).wait()

    for copy in copies:
        copy.wait()


def prep(mats, tab, w_in, w_down, rows, bits):
    depth = w_in.shape[0]
    return pl.pallas_call(
        functools.partial(prep_kernel, rows, bits, len(mats)),
        in_specs=[ANY] * len(mats) + [VMEM, ANY, ANY],
        out_specs=[VMEM, VMEM, VMEM],
        out_shape=[like((rows + EXTRA, depth), BF), like((2, rows, depth), BF), like((1, EXTRA, TILE), BF)],
        scratch_shapes=[pltpu.SemaphoreType.DMA((3,))],
        compiler_params=params(60),
        cost_estimate=cost(0),
        name="prep",
    )(*mats, tab, w_in, w_down)


def join_kernel(count, *refs):
    parts, (a_ref, tab_ref) = refs[:count], refs[count:]
    rows = a_ref.shape[1]
    for j, part in enumerate(parts):
        a_ref[j] = part[:rows, :]
        tab_ref[j] = part[rows:, :TILE]


def join(parts):
    rows, depth = parts[0].shape
    return pl.pallas_call(
        functools.partial(join_kernel, len(parts)),
        in_specs=[VMEM] * len(parts),
        out_specs=[VMEM, VMEM],
        out_shape=[like((len(parts), rows - EXTRA, depth), BF), like((len(parts), EXTRA, TILE), BF)],
        compiler_params=params(16),
        cost_estimate=cost(0),
        name="join",
    )(*parts)


def row_runs(left, bit, rows):
    inner = rows
    for b in left[left.index(bit) + 1 :]:
        inner *= 2
    outer = 1
    for b in left[: left.index(bit)]:
        outer *= 2
    return [(o * 2 * inner, inner, o * inner) for o in range(outer)]


def fold_kernel(runs, extra, joined, split, ids_ref, *refs):
    if joined:
        keep_ref, recv_ref = refs[:2]
        n = keep_ref.shape[0] // 2
        ins = [(keep_ref.at[pl.ds(g * n, n)], recv_ref.at[pl.ds(g * n, n)]) for g in range(2)]
        outs = refs[2:]
    else:
        ins, outs = [refs[0:2], refs[2:4]], refs[4:]
    packed = None
    if extra:
        keep, recv = ins[1]
        tail = pl.ds(keep.shape[1] - extra, extra)
        packed = split_small(join_small(keep[0, tail, :]) + join_small(recv[0, tail, :]))
    for g, (keep, recv) in enumerate(ins):
        def total(rows):
            return (keep[:, rows, :].astype(F32) + recv[:, rows, :].astype(F32)).astype(BF)

        if runs is None:
            value, done = total(pl.ds(0, outs[0].shape[1])), 0
            for ref in outs[: split[0]] if g == 0 else outs[split[0] : split[0] + split[1]]:
                ref[...] = value[done : done + ref.shape[0]]
                done += ref.shape[0]
            continue
        bit, group_runs = runs[g]
        mine = side_of(ids_ref, bit)
        for ref, side in ((outs[2 * g], 1 - mine), (outs[2 * g + 1], mine)):
            for source, length, target in group_runs:
                ref[:, target : target + length, :] = total(pl.ds(pl.multiple_of(source + side * length, length), length))
            if extra and g == 1:
                done = sum(length for _, length, _ in group_runs)
                for m in range(ref.shape[0]):
                    ref[m, done:, :] = packed
    if extra and runs is None:
        outs[-1][...] = packed


def fold(ids, groups, runs, extra, split=(1, 1)):
    joined = len(groups) == 1
    arrays = [a for group in groups for a in group]
    if joined:
        count = arrays[0].shape[0] // 2
        bodies = [arrays[0].shape[1] - extra] * 2
    else:
        count = arrays[0].shape[0]
        bodies = [arrays[0].shape[1], arrays[2].shape[1] - extra]
    cols = arrays[0].shape[2]
    if runs is None:
        out_shape = [like((count // n, bodies[0], cols), BF) for n in split for _ in range(n)]
        out_shape += [like((extra, cols), BF)] if extra else []
    else:
        tails = (0, extra)
        out_shape = [like((count, bodies[g] // 2 + tails[g], cols), BF) for g in (0, 0, 1, 1)]
    return pl.pallas_call(
        functools.partial(fold_kernel, runs, extra, joined, split),
        in_specs=[SMEM] + [VMEM] * len(arrays),
        out_specs=[VMEM] * len(out_shape),
        out_shape=out_shape,
        compiler_params=params(24),
        cost_estimate=cost(0),
        name="fold",
    )(ids, *arrays)


def add_kernel(a_ref, b_ref, out_ref):
    out_ref[...] = (a_ref[...].astype(F32) + b_ref[...].astype(F32)).astype(BF)


def add(a, b):
    return pl.pallas_call(
        add_kernel, in_specs=[VMEM, VMEM], out_specs=VMEM, out_shape=like(a.shape, BF),
        compiler_params=params(16), cost_estimate=cost(0), name="add",
    )(a, b)


def add_small_kernel(a_ref, b_ref, out_ref):
    out_ref[...] = split_small(join_small(a_ref[...]) + join_small(b_ref[...]))


def add_small(a, b):
    return pl.pallas_call(
        add_small_kernel, in_specs=[VMEM, VMEM], out_specs=VMEM, out_shape=like(a.shape, BF),
        compiler_params=params(16), cost_estimate=cost(0), name="add_small",
    )(a, b)


def total_kernel(*refs):
    total = refs[0][...].astype(F32)
    for ref in refs[1:-1]:
        total = total + ref[...].astype(F32)
    refs[-1][...] = total.astype(BF)


def total_of(parts):
    return pl.pallas_call(
        total_kernel, in_specs=[VMEM] * len(parts), out_specs=VMEM, out_shape=like(parts[0].shape, BF),
        compiler_params=params(16), cost_estimate=cost(0), name="total",
    )(*parts)


def pack_kernel(places, count, *refs):
    parts, small_ref, outs = refs[:count], refs[count], refs[count + 1 :]
    for (j, m), ref in zip(places, outs):
        rows = parts[j].shape[1]
        ref[:rows, :] = parts[j][m]
        ref[rows:, :] = small_ref[...]


def pack(places, parts, small):
    rows, cols = parts[0].shape[1:]
    return pl.pallas_call(
        functools.partial(pack_kernel, places, len(parts)),
        in_specs=[VMEM] * (len(parts) + 1),
        out_specs=[VMEM] * len(places),
        out_shape=[like((rows + EXTRA, cols), BF)] * len(places),
        compiler_params=params(16),
        cost_estimate=cost(0),
        name="pack",
    )(*parts, small)


def unpack_kernel(count, *refs):
    parts, (out_ref, tab_ref, gains_ref) = refs[:count], refs[count:]
    rows = out_ref.shape[1]
    total, table, gains = None, None, None
    for j, part in enumerate(parts):
        piece = part[:rows, :].astype(F32)
        wide = join_small(part[rows:, :])
        total = piece if total is None else total + piece
        table = wide[j : j + 1] if table is None else table + wide[j : j + 1]
        gains = wide if gains is None else gains + wide
    out_ref[0] = total.astype(BF)
    tab_ref[...] = jnp.broadcast_to(table, tab_ref.shape)
    gains_ref[...] = gains


def unpack(parts):
    rows, cols = parts[0].shape
    shape = like((EXTRA // 2, cols), F32)
    return pl.pallas_call(
        functools.partial(unpack_kernel, len(parts)),
        in_specs=[VMEM] * len(parts),
        out_specs=[VMEM] * 3,
        out_shape=[like((1, rows - EXTRA, cols), BF), shape, shape],
        compiler_params=params(16),
        cost_estimate=cost(0),
        name="unpack",
    )(*parts)


def cat_kernel(count, *refs):
    for j in range(count):
        refs[count][j] = refs[j][...]


def cat(parts):
    return pl.pallas_call(
        functools.partial(cat_kernel, len(parts)),
        in_specs=[VMEM] * len(parts),
        out_specs=VMEM,
        out_shape=like((len(parts),) + parts[0].shape, BF),
        compiler_params=params(16),
        cost_estimate=cost(0),
        name="cat",
    )(*parts)


def finish_kernel(count, split, masks, ids_ref, *refs):
    parts, out_refs, mat = refs[:count], refs[count:-1], refs[-1]
    for j in range(parts[0].shape[1]):
        if split:
            put_blocks(ids_ref, masks, parts, mat, j)
            rows = mat.shape[0] // len(out_refs)
            for i, ref in enumerate(out_refs):
                ref[...] = mat[i * rows : (i + 1) * rows, :].astype(F32)
        else:
            put_blocks(ids_ref, masks, parts, out_refs[j], j)


def finish(ids, masks, parts, outs, rows):
    depth = parts[0].shape[-1]
    split = parts[0].shape[1] != outs
    return pl.pallas_call(
        functools.partial(finish_kernel, len(parts), split, masks),
        in_specs=[SMEM] + [VMEM] * len(parts),
        out_specs=[VMEM] * outs,
        out_shape=[like((rows, depth), F32)] * outs,
        scratch_shapes=[pltpu.VMEM((depth, depth), BF)],
        compiler_params=params(24),
        cost_estimate=cost(0),
        name="finish",
    )(ids, *parts)


def bar(*values):
    return list(lax.optimization_barrier(values))


def after(x, *deps):
    return lax.optimization_barrier((x,) + deps)[0]


class Ring:
    def __init__(self, n_dp, n_mp, depth, ids):
        self.n_dp, self.n_mp = n_dp, n_mp
        self.all_bits = (n_dp - 1).bit_length()
        self.bits = min(3, self.all_bits)
        self.rows = depth // (1 << self.bits)
        self.ids = ids
        self.masks = {flip: self.block_masks(flip) for flip in (False, True)}

    def block_masks(self, flip):
        masks, high = [0], list(range(1, self.bits))
        for bit in (high[::-1] if flip else high) + [0]:
            masks = masks + [m | (1 << bit) for m in masks]
        return masks

    def swap(self, x, mask):
        return lax.ppermute(x, "dp", [(i, i ^ mask) for i in range(self.n_dp)])

    def pull(self, x, shift):
        return lax.ppermute(x, "mp", [(i, (i - shift) % self.n_mp) for i in range(self.n_mp)])

    def push(self, x, shift):
        return lax.ppermute(x, "mp", [(i, (i + shift) % self.n_mp) for i in range(self.n_mp)])


class Reduce:
    def __init__(self, ring, send, keep, extra=0, split=(1, 1)):
        self.ring, self.extra, self.split = ring, extra, split
        order = list(range(1, ring.bits))
        self.orders = [order, order[::-1]]
        self.left = [order[::-1], order[::-1]]
        self.groups = [[keep, ring.swap(send, 1)]]
        self.done = False

    def received(self):
        return [group[1] for group in self.groups]

    def set_received(self, values):
        for group, value in zip(self.groups, values):
            group[1] = value

    def step(self):
        ring = self.ring
        if not self.orders[0]:
            out = fold(ring.ids, self.groups, None, self.extra, self.split)
            self.out, self.small = list(out[: sum(self.split)]), out[-1] if self.extra else None
            for bit in range(ring.bits, ring.all_bits):
                self.out = [add(out, ring.swap(out, 1 << bit)) for out in self.out]
                if self.extra:
                    self.small = add_small(self.small, ring.swap(self.small, 1 << bit))
            self.done = True
            return list(self.out)
        runs, bits = [], []
        for g in range(2):
            bit = self.orders[g].pop(0)
            runs.append((bit, row_runs(self.left[g], bit, ring.rows)))
            self.left[g] = [b for b in self.left[g] if b != bit]
            bits.append(bit)
        outs = fold(ring.ids, self.groups, runs, self.extra)
        self.groups = [[outs[2 * g + 1], ring.swap(outs[2 * g], 1 << bits[g])] for g in range(2)]
        return [outs[1], outs[3]]


def body(
    n_dp, n_mp, inputs, gain_attn, w_query, w_key, w_value, w_out, rel_table, gain_ffn, w_in, w_down,
    cotangent, bucket, lengths,
):
    rows, depth = inputs.shape
    buckets, heads = rel_table.shape
    width = heads * HEAD
    slots = lengths.shape[1]
    low = lax.axis_index("dp") & ((1 << min(3, (n_dp - 1).bit_length())) - 1)
    first_row = lax.axis_index("mp") * BIG
    ids = jnp.concatenate([low[None].astype(jnp.int32), bucket, first_row[None].astype(jnp.int32), lengths[0]])
    ring = Ring(n_dp, n_mp, depth, ids)
    shifts = list(range(1, n_mp))
    hot = jnp.asarray(offset_one_hot(buckets), BF)
    gain_one, gain_two = gain_attn[None], gain_ffn[None]

    a_own = [w_out, w_query.T, w_key.T, w_value.T]
    a_piece, f_piece, tab_own = prep(a_own, rel_table.T, w_in, w_down, ring.rows, ring.bits)
    v = {}

    def close(*keys):
        v.update(zip(keys, bar(*[v[key] for key in keys])))

    def swap(new, old, mask):
        v[new] = ring.swap(v[old], mask)

    f3 = n_mp // 2
    f1, f2 = [s for s in shifts if s != f3]
    masks = ring.masks[False]
    v["piece"] = f_piece
    for s in shifts:
        v["z", s] = ring.pull(a_piece, s)
    x_value = inputs.astype(F32)
    n1 = (rms(x_value)[0] * gain_attn.astype(F32)).astype(BF)
    *kept_own, v["hidden"] = attn_fwd(ids, None, n1, a_own, 0, 1, tab_own, hot, inputs, None, slots, heads)
    v["gain1"], v["gain2"] = gain_one, gain_two
    close(*[("z", s) for s in shifts], "hidden", "gain1", "gain2")
    gain_one, gain_two = v["gain1"], v["gain2"]
    v["a"], tab_rest = join([v["z", s] for s in shifts])
    close("a", "piece")
    swap("ax", "a", 2)
    swap("ay", "a", 4)
    v["f", f1] = ring.pull(v["piece"], f1)
    close("ax", "ay", "a", ("f", f1), "piece")
    swap("ayx", "ax", 4)
    v["a3"] = cat([v["a"], v["ax"], v["ay"]])
    swap("a3c", "a3", 1)
    swap(("fx", f1), ("f", f1), 2)
    v["f", f2] = ring.pull(v["piece"], f2)
    close("ayx", "a3c", ("fx", f1), ("f", f2), "piece")
    v["a1"] = v["ayx"][None]
    swap("a1c", "a1", 1)
    close("a1c", "hidden")
    v["cat", f1] = cat([v["f", f1], v["fx", f1]])
    swap(("far", f1), ("cat", f1), 4)
    swap(("fx", f2), ("f", f2), 2)
    v["f", f3] = ring.pull(v["piece"], f3)
    a_parts = [v["a3"], v["a1"], v["a3c"], v["a1c"]]
    cut = n_mp - 2
    *kept_one, v["hidden"] = attn_fwd(
        ids, masks, n1, a_parts, 0, cut, tab_rest, hot, v["hidden"], None, slots, heads
    )
    close("hidden", ("fx", f2), ("f", f3), ("far", f1))
    v["cat", f2] = cat([v["f", f2], v["fx", f2]])
    swap(("far", f2), ("cat", f2), 4)
    swap(("fx", f3), ("f", f3), 2)
    swap(("catc", f1), ("cat", f1), 1)
    swap(("farc", f1), ("far", f1), 1)
    *kept_two, v["hidden"], v["n2"] = attn_fwd(
        ids, masks, n1, a_parts, cut, 1, tab_rest, hot, v["hidden"], gain_two, slots, heads
    )
    close("hidden", "n2", ("fx", f3), ("catc", f1), ("farc", f1))
    v["cat", f3] = cat([v["f", f3], v["fx", f3]])
    swap(("far", f3), ("cat", f3), 4)
    swap(("catc", f2), ("cat", f2), 1)
    swap(("catc", f3), ("cat", f3), 1)

    def parts_of(s):
        return masks, [v["cat", s], v["far", s], v["catc", s], v["farc", s]]

    v["out"], v["gn"], v["send"], v["keep"] = ffn(
        ids, v["n2"], cotangent, [(None, [w_in, w_down]), parts_of(f1)], None, None
    )
    close("out", "gn", "n2", "send", "keep", ("far", f3), ("far", f2), ("catc", f3), ("catc", f2))
    red = {}

    def reduce(name, extra=0, split=(1, 1)):
        red[name] = Reduce(ring, v["send"], v["keep"], extra, split)

    def close_with(names, *keys):
        groups = [group for name in names for group in red[name].groups]
        values = bar(*[group[1] for group in groups], *[v[key] for key in keys])
        for group, value in zip(groups, values):
            group[1] = value
        v.update(zip(keys, values[len(groups) :]))

    def folded(names, *keys):
        outs = [out for name in names for out in red[name].step()]
        v.update(zip(keys, bar(*[v[key] for key in keys], *outs)))

    swap(("farc", f2), ("far", f2), 1)
    swap(("farc", f3), ("far", f3), 1)
    reduce("a")
    close_with(["a"], "n2", "out", "gn", ("farc", f3), ("farc", f2))
    folded(["a"], "n2", "out", "gn")
    outputs, v["send"], v["keep"], grad_hidden, v["gh"], gg = ffn(
        ids, v["n2"], cotangent, [parts_of(f2), parts_of(f3)], (v["out"], v["gn"]), (v["hidden"], gain_two)
    )
    close_with(["a"], "send", "keep", "gh")
    reduce("b")
    folded(["a"], "gh")
    close_with(["b"], "gh")
    folded(["b"], "gh")

    places = [(tuple(range(cut)), kept_one), ((cut,), kept_two)]
    rest = (a_parts, tab_rest, places)
    own = (a_own, [*kept_own, tab_own])
    v["send"], v["keep"], v["gn"], tabs = attn_bwd(
        ids, masks, n1, v["gh"], hot, list(range(cut)), rest, None, None, None, slots, heads
    )
    close_with(["a", "b"], "send", "keep", "gh", "gn")
    reduce("c")
    folded(["b", "a"], "gh", "gn")
    v["f1"] = ring.push(red["a"].out[1], f1)
    close_with(["c"], "gh", "gn")
    folded(["c"], "gh", "gn")
    final = (inputs, gain_one, grad_hidden, gg, tabs)
    v["send"], v["keep"], v["gin"] = attn_bwd(
        ids, masks, n1, v["gh"], hot, [cut, None], rest, own, v["gn"], final, slots, heads
    )
    close_with(["b", "c"], "send", "keep", "gin", "f1")
    reduce("d", EXTRA)
    folded(["b", "c"], "gin")
    v["f2"] = ring.push(red["b"].out[0], f2)
    v["f3"] = ring.push(red["b"].out[1], f3)

    def spread(name, piece):
        v[name, 0] = piece
        for mask in (2, 4, 6):
            v[name, mask] = ring.swap(piece, mask)

    def gathered(name):
        v[name] = cat([v[name, mask] for mask in (0, 2, 4, 6)])
        v[name, 1] = ring.swap(v[name], 1)

    close_with(["d", "c"], "gin", "f2")
    folded(["d", "c"], "gin")
    close_with(["d"], "gin")
    folded(["d"], "gin")
    close_with(["d"], "gin", "f3")
    folded(["d"], "gin")
    packed = pack(((3, 0), (0, 0), (1, 0), (2, 0)), [*red["c"].out, *red["d"].out], red["d"].small)
    for s in shifts:
        v["a", s] = ring.push(packed[s], s)
    spread("f", total_of([red["a"].out[0], v["f1"], v["f2"], v["f3"]]))
    close(*[("a", s) for s in shifts], "gin")
    a_total, table, gains = unpack([packed[0]] + [v["a", s] for s in shifts])
    spread("a", a_total)
    close(("f", 2), ("f", 4), ("f", 6), "gin")
    gathered("f")
    close(("f", 1), "gin")
    v["in"], v["down"] = finish(ids, masks, [v["f"], v["f", 1]], 2, depth)
    v["table"] = table[0, : heads * TILE].reshape(heads, TILE)[:, :buckets].T
    v["gain_attn"], v["gain_ffn"] = gains[n_mp], gains[n_mp + 1]
    close("in", "down", "table", "gain_attn", "gain_ffn", ("a", 2), ("a", 4), ("a", 6), "gin")
    gathered("a")
    grad_in, grad_down, grad_inputs = v["in"], v["down"], v["gin"]
    grads = finish(ids, masks, [v["a"], v["a", 1]], 4, width)
    grad_out, grad_query, grad_key, grad_value = grads[0], grads[1].T, grads[2].T, grads[3].T

    return (
        outputs, grad_inputs, grad_query, grad_key, grad_value, grad_out, v["table"],
        v["gain_attn"], v["gain_ffn"], grad_in, grad_down,
    )


def solution(mesh):
    placed = (
        P(("dp", "mp"), None), P(), P(None, "mp"), P(None, "mp"), P(None, "mp"), P("mp", None),
        P(None, "mp"), P(), P(None, "mp"), P("mp", None), P(("dp", "mp"), None), P("dp"), P("dp", None),
    )
    return jax.shard_map(
        functools.partial(body, mesh.shape["dp"], mesh.shape["mp"]),
        mesh=mesh,
        in_specs=placed,
        out_specs=(
            P(("dp", "mp"), None), P(("dp", "mp"), None), P(None, "mp"), P(None, "mp"), P(None, "mp"),
            P("mp", None), P(None, "mp"), P(), P(), P(None, "mp"), P("mp", None),
        ),
        check_vma=False,
    )
```

```python
import functools

import jax
import jax.numpy as jnp
import numpy as np
from jax import lax
from jax.experimental import pallas as pl
from jax.experimental.pallas import tpu as pltpu
from jax.sharding import PartitionSpec as P

BIG = 512
HEAD = 64
EPS = 1e-06
THRESHOLDS = (12, 16, 23, 32, 46, 64, 91)
MASKED = -1e30
TILE = 128
SPAN = 512
EXTRA = 16
BF = jnp.bfloat16
F32 = jnp.float32
MIB = 1024 * 1024
LIMIT = 56
SMEM = pl.BlockSpec(memory_space=pltpu.SMEM)
VMEM = pl.BlockSpec(memory_space=pltpu.VMEM)
ANY = pl.BlockSpec(memory_space=pl.ANY)


def offset_one_hot(buckets):
    offsets = np.arange(SPAN) - SPAN // 2
    distance = np.abs(offsets)
    far = 8 + sum((distance >= t).astype(np.int32) for t in THRESHOLDS)
    bucket = np.where(distance < 8, distance, far) + np.where(offsets > 0, buckets // 2, 0)
    return (np.arange(TILE)[:, None] == bucket[None, :]).astype(np.float32)


def dot_nn(a, b):
    return lax.dot_general(a, b, (((1,), (0,)), ((), ())), preferred_element_type=F32)


def dot_nt(a, b):
    return lax.dot_general(a, b, (((1,), (1,)), ((), ())), preferred_element_type=F32)


def dot_tn(a, b):
    return lax.dot_general(a, b, (((0,), (0,)), ((), ())), preferred_element_type=F32)


def like(shape, dtype):
    return jax.ShapeDtypeStruct(shape, dtype)


def params(mib):
    return pltpu.CompilerParams(vmem_limit_bytes=mib * MIB)


def cost(micros):
    return pl.CostEstimate(flops=micros * 10**9, bytes_accessed=micros * 10**6, transcendentals=0)


def mask_rows(ids_ref, slots):
    bucket = ids_ref[1]
    half = BIG // 2
    segs, starts = [], []
    for part in range(2):
        first = ids_ref[2] + part * half
        seg = jnp.int32(0)
        for j in range(1, slots):
            seg = seg + jnp.where(first >= j * bucket, 1, 0).astype(jnp.int32)
        segs.append(seg)
        starts.append(first - seg * bucket)
    iota = lax.broadcasted_iota(jnp.int32, (1, half), 1)
    rows = []
    for query_part in range(2):
        cols = []
        for key_part in range(2):
            same = segs[query_part] == segs[key_part]
            limit = jnp.where(same, ids_ref[3 + segs[key_part]] - starts[key_part], 0)
            cols.append(jnp.where(iota < limit, 0.0, MASKED).astype(F32))
        rows.append(jnp.concatenate(cols, axis=1))
    return rows


def bias_band(rel_row):
    return pltpu.roll(jnp.broadcast_to(rel_row, (TILE, SPAN)), 0, 1, stride=1, stride_axis=0)


def masked_bias(i, near, rel_row, mask):
    tiles = []
    for j in range(BIG // TILE):
        keys = mask[:, j * TILE : (j + 1) * TILE]
        if abs(j - i) <= 1:
            tiles.append(near[:, (j - i + 2) * TILE : (j - i + 3) * TILE] + keys)
        else:
            far = rel_row[:, SPAN - 1 :] if j > i else rel_row[:, :1]
            tiles.append(jnp.broadcast_to(far + keys, (TILE, TILE)))
    return jnp.concatenate(tiles, axis=1)


def row_block(low, bits):
    return ((low & 1) << (bits - 1)) | (low >> 1)


def side_of(ids_ref, bit):
    return (ids_ref[0] >> bit) & 1


def block_rows(ids_ref, mask, bits, rows):
    return pl.ds(pl.multiple_of(row_block(ids_ref[0] ^ mask, bits) * rows, rows), rows)


class Mover:
    def __init__(self, sems):
        self.sems, self.used, self.out = sems, 0, []

    def copy(self, source, target):
        one = pltpu.make_async_copy(source, target, self.sems.at[self.used])
        self.used += 1
        one.start()
        return one

    def load(self, source, target):
        return [self.copy(source, target)]

    def blocks(self, ids_ref, masks, part_refs, mat, which):
        copies, j, first = [], 0, 0
        for part in part_refs:
            if masks is None:
                copies.append(self.copy(part, mat.at[pl.ds(first, part.shape[0])]))
                first += part.shape[0]
                continue
            bits = (len(masks) - 1).bit_length()
            for e in range(part.shape[0]):
                copies.append(self.copy(part.at[e, which], mat.at[block_rows(ids_ref, masks[j], bits, part.shape[2])]))
                j += 1
        return copies

    def store(self, source, target):
        self.out.append(self.copy(source, target))

    def halves(self, ids_ref, source, send, keep):
        size = source.shape[0] // 2
        for ref, side in ((send, 1 - side_of(ids_ref, 0)), (keep, side_of(ids_ref, 0))):
            self.store(source.at[pl.ds(pl.multiple_of(side * size, size), size)], ref)

    def finish(self):
        wait(self.out)


def wait(copies):
    for one in copies:
        one.wait()


def put_blocks(ids_ref, masks, part_refs, mat, which):
    j, bits = 0, (len(masks) - 1).bit_length()
    for part in part_refs:
        for e in range(part.shape[0]):
            mat[block_rows(ids_ref, masks[j], bits, part.shape[2]), :] = part[e, which].astype(mat.dtype)
            j += 1


def rms(values):
    root = lax.rsqrt(jnp.mean(values * values, axis=1, keepdims=True) + EPS)
    return values * root, root


def rms_back(grad, unit, root, gain):
    scaled = grad * gain
    centred = scaled - unit * jnp.mean(scaled * unit, axis=1, keepdims=True)
    return root * centred, jnp.sum(grad * unit, axis=0, keepdims=True)


def head_slices(qkv_ref, heads, h):
    width = heads * HEAD
    return [qkv_ref[:, j * width + h * HEAD : j * width + (h + 1) * HEAD] for j in (1, 2, 3)]


def forward_scores(h, band, rel, masks, scores, lse_ref):
    probs = []
    for i in range(BIG // TILE):
        rows = slice(i * TILE, (i + 1) * TILE)
        s = scores[h, rows, :] + masked_bias(i, band[h], rel[h : h + 1], masks[i // 2])
        top = jnp.max(s, axis=1, keepdims=True)
        e = jnp.exp(s - top)
        total = jnp.sum(e, axis=1, keepdims=True)
        probs.append((e * (1.0 / total)).astype(BF))
        lse_ref[rows, h : h + 1] = top + jnp.log(total)
    return jnp.concatenate(probs, axis=0)


def attn_fwd_kernel(slots, heads, parts, masks, start, shards, last, ids_ref, *refs):
    refs = list(refs)
    take = lambda n: [refs.pop(0) for _ in range(n)]
    n1_hbm = take(1)[0]
    a_parts = take(parts)
    tab_hbm, hot_hbm, prior_hbm = take(3)
    gain_hbm = take(1)[0] if last else None
    qkv_out, o_out, lse_out, hid_out = take(4)
    n2_out = take(1)[0] if last else None
    n1_ref, mat, tab_ref, hot_ref, prior_ref, gain_ref, qkv_ref, o_ref, lse_ref, hid_ref, n2_ref, band, scores, sems = refs
    move = Mover(sems)
    width = heads * HEAD
    half = BIG // 2
    got_mat = [move.blocks(ids_ref, masks, a_parts, mat.at[0], start)]
    got_n1 = move.load(n1_hbm, n1_ref)
    got_tab = move.load(tab_hbm.at[pl.ds(start, shards)], tab_ref) + move.load(hot_hbm, hot_ref)
    allowed = mask_rows(ids_ref, slots)
    wait(got_tab)
    wait(got_n1)
    for s in range(shards):
        rel = dot_nn(tab_ref[s], hot_ref[...])
        for h in range(heads):
            band[h] = bias_band(rel[h : h + 1])
        wait(got_mat[s])
        if s == 0:
            got_mat += [move.blocks(ids_ref, masks, a_parts, mat.at[t], start + t) for t in range(1, shards)]
            got_prior = move.load(prior_hbm, prior_ref)
            if last:
                got_prior += move.load(gain_hbm, gain_ref)
        qkv_ref[s] = dot_nt(n1_ref[...], mat[s]).astype(BF)
        move.store(qkv_ref.at[s], qkv_out.at[s])
        for h in range(heads):
            q, k, _ = head_slices(qkv_ref.at[s], heads, h)
            scores[h] = dot_nt(q, k)
        for h in range(heads):
            v = head_slices(qkv_ref.at[s], heads, h)[2]
            pb = forward_scores(h, band, rel, allowed, scores, lse_ref.at[s])
            o_ref[s, :, h * HEAD : (h + 1) * HEAD] = dot_nn(pb, v).astype(BF)
        move.store(o_ref.at[s], o_out.at[s])
        move.store(lse_ref.at[s], lse_out.at[s])
        if s == 0:
            wait(got_prior)
        pieces = 2 if s == shards - 1 else 1
        size = BIG // pieces
        for part in range(pieces):
            rows = pl.ds(part * size, size)
            before = prior_ref[rows, :].astype(F32) if s == 0 else hid_ref[rows, :]
            hidden = before + dot_nn(o_ref[s, rows, :], mat[s, :width, :])
            hid_ref[rows, :] = hidden
            if s == shards - 1:
                move.store(hid_ref.at[rows], hid_out.at[rows])
                if last:
                    n2_ref[rows, :] = (rms(hidden)[0] * gain_ref[...].astype(F32)).astype(BF)
                    move.store(n2_ref.at[rows], n2_out.at[rows])
    move.finish()


HBM = pl.BlockSpec(memory_space=pltpu.HBM)


def attn_fwd(ids, masks, n1, a_parts, start, shards, tab, hot, prior, gain, slots, heads):
    last = gain is not None
    rows, depth = n1.shape
    width = heads * HEAD
    cols = 4 * width
    args = [n1, *a_parts, tab, hot, prior] + ([gain] if last else [])
    out_shape = [
        like((shards, rows, cols), BF),
        like((shards, rows, width), BF),
        like((shards, rows, TILE), F32),
        like((rows, depth), F32),
    ]
    if last:
        out_shape.append(like((rows, depth), BF))
    return pl.pallas_call(
        functools.partial(attn_fwd_kernel, slots, heads, len(a_parts), masks, start, shards, last),
        in_specs=[SMEM] + [ANY] * len(args),
        out_specs=[HBM] * len(out_shape),
        out_shape=out_shape,
        scratch_shapes=[
            pltpu.VMEM((rows, depth), BF),
            pltpu.VMEM((shards, cols, depth), BF),
            pltpu.VMEM((shards,) + tab.shape[1:], BF),
            pltpu.VMEM(hot.shape, BF),
            pltpu.VMEM(prior.shape, prior.dtype),
            pltpu.VMEM((1, depth), BF),
            pltpu.VMEM((shards, rows, cols), BF),
            pltpu.VMEM((shards, rows, width), BF),
            pltpu.VMEM((shards, rows, TILE), F32),
            pltpu.VMEM((rows, depth), F32),
            pltpu.VMEM((rows, depth), BF),
            pltpu.VMEM((heads, TILE, SPAN), F32),
            pltpu.VMEM((heads, BIG, BIG), F32),
            pltpu.SemaphoreType.DMA((12 + 12 * shards,)),
        ],
        compiler_params=params(LIMIT),
        cost_estimate=cost(16 * shards),
        name="attn_fwd",
    )(ids, *args)


def attn_bwd_kernel(slots, heads, masks, shards, rest, sources, own, first, befores, ids_ref, *refs):
    refs = list(refs)
    take = lambda n: [refs.pop(0) for _ in range(n)]
    last = None in shards
    count = len(shards)
    n1_hbm, gh_hbm, hot_hbm = take(3)
    rest_parts = take(rest)
    rest_tab = take(1)[0]
    rest_kept, rest_at = {}, {}
    for places in sources:
        kept = take(3) + [rest_tab]
        for base, which in enumerate(places):
            rest_kept[which], rest_at[which] = kept, base
    own_parts, own_kept = (take(own), take(4)) if last else ([], [])
    prior_hbm = None if first else take(1)[0]
    if last:
        x_hbm, gain_hbm, ghid_hbm, gain2_hbm = take(4)
        tabs_hbm = take(befores)
        send_out, keep_out, gin_out = take(3)
    else:
        send_out, keep_out, gn_out, tabs_out = take(4)
    n1_ref, gh_ref, hot_ref, mat, qkv_ref, o_ref, lse_ref, tab_ref, gn_ref = take(9)
    band, acc, gs_all, pb_all, gq_all, grads_mat, tabs_ref, sems = take(8)
    move = Mover(sems)
    width = heads * HEAD
    half = BIG // 2
    if last:
        x_ref, gain_ref, ghid_ref, gain2_ref, before_ref, small, packed = take(7)

    def load(c):
        which = shards[c]
        parts, kept = (own_parts, own_kept) if which is None else (rest_parts, rest_kept[which])
        at = 0 if which is None else which
        base = 0 if which is None else rest_at[which]
        got_tab = move.load(kept[3].at[at], tab_ref.at[c])
        got_mat = move.blocks(ids_ref, None if which is None else masks, parts, mat.at[c], at)
        got_kept = move.load(kept[0].at[base], qkv_ref.at[c]) + move.load(kept[2].at[base], lse_ref.at[c])
        return got_tab, got_mat, got_kept, move.load(kept[1].at[base], o_ref.at[c])

    got_first = move.load(hot_hbm, hot_ref) + move.load(gh_hbm, gh_ref)
    got = [load(0)]
    got_n1 = move.load(n1_hbm, n1_ref)
    allowed = mask_rows(ids_ref, slots)
    lane = lax.broadcasted_iota(jnp.int32, (1, SPAN), 1)
    wait(got_first)
    gh = gh_ref[...]
    for c in range(count):
        got_tab, got_mat, got_kept, got_late = got[c]
        acc[...] = jnp.zeros(acc.shape, F32)
        gq_all[c, :, :width] = jnp.zeros((gq_all.shape[1], width), BF)
        wait(got_tab)
        rel = dot_nn(tab_ref[c], hot_ref[...])
        for h in range(heads):
            band[h] = bias_band(rel[h : h + 1])
        wait(got_mat)
        go_all = dot_nt(gh, mat[c, :width, :]).astype(BF)
        wait(got_kept)
        if c == 0:
            got += [load(t) for t in range(1, count)]
            got_prior = [] if first else move.load(prior_hbm, gn_ref)
            if last:
                got_prior += move.load(x_hbm, x_ref) + move.load(gain_hbm, gain_ref)
                got_prior += move.load(ghid_hbm, ghid_ref) + move.load(gain2_hbm, gain2_ref)
                done = 0
                for ref in tabs_hbm:
                    got_prior += move.load(ref, before_ref.at[pl.ds(done, ref.shape[0])])
                    done += ref.shape[0]
        far = []
        for h in range(heads):
            q, k, v = head_slices(qkv_ref.at[c], heads, h)
            go = go_all[:, h * HEAD : (h + 1) * HEAD]
            low = jnp.zeros((1, TILE), F32)
            high = jnp.zeros((1, TILE), F32)
            for i in range(BIG // TILE):
                rows = slice(i * TILE, (i + 1) * TILE)
                s = dot_nt(q[rows], k) + masked_bias(i, band[h], rel[h : h + 1], allowed[i // 2])
                p = jnp.exp(s - lse_ref[c, rows, h : h + 1])
                dp = dot_nt(go[rows], v)
                inner = jnp.sum(p * dp, axis=1, keepdims=True)
                gs = (p * (dp - inner)).astype(BF)
                gs_all[h, rows, :] = gs
                pb_all[h, rows, :] = p.astype(BF)
                wide = gs.astype(F32)
                for j in range(BIG // TILE):
                    tile = wide[:, j * TILE : (j + 1) * TILE]
                    if abs(j - i) <= 1:
                        acc[h, :, (j - i + 2) * TILE : (j - i + 3) * TILE] += tile
                    elif j > i:
                        high = high + jnp.sum(tile, axis=0, keepdims=True)
                    else:
                        low = low + jnp.sum(tile, axis=0, keepdims=True)
            at = lambda j: slice(j * width + h * HEAD, j * width + (h + 1) * HEAD)
            gq_all[c, :, at(1)] = dot_nn(gs_all[h], k).astype(BF)
            gq_all[c, :, at(2)] = dot_tn(gs_all[h], q).astype(BF)
            gq_all[c, :, at(3)] = dot_tn(pb_all[h], go).astype(BF)
            far.append((low, high))
        wait(got_late)
        if c == 0:
            wait(got_n1)
        grads_mat[c] = dot_tn(gq_all[c], n1_ref[...]).astype(BF)
        grads_mat[c, :width, :] = dot_tn(o_ref[c], gh).astype(BF)
        size = pl.ds(0, grads_mat.shape[1] // 2)
        move.halves(ids_ref, grads_mat.at[c], send_out.at[c, size], keep_out.at[c, size])
        near = acc[...]
        n = TILE // 2
        while n >= 8:
            near = near[:, :n] + pltpu.roll(near[:, n:], SPAN - n, 2)
            n //= 2
        line = near[:, 0:1]
        for j in range(1, 8):
            line = line + pltpu.roll(near[:, j : j + 1], SPAN - j, 2)
        lines = []
        for h, (low, high) in enumerate(far):
            ends = jnp.where(lane == 0, jnp.sum(low, axis=1, keepdims=True), 0.0)
            ends = ends + jnp.where(lane == SPAN - 1, jnp.sum(high, axis=1, keepdims=True), 0.0)
            lines.append(line[h] + ends)
        lines = jnp.concatenate(lines + [jnp.zeros((8 - heads, SPAN), F32)], axis=0)
        tabs_ref[c] = lax.dot_general(
            lines, hot_ref[...].astype(F32), (((1,), (1,)), ((), ())),
            precision=lax.Precision.HIGHEST, preferred_element_type=F32,
        )
        if c == 0:
            wait(got_prior)
        pieces = 2 if c == count - 1 and not last else 1
        size = BIG // pieces
        for part in range(pieces):
            rows = pl.ds(part * size, size)
            gn = dot_nn(gq_all[c, rows, :], mat[c])
            if not (first and c == 0):
                gn = gn + gn_ref[rows, :]
            gn_ref[rows, :] = gn
            if c == count - 1 and not last:
                move.store(gn_ref.at[rows], gn_out.at[rows])
    if not last:
        move.store(tabs_ref, tabs_out)
        move.finish()
        return
    unit, root = rms(x_ref[...].astype(F32))
    back, gain_grad = rms_back(gn_ref[...], unit, root, gain_ref[...].astype(F32))
    small[...] = jnp.zeros_like(small)
    total = before_ref.shape[0] + count
    tables = [tabs_ref[count - 1]] + [before_ref[j] for j in range(total - count)]
    tables += [tabs_ref[c] for c in range(count - 1)]
    for row, value in enumerate(tables):
        for h in range(heads):
            small[row : row + 1, h * TILE : (h + 1) * TILE] = value[h : h + 1]
    small[total : total + 1, :] = gain_grad
    small[total + 1 : total + 2, :] = gain2_ref[0:1, :]
    packed[...] = split_small(small[...])
    tail = pl.ds(grads_mat.shape[1] // 2, EXTRA)
    for c in range(count):
        move.store(packed, send_out.at[c, tail])
        move.store(packed, keep_out.at[c, tail])
    gh_ref[...] = (ghid_ref[...] + back).astype(BF)
    move.store(gh_ref, gin_out)
    move.finish()


def split_small(value):
    high = value.astype(BF)
    low = (value - high.astype(F32)).astype(BF)
    return jnp.concatenate([high.astype(F32), low.astype(F32)], axis=0).astype(BF)


def join_small(packed):
    wide = packed.astype(F32)
    return wide[: EXTRA // 2] + wide[EXTRA // 2 :]


def attn_bwd(ids, masks, n1, gh, hot, shards, rest, own, prior, final, slots, heads):
    last, first = None in shards, prior is None
    count = len(shards)
    rows, depth = n1.shape
    width = heads * HEAD
    cols = 4 * width
    parts, tab, sources = rest
    sources = [(places, kept) for places, kept in sources if set(places) & set(shards)]
    args = [n1, gh, hot, *parts, tab] + [k for _, kept in sources for k in kept]
    args += [*own[0], *own[1]] if last else []
    args += ([] if first else [prior]) + (list(final) if last else [])
    befores = len(final) - 4 if last else 0
    half = like((count, cols // 2 + (EXTRA if last else 0), depth), BF)
    if last:
        out_shape = [half, half, like((rows, depth), BF)]
    else:
        out_shape = [half, half, like((rows, depth), F32), like((count, 8, TILE), F32)]
    scratch = [
        pltpu.VMEM((rows, depth), BF),
        pltpu.VMEM((rows, depth), BF),
        pltpu.VMEM(hot.shape, BF),
        pltpu.VMEM((count, cols, depth), BF),
        pltpu.VMEM((count, rows, cols), BF),
        pltpu.VMEM((count, rows, width), BF),
        pltpu.VMEM((count, rows, TILE), F32),
        pltpu.VMEM((count,) + tab.shape[1:], BF),
        pltpu.VMEM((rows, depth), F32),
        pltpu.VMEM((heads, TILE, SPAN), F32),
        pltpu.VMEM((heads, TILE, SPAN), F32),
        pltpu.VMEM((heads, BIG, BIG), BF),
        pltpu.VMEM((heads, BIG, BIG), BF),
        pltpu.VMEM((count, rows, cols), BF),
        pltpu.VMEM((count, cols, depth), BF),
        pltpu.VMEM((count, 8, TILE), F32),
        pltpu.SemaphoreType.DMA((16 + 18 * count,)),
    ]
    if last:
        scratch += [
            pltpu.VMEM((rows, depth), BF),
            pltpu.VMEM((1, depth), BF),
            pltpu.VMEM((rows, depth), F32),
            pltpu.VMEM((8, depth), F32),
            pltpu.VMEM((sum(f.shape[0] for f in final[4:]), 8, TILE), F32),
            pltpu.VMEM((8, depth), F32),
            pltpu.VMEM((EXTRA, depth), BF),
        ]
    return pl.pallas_call(
        functools.partial(
            attn_bwd_kernel, slots, heads, masks, tuple(shards), len(parts), tuple(p for p, _ in sources),
            len(own[0]) if last else 0, first, befores,
        ),
        in_specs=[SMEM] + [ANY] * len(args),
        out_specs=[HBM] * len(out_shape),
        out_shape=out_shape,
        scratch_shapes=scratch,
        compiler_params=params(LIMIT),
        cost_estimate=cost(32 * count),
        name="attn_bwd",
    )(ids, *args)


def ffn_kernel(parts, masks, first, last, ids_ref, *refs):
    refs = list(refs)
    take = lambda n: [refs.pop(0) for _ in range(n)]
    count = len(parts)
    n2_hbm, cot_hbm = take(2)
    f_parts = [take(n or 2) for n in parts]
    out_in, gn_in = (None, None) if first else take(2)
    if last:
        hid_in, gain_in = take(2)
        out_out, send_out, keep_out, ghid_out, gh_out, gg_out = take(6)
    else:
        out_out, gn_out, send_out, keep_out = take(4)
    n2_ref, cot_ref, i_mat, w_mat, act_ref, gp_ref, gi_mat, gw_mat, out_ref, gn_ref, sems = take(11)
    move = Mover(sems)
    hid_ref, gain_ref, y_ref, gg_ref = take(4) if last else [None] * 4

    def load(c):
        if not parts[c]:
            return move.load(f_parts[c][0], i_mat.at[c]), move.load(f_parts[c][1], w_mat.at[c])
        return tuple(move.blocks(ids_ref, masks[c], f_parts[c], mat.at[c], j) for j, mat in enumerate((i_mat, w_mat)))

    got_n2 = move.load(n2_hbm, n2_ref)
    got = [load(0)]
    got_cot = move.load(cot_hbm, cot_ref)
    c0 = 0.7978845608028654
    c1 = 0.044715
    size = n2_ref.shape[0] // 2
    gain_grad = None
    for c in range(count):
        wait(got[c][0])
        if c == 0:
            wait(got_n2)
            got += [load(t) for t in range(1, count)]
            got_sums = [] if first else move.load(out_in, out_ref) + move.load(gn_in, gn_ref)
            if last:
                got_sums += move.load(hid_in, hid_ref) + move.load(gain_in, gain_ref)
        pre = dot_nn(n2_ref[...], i_mat[c])
        square = pre * pre
        th = jnp.tanh(pre * (c0 + (c0 * c1) * square))
        half = 0.5 * (1.0 + th)
        act_ref[c] = (pre * half).astype(BF)
        slope = half + (0.5 * pre) * (1.0 - th * th) * (c0 + (3.0 * c0 * c1) * square)
        wait(got[c][1])
        if c == 0:
            wait(got_cot)
        cot = cot_ref[...]
        gp_ref[c] = (dot_nt(cot, w_mat[c]) * slope).astype(BF)
        gw_mat[c] = dot_tn(act_ref[c], cot).astype(BF)
        move.halves(ids_ref, gw_mat.at[c], send_out.at[2 * c + 1], keep_out.at[2 * c + 1])
        gi_mat[c] = dot_tn(n2_ref[...], gp_ref[c]).astype(BF)
        move.halves(ids_ref, gi_mat.at[c], send_out.at[2 * c], keep_out.at[2 * c])
        if c == 0:
            wait(got_sums)
        ending = c == count - 1
        pieces = 2 if ending else 1
        size = n2_ref.shape[0] // pieces
        for part in range(pieces):
            rows = pl.ds(part * size, size)
            gn = dot_nt(gp_ref[c, rows, :], i_mat[c])
            out = dot_nn(act_ref[c, rows, :], w_mat[c])
            if not (first and c == 0):
                out = out + out_ref[rows, :]
                gn = gn + gn_ref[rows, :]
            if not (last and ending):
                gn_ref[rows, :] = gn
                out_ref[rows, :] = out
                if ending:
                    move.store(gn_ref.at[rows], gn_out.at[rows])
                    move.store(out_ref.at[rows], out_out.at[rows])
                continue
            hidden = hid_ref[rows, :]
            y_ref[rows, :] = (hidden + out).astype(BF)
            move.store(y_ref.at[rows], out_out.at[rows])
            unit, root = rms(hidden)
            back, gain_part = rms_back(gn, unit, root, gain_ref[...].astype(F32))
            gain_grad = gain_part if gain_grad is None else gain_grad + gain_part
            grad_hidden = cot_ref[rows, :].astype(F32) + back
            gn_ref[rows, :] = grad_hidden
            move.store(gn_ref.at[rows], ghid_out.at[rows])
            n2_ref[rows, :] = grad_hidden.astype(BF)
            move.store(n2_ref.at[rows], gh_out.at[rows])
    if last:
        gg_ref[...] = jnp.broadcast_to(gain_grad, gg_ref.shape)
        move.store(gg_ref, gg_out)
    move.finish()


def ffn(ids, n2, cot, shards, sums, final):
    first, last = sums is None, final is not None
    rows, depth = n2.shape
    count = len(shards)
    units = shards[-1][1][0].shape[-1]
    half = like((2 * count, depth // 2, units), BF)
    total = like((rows, depth), F32)
    args = [n2, cot] + [p for _, ps in shards for p in ps]
    args += ([] if first else list(sums)) + ([] if not last else list(final))
    if last:
        out_shape = [like((rows, depth), BF), half, half, total, like((rows, depth), BF), like((8, depth), F32)]
    else:
        out_shape = [total, total, half, half]
    scratch = [
        pltpu.VMEM((rows, depth), BF),
        pltpu.VMEM((rows, depth), BF),
        pltpu.VMEM((count, depth, units), BF),
        pltpu.VMEM((count, units, depth), BF),
        pltpu.VMEM((count, rows, units), BF),
        pltpu.VMEM((count, rows, units), BF),
        pltpu.VMEM((count, depth, units), BF),
        pltpu.VMEM((count, units, depth), BF),
        pltpu.VMEM((rows, depth), F32),
        pltpu.VMEM((rows, depth), F32),
        pltpu.SemaphoreType.DMA((20 + 20 * count,)),
    ]
    if last:
        scratch += [
            pltpu.VMEM((rows, depth), F32),
            pltpu.VMEM((1, depth), BF),
            pltpu.VMEM((rows, depth), BF),
            pltpu.VMEM((8, depth), F32),
        ]
    return pl.pallas_call(
        functools.partial(
            ffn_kernel, tuple(0 if m is None else len(p) for m, p in shards), [m for m, _ in shards], first, last
        ),
        in_specs=[SMEM] + [ANY] * len(args),
        out_specs=[HBM] * len(out_shape),
        out_shape=out_shape,
        scratch_shapes=scratch,
        compiler_params=params(LIMIT),
        cost_estimate=cost(32 * count),
        name="ffn",
    )(ids, *args)


def prep_kernel(rows, bits, count, *refs):
    mats, (tab_ref, a_ref, wide_ref, sem) = refs[:count], refs[count:]
    block = row_block(lax.axis_index("dp") & ((1 << bits) - 1), bits)
    per = mats[0].shape[0] // rows

    def piece(j, mat):
        at = pl.ds(pl.multiple_of((block - j * per) * rows, rows), rows)
        return pltpu.make_async_copy(mat.at[at], a_ref.at[pl.ds(0, rows)], sem)

    for j, mat in enumerate(mats):
        @pl.when(block // per == j)
        def _():
            piece(j, mat).start()

    tab = tab_ref[...].astype(F32)
    heads, buckets = tab.shape
    tab = jnp.concatenate([tab, jnp.zeros((heads, TILE - buckets), F32)], axis=1)
    tab = jnp.concatenate([tab, jnp.zeros((EXTRA - heads, TILE), F32)], axis=0).astype(BF)
    wide_ref[0] = tab
    a_ref[rows:, :] = jnp.zeros((EXTRA, a_ref.shape[1]), BF)
    a_ref[rows:, :TILE] = tab
    for j, mat in enumerate(mats):
        @pl.when(block // per == j)
        def _():
            piece(j, mat).wait()


def prep(mats, tab, depth, rows, bits):
    return pl.pallas_call(
        functools.partial(prep_kernel, rows, bits, len(mats)),
        in_specs=[ANY] * len(mats) + [VMEM],
        out_specs=[VMEM, VMEM],
        out_shape=[like((rows + EXTRA, depth), BF), like((1, EXTRA, TILE), BF)],
        scratch_shapes=[pltpu.SemaphoreType.DMA],
        compiler_params=params(60),
        cost_estimate=cost(0),
        name="prep",
    )(*mats, tab)


def prep_ffn_kernel(rows, bits, in_ref, down_ref, f_ref, sems):
    block = row_block(lax.axis_index("dp") & ((1 << bits) - 1), bits)
    first = pl.ds(pl.multiple_of(block * rows, rows), rows)
    copies = [
        pltpu.make_async_copy(in_ref.at[first], f_ref.at[0], sems.at[0]),
        pltpu.make_async_copy(down_ref.at[first], f_ref.at[1], sems.at[1]),
    ]
    for copy in copies:
        copy.start()
    for copy in copies:
        copy.wait()


def prep_ffn(w_in, w_down, rows, bits):
    return pl.pallas_call(
        functools.partial(prep_ffn_kernel, rows, bits),
        in_specs=[ANY, ANY],
        out_specs=VMEM,
        out_shape=like((2, rows, w_in.shape[1]), BF),
        scratch_shapes=[pltpu.SemaphoreType.DMA((2,))],
        compiler_params=params(60),
        cost_estimate=cost(0),
        name="prep_ffn",
    )(w_in, w_down)


def join_kernel(count, *refs):
    parts, (a_ref, tab_ref) = refs[:count], refs[count:]
    rows = a_ref.shape[1]
    for j, part in enumerate(parts):
        a_ref[j] = part[:rows, :]
        tab_ref[j] = part[rows:, :TILE]


def join(parts):
    rows, depth = parts[0].shape
    return pl.pallas_call(
        functools.partial(join_kernel, len(parts)),
        in_specs=[VMEM] * len(parts),
        out_specs=[VMEM, VMEM],
        out_shape=[like((len(parts), rows - EXTRA, depth), BF), like((len(parts), EXTRA, TILE), BF)],
        compiler_params=params(16),
        cost_estimate=cost(0),
        name="join",
    )(*parts)


def row_runs(left, bit, rows):
    inner = rows
    for b in left[left.index(bit) + 1 :]:
        inner *= 2
    outer = 1
    for b in left[: left.index(bit)]:
        outer *= 2
    return [(o * 2 * inner, inner, o * inner) for o in range(outer)]


def fold_kernel(runs, extra, joined, split, ids_ref, *refs):
    if joined:
        keep_ref, recv_ref = refs[:2]
        n = keep_ref.shape[0] // 2
        ins = [(keep_ref.at[pl.ds(g * n, n)], recv_ref.at[pl.ds(g * n, n)]) for g in range(2)]
        outs = refs[2:]
    else:
        ins, outs = [refs[0:2], refs[2:4]], refs[4:]
    packed = None
    if extra:
        keep, recv = ins[1]
        tail = pl.ds(keep.shape[1] - extra, extra)
        packed = split_small(join_small(keep[0, tail, :]) + join_small(recv[0, tail, :]))
    for g, (keep, recv) in enumerate(ins):
        def total(rows):
            return (keep[:, rows, :].astype(F32) + recv[:, rows, :].astype(F32)).astype(BF)

        if runs is None:
            value, done = total(pl.ds(0, outs[0].shape[1])), 0
            for ref in outs[: split[0]] if g == 0 else outs[split[0] : split[0] + split[1]]:
                ref[...] = value[done : done + ref.shape[0]]
                done += ref.shape[0]
            continue
        bit, group_runs = runs[g]
        mine = side_of(ids_ref, bit)
        for ref, side in ((outs[2 * g], 1 - mine), (outs[2 * g + 1], mine)):
            for source, length, target in group_runs:
                ref[:, target : target + length, :] = total(pl.ds(pl.multiple_of(source + side * length, length), length))
            if extra and g == 1:
                done = sum(length for _, length, _ in group_runs)
                for m in range(ref.shape[0]):
                    ref[m, done:, :] = packed
    if extra and runs is None:
        outs[-1][...] = packed


def fold(ids, groups, runs, extra, split=(1, 1)):
    joined = len(groups) == 1
    arrays = [a for group in groups for a in group]
    if joined:
        count = arrays[0].shape[0] // 2
        bodies = [arrays[0].shape[1] - extra] * 2
    else:
        count = arrays[0].shape[0]
        bodies = [arrays[0].shape[1], arrays[2].shape[1] - extra]
    cols = arrays[0].shape[2]
    if runs is None:
        out_shape = [like((count // n, bodies[0], cols), BF) for n in split for _ in range(n)]
        out_shape += [like((extra, cols), BF)] if extra else []
    else:
        tails = (0, extra)
        out_shape = [like((count, bodies[g] // 2 + tails[g], cols), BF) for g in (0, 0, 1, 1)]
    return pl.pallas_call(
        functools.partial(fold_kernel, runs, extra, joined, split),
        in_specs=[SMEM] + [VMEM] * len(arrays),
        out_specs=[VMEM] * len(out_shape),
        out_shape=out_shape,
        compiler_params=params(24),
        cost_estimate=cost(0),
        name="fold",
    )(ids, *arrays)


def add_kernel(a_ref, b_ref, out_ref):
    out_ref[...] = (a_ref[...].astype(F32) + b_ref[...].astype(F32)).astype(BF)


def add(a, b):
    return pl.pallas_call(
        add_kernel, in_specs=[VMEM, VMEM], out_specs=VMEM, out_shape=like(a.shape, BF),
        compiler_params=params(16), cost_estimate=cost(0), name="add",
    )(a, b)


def add_small_kernel(a_ref, b_ref, out_ref):
    out_ref[...] = split_small(join_small(a_ref[...]) + join_small(b_ref[...]))


def add_small(a, b):
    return pl.pallas_call(
        add_small_kernel, in_specs=[VMEM, VMEM], out_specs=VMEM, out_shape=like(a.shape, BF),
        compiler_params=params(16), cost_estimate=cost(0), name="add_small",
    )(a, b)


def total_kernel(*refs):
    total = refs[0][...].astype(F32)
    for ref in refs[1:-1]:
        total = total + ref[...].astype(F32)
    refs[-1][...] = total.astype(BF)


def total_of(parts):
    return pl.pallas_call(
        total_kernel, in_specs=[VMEM] * len(parts), out_specs=VMEM, out_shape=like(parts[0].shape, BF),
        compiler_params=params(16), cost_estimate=cost(0), name="total",
    )(*parts)


def pack_kernel(places, count, *refs):
    parts, small_ref, outs = refs[:count], refs[count], refs[count + 1 :]
    for (j, m), ref in zip(places, outs):
        rows = parts[j].shape[1]
        ref[:rows, :] = parts[j][m]
        ref[rows:, :] = small_ref[...]


def pack(places, parts, small):
    rows, cols = parts[0].shape[1:]
    return pl.pallas_call(
        functools.partial(pack_kernel, places, len(parts)),
        in_specs=[VMEM] * (len(parts) + 1),
        out_specs=[VMEM] * len(places),
        out_shape=[like((rows + EXTRA, cols), BF)] * len(places),
        compiler_params=params(16),
        cost_estimate=cost(0),
        name="pack",
    )(*parts, small)


def unpack_kernel(count, *refs):
    parts, (out_ref, tab_ref, gains_ref) = refs[:count], refs[count:]
    rows = out_ref.shape[1]
    total, table, gains = None, None, None
    for j, part in enumerate(parts):
        piece = part[:rows, :].astype(F32)
        wide = join_small(part[rows:, :])
        total = piece if total is None else total + piece
        table = wide[j : j + 1] if table is None else table + wide[j : j + 1]
        gains = wide if gains is None else gains + wide
    out_ref[0] = total.astype(BF)
    tab_ref[...] = jnp.broadcast_to(table, tab_ref.shape)
    gains_ref[...] = gains


def unpack(parts):
    rows, cols = parts[0].shape
    shape = like((EXTRA // 2, cols), F32)
    return pl.pallas_call(
        functools.partial(unpack_kernel, len(parts)),
        in_specs=[VMEM] * len(parts),
        out_specs=[VMEM] * 3,
        out_shape=[like((1, rows - EXTRA, cols), BF), shape, shape],
        compiler_params=params(16),
        cost_estimate=cost(0),
        name="unpack",
    )(*parts)


def cat_kernel(count, *refs):
    for j in range(count):
        refs[count][j] = refs[j][...]


def cat(parts):
    return pl.pallas_call(
        functools.partial(cat_kernel, len(parts)),
        in_specs=[VMEM] * len(parts),
        out_specs=VMEM,
        out_shape=like((len(parts),) + parts[0].shape, BF),
        compiler_params=params(16),
        cost_estimate=cost(0),
        name="cat",
    )(*parts)


def finish_kernel(count, split, masks, ids_ref, *refs):
    parts, out_refs, mat = refs[:count], refs[count:-1], refs[-1]
    for j in range(parts[0].shape[1]):
        if split:
            put_blocks(ids_ref, masks, parts, mat, j)
            rows = mat.shape[0] // len(out_refs)
            for i, ref in enumerate(out_refs):
                ref[...] = mat[i * rows : (i + 1) * rows, :].astype(F32)
        else:
            put_blocks(ids_ref, masks, parts, out_refs[j], j)


def finish(ids, masks, parts, outs, rows):
    depth = parts[0].shape[-1]
    split = parts[0].shape[1] != outs
    return pl.pallas_call(
        functools.partial(finish_kernel, len(parts), split, masks),
        in_specs=[SMEM] + [VMEM] * len(parts),
        out_specs=[VMEM] * outs,
        out_shape=[like((rows, depth), F32)] * outs,
        scratch_shapes=[pltpu.VMEM((depth, depth), BF)],
        compiler_params=params(24),
        cost_estimate=cost(0),
        name="finish",
    )(ids, *parts)


def bar(*values):
    return list(lax.optimization_barrier(values))


def after(x, *deps):
    return lax.optimization_barrier((x,) + deps)[0]


class Ring:
    def __init__(self, n_dp, n_mp, depth, ids):
        self.n_dp, self.n_mp = n_dp, n_mp
        self.all_bits = (n_dp - 1).bit_length()
        self.bits = min(3, self.all_bits)
        self.rows = depth // (1 << self.bits)
        self.ids = ids
        self.masks = {flip: self.block_masks(flip) for flip in (False, True)}

    def block_masks(self, flip):
        masks, high = [0], list(range(1, self.bits))
        for bit in (high[::-1] if flip else high) + [0]:
            masks = masks + [m | (1 << bit) for m in masks]
        return masks

    def swap(self, x, mask):
        return lax.ppermute(x, "dp", [(i, i ^ mask) for i in range(self.n_dp)])

    def pull(self, x, shift):
        return lax.ppermute(x, "mp", [(i, (i - shift) % self.n_mp) for i in range(self.n_mp)])

    def push(self, x, shift):
        return lax.ppermute(x, "mp", [(i, (i + shift) % self.n_mp) for i in range(self.n_mp)])


class Reduce:
    def __init__(self, ring, send, keep, extra=0, split=(1, 1)):
        self.ring, self.extra, self.split = ring, extra, split
        order = list(range(1, ring.bits))
        self.orders = [order, order[::-1]]
        self.left = [order[::-1], order[::-1]]
        self.groups = [[keep, ring.swap(send, 1)]]
        self.done = False

    def received(self):
        return [group[1] for group in self.groups]

    def set_received(self, values):
        for group, value in zip(self.groups, values):
            group[1] = value

    def step(self):
        ring = self.ring
        if not self.orders[0]:
            out = fold(ring.ids, self.groups, None, self.extra, self.split)
            self.out, self.small = list(out[: sum(self.split)]), out[-1] if self.extra else None
            for bit in range(ring.bits, ring.all_bits):
                self.out = [add(out, ring.swap(out, 1 << bit)) for out in self.out]
                if self.extra:
                    self.small = add_small(self.small, ring.swap(self.small, 1 << bit))
            self.done = True
            return list(self.out)
        runs, bits = [], []
        for g in range(2):
            bit = self.orders[g].pop(0)
            runs.append((bit, row_runs(self.left[g], bit, ring.rows)))
            self.left[g] = [b for b in self.left[g] if b != bit]
            bits.append(bit)
        outs = fold(ring.ids, self.groups, runs, self.extra)
        self.groups = [[outs[2 * g + 1], ring.swap(outs[2 * g], 1 << bits[g])] for g in range(2)]
        return [outs[1], outs[3]]


def body(
    n_dp, n_mp, inputs, gain_attn, w_query, w_key, w_value, w_out, rel_table, gain_ffn, w_in, w_down,
    cotangent, bucket, lengths,
):
    rows, depth = inputs.shape
    buckets, heads = rel_table.shape
    width = heads * HEAD
    slots = lengths.shape[1]
    low = lax.axis_index("dp") & ((1 << min(3, (n_dp - 1).bit_length())) - 1)
    first_row = lax.axis_index("mp") * BIG
    ids = jnp.concatenate([low[None].astype(jnp.int32), bucket, first_row[None].astype(jnp.int32), lengths[0]])
    ring = Ring(n_dp, n_mp, depth, ids)
    shifts = list(range(1, n_mp))
    hot = jnp.asarray(offset_one_hot(buckets), BF)

    a_own = [w_out, w_query.T, w_key.T, w_value.T]
    a_piece, tab_own = prep(a_own, rel_table.T, depth, ring.rows, ring.bits)
    f_piece = prep_ffn(w_in, w_down, ring.rows, ring.bits)
    v = {}

    def close(*keys):
        v.update(zip(keys, bar(*[v[key] for key in keys])))

    def swap(new, old, mask):
        v[new] = ring.swap(v[old], mask)

    f3 = n_mp // 2
    f1, f2 = [s for s in shifts if s != f3]
    masks = ring.masks[False]
    v["piece"] = f_piece
    for s in shifts:
        v["z", s] = ring.pull(a_piece, s)
    x_value = inputs.astype(F32)
    n1 = (rms(x_value)[0] * gain_attn.astype(F32)).astype(BF)
    *kept_own, v["hidden"] = attn_fwd(ids, None, n1, a_own, 0, 1, tab_own, hot, inputs, None, slots, heads)
    v["gain1"], v["gain2"] = gain_attn, gain_ffn
    close(*[("z", s) for s in shifts], "hidden", "gain1", "gain2")
    v["a"], tab_rest = join([v["z", s] for s in shifts])
    close("a", "piece")
    swap("ax", "a", 2)
    swap("ay", "a", 4)
    v["f", f1] = ring.pull(v["piece"], f1)
    v["gain1"], v["gain2"] = v["gain1"][None], v["gain2"][None]
    close("ax", "ay", "a", ("f", f1), "piece", "gain1", "gain2")
    gain_one, gain_two = v["gain1"], v["gain2"]
    swap("ayx", "ax", 4)
    v["a3"] = cat([v["a"], v["ax"], v["ay"]])
    swap("a3c", "a3", 1)
    swap(("fx", f1), ("f", f1), 2)
    v["f", f2] = ring.pull(v["piece"], f2)
    close("ayx", "a3c", ("fx", f1), ("f", f2), "piece")
    v["a1"] = v["ayx"][None]
    swap("a1c", "a1", 1)
    close("a1c", "hidden")
    v["cat", f1] = cat([v["f", f1], v["fx", f1]])
    swap(("far", f1), ("cat", f1), 4)
    swap(("fx", f2), ("f", f2), 2)
    v["f", f3] = ring.pull(v["piece"], f3)
    a_parts = [v["a3"], v["a1"], v["a3c"], v["a1c"]]
    cut = n_mp - 2
    *kept_one, v["hidden"] = attn_fwd(
        ids, masks, n1, a_parts, 0, cut, tab_rest, hot, v["hidden"], None, slots, heads
    )
    close("hidden", ("fx", f2), ("f", f3), ("far", f1))
    v["cat", f2] = cat([v["f", f2], v["fx", f2]])
    swap(("far", f2), ("cat", f2), 4)
    swap(("fx", f3), ("f", f3), 2)
    swap(("catc", f1), ("cat", f1), 1)
    swap(("farc", f1), ("far", f1), 1)
    *kept_two, v["hidden"], v["n2"] = attn_fwd(
        ids, masks, n1, a_parts, cut, 1, tab_rest, hot, v["hidden"], gain_two, slots, heads
    )
    close("hidden", "n2", ("fx", f3), ("catc", f1), ("farc", f1))
    v["cat", f3] = cat([v["f", f3], v["fx", f3]])
    swap(("far", f3), ("cat", f3), 4)
    swap(("catc", f2), ("cat", f2), 1)
    swap(("catc", f3), ("cat", f3), 1)

    def parts_of(s):
        return masks, [v["cat", s], v["far", s], v["catc", s], v["farc", s]]

    v["out"], v["gn"], v["send"], v["keep"] = ffn(
        ids, v["n2"], cotangent, [(None, [w_in, w_down]), parts_of(f1)], None, None
    )
    close("out", "gn", "n2", "send", "keep", ("far", f3), ("far", f2), ("catc", f3), ("catc", f2))
    red = {}

    def reduce(name, extra=0, split=(1, 1)):
        red[name] = Reduce(ring, v["send"], v["keep"], extra, split)

    def close_with(names, *keys):
        groups = [group for name in names for group in red[name].groups]
        values = bar(*[group[1] for group in groups], *[v[key] for key in keys])
        for group, value in zip(groups, values):
            group[1] = value
        v.update(zip(keys, values[len(groups) :]))

    def folded(names, *keys):
        outs = [out for name in names for out in red[name].step()]
        v.update(zip(keys, bar(*[v[key] for key in keys], *outs)))

    swap(("farc", f2), ("far", f2), 1)
    swap(("farc", f3), ("far", f3), 1)
    reduce("a")
    close_with(["a"], "n2", "out", "gn", ("farc", f3), ("farc", f2))
    folded(["a"], "n2", "out", "gn")
    outputs, v["send"], v["keep"], grad_hidden, v["gh"], gg = ffn(
        ids, v["n2"], cotangent, [parts_of(f2), parts_of(f3)], (v["out"], v["gn"]), (v["hidden"], gain_two)
    )
    close_with(["a"], "send", "keep", "gh")
    reduce("b")
    folded(["a"], "gh")
    close_with(["b"], "gh")
    folded(["b"], "gh")

    places = [(tuple(range(cut)), kept_one), ((cut,), kept_two)]
    rest = (a_parts, tab_rest, places)
    own = (a_own, [*kept_own, tab_own])
    v["send"], v["keep"], v["gn"], tabs = attn_bwd(
        ids, masks, n1, v["gh"], hot, list(range(cut)), rest, None, None, None, slots, heads
    )
    close_with(["a", "b"], "send", "keep", "gh", "gn")
    reduce("c")
    folded(["b", "a"], "gh", "gn")
    v["f1"] = ring.push(red["a"].out[1], f1)
    close_with(["c"], "gh", "gn")
    folded(["c"], "gh", "gn")
    final = (inputs, gain_one, grad_hidden, gg, tabs)
    v["send"], v["keep"], v["gin"] = attn_bwd(
        ids, masks, n1, v["gh"], hot, [cut, None], rest, own, v["gn"], final, slots, heads
    )
    close_with(["b", "c"], "send", "keep", "gin", "f1")
    reduce("d", EXTRA)
    folded(["b", "c"], "gin")
    v["f2"] = ring.push(red["b"].out[0], f2)
    v["f3"] = ring.push(red["b"].out[1], f3)

    def spread(name, piece):
        v[name, 0] = piece
        for mask in (2, 4, 6):
            v[name, mask] = ring.swap(piece, mask)

    def gathered(name):
        v[name] = cat([v[name, mask] for mask in (0, 2, 4, 6)])
        v[name, 1] = ring.swap(v[name], 1)

    close_with(["d", "c"], "gin", "f2")
    folded(["d", "c"], "gin")
    close_with(["d"], "gin")
    folded(["d"], "gin")
    close_with(["d"], "gin", "f3")
    folded(["d"], "gin")
    packed = pack(((3, 0), (0, 0), (1, 0), (2, 0)), [*red["c"].out, *red["d"].out], red["d"].small)
    for s in shifts:
        v["a", s] = ring.push(packed[s], s)
    spread("f", total_of([red["a"].out[0], v["f1"], v["f2"], v["f3"]]))
    close(*[("a", s) for s in shifts], "gin")
    a_total, table, gains = unpack([packed[0]] + [v["a", s] for s in shifts])
    spread("a", a_total)
    close(("f", 2), ("f", 4), ("f", 6), "gin")
    gathered("f")
    close(("f", 1), "gin")
    v["in"], v["down"] = finish(ids, masks, [v["f"], v["f", 1]], 2, depth)
    v["table"] = table[0, : heads * TILE].reshape(heads, TILE)[:, :buckets].T
    v["gain_attn"], v["gain_ffn"] = gains[n_mp], gains[n_mp + 1]
    close("in", "down", "table", "gain_attn", "gain_ffn", ("a", 2), ("a", 4), ("a", 6), "gin")
    gathered("a")
    grad_in, grad_down, grad_inputs = v["in"], v["down"], v["gin"]
    grads = finish(ids, masks, [v["a"], v["a", 1]], 4, width)
    grad_out, grad_query, grad_key, grad_value = grads[0], grads[1].T, grads[2].T, grads[3].T

    return (
        outputs, grad_inputs, grad_query, grad_key, grad_value, grad_out, v["table"],
        v["gain_attn"], v["gain_ffn"], grad_in, grad_down,
    )


def solution(mesh):
    placed = (
        P(("dp", "mp"), None), P(), P(None, "mp"), P(None, "mp"), P(None, "mp"), P("mp", None),
        P(None, "mp"), P(), P(None, "mp"), P("mp", None), P(("dp", "mp"), None), P("dp"), P("dp", None),
    )
    return jax.shard_map(
        functools.partial(body, mesh.shape["dp"], mesh.shape["mp"]),
        mesh=mesh,
        in_specs=placed,
        out_specs=(
            P(("dp", "mp"), None), P(("dp", "mp"), None), P(None, "mp"), P(None, "mp"), P(None, "mp"),
            P("mp", None), P(None, "mp"), P(), P(), P(None, "mp"), P("mp", None),
        ),
        check_vma=False,
    )
```
